32 devices in a mesh: groups: 2 (over y), seq: 4 (over z), tensor: 2 (over x), dp: 2 (over core).
Axes of the slice: x: 2, y: 2, z: 4, core: 2. Of those that a mesh axis runs over, the one named last changes fastest.
Arguments:
- hidden_in: bfloat16 [1024, 14336], P(('groups', 'seq'), ('tensor', 'dp')), parts along dimension 0, may hold values from -6 to 6
- cotangent: bfloat16 [1024, 8192], P(('groups', 'tensor', 'dp'), 'seq'), parts along dimension 0, may hold values from -6 to 6
- down_weight: bfloat16 [14336, 8192], P(('tensor', 'dp'), 'seq'), may hold values from -0.0625 to 0.0625
- tile_ids: int32 [8, 4, 4], P(('groups', 'seq'), ('tensor', 'dp')), parts along dimension 0, may hold values from 0 to 447, as said below
- tile_live: int32 [8, 4, 4], P(('groups', 'seq'), ('tensor', 'dp')), parts along dimension 0, may hold values from 0 to 1, as said below
- values: float32 [8, 4, 4, 128, 128], P(('groups', 'seq'), ('tensor', 'dp')), parts along dimension 0, may hold values from -0.5 to 0.5
- moment_one: float32 [8, 4, 4, 128, 128], P(('groups', 'seq'), ('tensor', 'dp')), parts along dimension 0, may hold values from -12 to 12
- moment_two: float32 [8, 4, 4, 128, 128], P(('groups', 'seq'), ('tensor', 'dp')), parts along dimension 0, may hold values from 0.01 to 4
Outputs:
- hidden_grad: bfloat16 [1024, 14336], P(('groups', 'seq'), ('tensor', 'dp')), parts along dimension 0
- values_new: float32 [8, 4, 4, 128, 128], P(('groups', 'seq'), ('tensor', 'dp')), parts along dimension 0
- moment_one_new: float32 [8, 4, 4, 128, 128], P(('groups', 'seq'), ('tensor', 'dp')), parts along dimension 0
- moment_two_new: float32 [8, 4, 4, 128, 128], P(('groups', 'seq'), ('tensor', 'dp')), parts along dimension 0
The draws below stay inside these ranges and needn't reach their ends.
There are 2 independent parts, one for each index of `groups`. The reference program is written for one: setup_inputs(seed, part) draws one part's arguments, and reference() takes and returns one part's arrays. A program takes and returns all parts, laid end to end along the dimension named above; an argument that names none is the same for every part. Nothing has to cross between parts.
Inputs may be any that keep to these rules, and one draw needn't show every extreme that they name: `tile_live`: in every region the live slots come first, every region has at least one, and some region has all 4 live. `tile_ids`: the 4 entries of a region are distinct tile numbers t = f * 16 + d of its 28 x 16 blocks.
All inputs are finite; a program needn't handle non-finite values.
Results may differ from the reference program's by a relative error of at most 0.009.
Values may be sent and summed in bfloat16 or wider, within the bound.
No kernel may reach another device: no remote copies, remote signals or barrier semaphores. Data moves between devices by JAX's collectives and lax.ppermute only.
A program may use at most 128 MiB of HBM per device.

```python
import math
import jax
import jax.numpy as jnp
from jax import lax

D = 8192
FF = 14336
BLK = 128
SLOTS = 4
STEP = 100
SPANS = 4
LINES = 4
TOKENS = 512
FBLK = 28
DBLK = 16


def region_counts(key):
    key_a, key_b, key_c = jax.random.split(key, 3)
    larger = jax.random.randint(key_a, (SPANS * LINES,), 1, SLOTS + 1)
    coin_flip = jax.random.randint(key_b, (SPANS * LINES,), 0, 2)
    counts = jnp.where(coin_flip == 1, larger, 1)
    chosen = jax.random.randint(key_c, (), 0, SPANS * LINES)
    counts = counts.at[chosen].set(SLOTS)
    return counts.reshape(SPANS, LINES)


def draw_tile_live(key, part):
    key = jax.random.fold_in(key, 3)
    counts = region_counts(key)
    slot_index = jnp.arange(SLOTS, dtype=jnp.int32)
    return (slot_index[None, None, :] < counts[:, :, None]).astype(jnp.int32)


def draw_tile_ids(key, part):
    key = jax.random.fold_in(key, 5)
    tile_total = FBLK * DBLK
    scores = jax.random.randint(key, (SPANS, LINES, tile_total), 0, 1 << 20) * tile_total
    scores = scores + jnp.arange(tile_total, dtype=jnp.int32)[None, None, :]
    ordered = jnp.argsort(scores, axis=-1, stable=True)
    return ordered[:, :, :SLOTS].astype(jnp.int32)


def block_scale(key, dims, cuts, low, top_value):
    loudness, own = 1.0, jax.random.fold_in(key, 6)
    for dim, parts in cuts:
        heights = jnp.exp(jax.random.uniform(jax.random.fold_in(own, dim), (parts,), jnp.float32, low / len(cuts), top_value / len(cuts)))
        loudness = loudness * jnp.repeat(heights, dims[dim] // parts).reshape([-1 if axis == dim else 1 for axis in range(len(dims))])
    return loudness


def scatter_about(rng, dims, spread, limit, shards=(), held_as=jnp.bfloat16):
    loudness = block_scale(rng, dims, shards, -0.22, 0.18) if shards else 1.0
    array = jax.random.normal(rng, dims, jnp.float32) * spread * loudness
    return jnp.minimum(jnp.maximum(array, -limit), limit).astype(held_as)


def setup_inputs(seed: int = 0, part: int = 0) -> dict:
    key_of = jax.random.split(jax.random.key(seed), 9)
    part_keys = jax.random.split(jax.random.fold_in(key_of[8], part), 9)
    return {
        "hidden_in": scatter_about(part_keys[0], (TOKENS, FF), 1.0, 6.0, ((0, 4), (1, 4))),
        "cotangent": scatter_about(part_keys[1], (TOKENS, D), 1.0, 6.0, ((0, 4), (1, 4))),
        "down_weight": scatter_about(key_of[2], (FF, D), D ** -0.5, 0.0625, ((0, 4), (1, 4))),
        "tile_ids": draw_tile_ids(jax.random.fold_in(jax.random.fold_in(key_of[8], part), 71), part),
        "tile_live": draw_tile_live(jax.random.fold_in(jax.random.fold_in(key_of[8], part), 71), part),
        "values": scatter_about(part_keys[5], (SPANS, LINES, SLOTS, BLK, BLK), 0.09, 0.5, ((0, 4), (1, 4)), jnp.float32),
        "moment_one": scatter_about(part_keys[6], (SPANS, LINES, SLOTS, BLK, BLK), 2.0, 12.0, ((0, 4), (1, 4)), jnp.float32),
        "moment_two": jnp.clip(jnp.exp(math.log(4.0) - 5.9914646 * jax.random.uniform(part_keys[7], (SPANS, LINES, SLOTS, BLK, BLK), jnp.float32) ** block_scale(part_keys[7], (SPANS, LINES, SLOTS, BLK, BLK), ((0, 4), (1, 4)), -0.2, 0.2)), 0.01, 4.0),
    }


BETA_ONE = 0.9
BETA_TWO = 0.999
RATE = 0.01
EPSILON = 1e-08

def reference(hidden_in, cotangent, down_weight, tile_ids, tile_live, values, moment_one, moment_two):
    counts = lax.optimization_barrier(jnp.sum(tile_live, axis=2)).astype(jnp.int32)
    prefix = (jnp.cumsum(counts, axis=0) - counts).astype(jnp.int32)
    line_total = lax.optimization_barrier(jnp.sum(counts, axis=0)).astype(jnp.int32)
    slot_index = jnp.arange(SLOTS, dtype=jnp.int32)
    is_live = tile_live > 0
    tile_rank = (prefix[:, :, None] + slot_index[None, None, :]).astype(jnp.int32)
    owner_seq = (tile_rank % SPANS).astype(jnp.int32)
    owner_slot = jnp.minimum(tile_rank // SPANS, SLOTS - 1).astype(jnp.int32)
    line_index = jnp.broadcast_to(jnp.arange(LINES, dtype=jnp.int32)[None, :, None], tile_rank.shape)
    held_tiles = values[owner_seq, line_index, owner_slot]
    held_tiles = jnp.where(is_live[:, :, :, None, None], held_tiles, jnp.zeros_like(held_tiles)).astype(jnp.bfloat16)
    f_block = (tile_ids // DBLK).astype(jnp.int32)
    d_block = (tile_ids % DBLK).astype(jnp.int32)
    f_pick = jax.nn.one_hot(f_block, FBLK, dtype=jnp.float32)
    d_pick = jax.nn.one_hot(d_block, DBLK, dtype=jnp.float32)
    d_span = D // SPANS

    def span_step(total_sum, inputs):
        span_index, span_tiles, f_sel, d_sel = inputs
        grad_rows = lax.dynamic_slice_in_dim(cotangent, span_index * d_span, d_span, 1)
        weights = lax.dynamic_slice_in_dim(down_weight, span_index * d_span, d_span, 1)
        dense_part = jnp.dot(grad_rows, weights.T, preferred_element_type=jnp.float32)
        sparse = jnp.einsum('ljfd,ljk,ljm->lkfmd', span_tiles.astype(jnp.float32), f_sel, d_sel)
        sparse = sparse.reshape(FF, d_span).astype(jnp.bfloat16)
        dense_part = dense_part + jnp.dot(grad_rows, sparse.T, preferred_element_type=jnp.float32)
        rounded = lax.optimization_barrier(dense_part.astype(jnp.bfloat16))
        return (total_sum + rounded.astype(jnp.float32), None)
    summed, _ = lax.scan(span_step, jnp.zeros((TOKENS, FF), jnp.float32), (jnp.arange(SPANS, dtype=jnp.int32), held_tiles, f_pick, d_pick))
    hidden_grad = summed.astype(jnp.bfloat16)
    f_global = (line_index * FBLK + f_block).astype(jnp.int32)
    span_ids = jnp.broadcast_to(jnp.arange(SPANS, dtype=jnp.int32)[:, None, None], tile_rank.shape)
    d_global = (span_ids * DBLK + d_block).astype(jnp.int32)

    def tile_grad(coords):
        f_start, d_start = coords
        h_cols = lax.dynamic_slice_in_dim(hidden_in, f_start * BLK, BLK, 1)
        d_cols = lax.dynamic_slice_in_dim(cotangent, d_start * BLK, BLK, 1)
        return jnp.dot(h_cols.T, d_cols, preferred_element_type=jnp.float32)
    tile_grads = lax.map(tile_grad, (f_global.reshape(-1), d_global.reshape(-1)))
    tile_grads = tile_grads.reshape(SPANS, LINES, SLOTS, BLK, BLK)
    tile_grads = jnp.where(is_live[:, :, :, None, None], tile_grads, jnp.zeros_like(tile_grads))
    gathered = jnp.zeros_like(values).at[owner_seq, line_index, owner_slot].add(tile_grads)
    own_rank = slot_index[None, None, :] * SPANS + jnp.arange(SPANS, dtype=jnp.int32)[:, None, None]
    own_live = (own_rank < line_total[None, :, None])[:, :, :, None, None]
    moment_new = BETA_ONE * moment_one + (1.0 - BETA_ONE) * gathered
    square_new = BETA_TWO * moment_two + (1.0 - BETA_TWO) * gathered * gathered
    stepped = moment_new / (1.0 - BETA_ONE ** STEP) / (jnp.sqrt(square_new / (1.0 - BETA_TWO ** STEP)) + EPSILON)
    updated = values - RATE * stepped
    values_new = jnp.where(own_live, updated, values)
    moment_one_new = jnp.where(own_live, moment_new, moment_one)
    moment_two_new = jnp.where(own_live, square_new, moment_two)
    return (hidden_grad, values_new, moment_one_new, moment_two_new)
```

```python
import functools

import jax
import jax.numpy as jnp
from jax import lax
from jax.experimental import pallas as pl
from jax.experimental.pallas import tpu as pltpu
from jax.sharding import PartitionSpec as P

STEP = 100
BETA_ONE = 0.9
BETA_TWO = 0.999
RATE = 0.01
EPSILON = 1e-08
VMEM_LIMIT = 48 * 1024 * 1024


def vmem():
    return pl.BlockSpec(memory_space=pltpu.VMEM)


def smem():
    return pl.BlockSpec(memory_space=pltpu.SMEM)


def params():
    return pltpu.CompilerParams(vmem_limit_bytes=VMEM_LIMIT)


def region_count(meta, region, slots):
    count = meta[region, slots]
    for slot in range(1, slots):
        count = count + meta[region, slots + slot]
    return count


def region_counts(meta, spans, slots):
    counts = [region_count(meta, region, slots) for region in range(spans)]
    prefix, total = [], jnp.int32(0)
    for count in counts:
        prefix.append(total)
        total = total + count
    return counts, prefix, total


def pick_kernel(spans, slots, block, d_blocks, meta, here, values, hidden, value_out, hidden_out):
    counts, prefix, _ = region_counts(meta, spans, slots)
    me = here[0]
    for region in range(spans):
        slot = lax.rem(me - lax.rem(prefix[region], spans) + spans, spans)
        live = slot < counts[region]
        owned = jnp.minimum(lax.div(prefix[region] + slot, spans), slots - 1)
        tile = values[owned]
        value_out[region] = jnp.where(live, tile, jnp.zeros_like(tile)).astype(jnp.bfloat16)
        for j in range(slots):
            start = pl.multiple_of(lax.div(meta[region, j], d_blocks) * block, block)
            hidden_out[region, j] = hidden[:, pl.ds(start, block)]


def grad_kernel(spans, slots, block, d_blocks, meta, here, hidden, rows, out):
    me = here[0]
    count = region_count(meta, me, slots)
    before = jnp.int32(0)
    for region in range(spans):
        before = before + jnp.where(region < me, region_count(meta, region, slots), 0)
    out[...] = jnp.zeros_like(out)
    chunk = hidden.shape[2]
    for j in range(slots):

        @pl.when(j < count)
        def _():
            d_start = pl.multiple_of(lax.rem(meta[me, j], d_blocks) * block, block)
            total = jnp.zeros((block, block), jnp.float32)
            for part in range(spans):
                total = total + lax.dot_general(
                    hidden[part, j],
                    rows[pl.ds(part * chunk, chunk), pl.ds(d_start, block)],
                    (((0,), (0,)), ((), ())),
                    preferred_element_type=jnp.float32,
                )
            out[lax.rem(before + j, spans)] = total.astype(out.dtype)


def adam_kernel(spans, slots, meta, here, grads, values, one, two, values_new, one_new, two_new):
    counts, prefix, total = region_counts(meta, spans, slots)
    me = here[0]
    for owned in range(slots):
        rank = owned * spans + me
        source = jnp.int32(0)
        for region in range(1, spans):
            source = jnp.where(prefix[region] <= rank, region, source)
        live = rank < total
        grad = grads[source].astype(jnp.float32)
        stored, old_one, old_two = values[owned], one[owned], two[owned]
        new_one = BETA_ONE * old_one + (1.0 - BETA_ONE) * grad
        new_two = BETA_TWO * old_two + (1.0 - BETA_TWO) * grad * grad
        stepped = (
            new_one
            / (1.0 - BETA_ONE**STEP)
            / (jnp.sqrt(new_two / (1.0 - BETA_TWO**STEP)) + EPSILON)
        )
        values_new[owned] = jnp.where(live, stored - RATE * stepped, stored)
        one_new[owned] = jnp.where(live, new_one, old_one)
        two_new[owned] = jnp.where(live, new_two, old_two)


def exchange(array):
    return lax.all_to_all(array, "seq", 0, 0, tiled=True)


def per_device(
    hidden_in, cotangent, down_weight, tile_ids, tile_live, values, moment_one, moment_two
):
    spans = lax.axis_size("seq")
    slots, block = values.shape[2], values.shape[3]
    f_width, d_width = down_weight.shape
    d_blocks, f_blocks = d_width // block, f_width // block
    chunk = hidden_in.shape[0]
    tokens = chunk * spans
    here = lax.axis_index("seq").astype(jnp.int32)[None]
    sizes = (spans, slots, block, d_blocks)

    meta = jnp.concatenate([tile_ids[0], tile_live[0]], axis=1)
    meta = lax.all_gather(meta, "seq", axis=0, tiled=True)
    rows = lax.all_gather(cotangent, ("tensor", "dp"), axis=0, tiled=True)

    value_send, hidden_send = pl.pallas_call(
        functools.partial(pick_kernel, *sizes),
        out_shape=(
            jax.ShapeDtypeStruct((spans, block, block), jnp.bfloat16),
            jax.ShapeDtypeStruct((spans, slots, chunk, block), jnp.bfloat16),
        ),
        in_specs=[smem(), smem(), vmem(), vmem()],
        out_specs=(vmem(), vmem()),
        compiler_params=params(),
        name="pick",
    )(meta, here, values[0, 0], hidden_in)
    held = exchange(value_send)
    hidden_cols = exchange(hidden_send)

    group = max(size for size in range(1, 5) if f_blocks % size == 0)
    width = group * block
    parts = 2 if (f_blocks // group) > 1 else 1
    steps_all = f_width // width
    cuts = [steps_all * part // parts for part in range(parts + 1)]
    pieces = []
    for low, high in zip(cuts[:-1], cuts[1:]):
        piece = pl.pallas_call(
            functools.partial(offset_kernel, low, *sizes),
            grid=(high - low,),
            out_shape=jax.ShapeDtypeStruct((tokens, (high - low) * width), jnp.bfloat16),
            in_specs=[
                smem(),
                smem(),
                pl.BlockSpec((tokens, d_width), lambda i: (0, 0)),
                pl.BlockSpec((width, d_width), lambda i, low=low: (i + low, 0)),
                pl.BlockSpec((spans, block, block), lambda i: (0, 0, 0)),
            ],
            out_specs=pl.BlockSpec((tokens, width), lambda i: (0, i)),
            scratch_shapes=[pltpu.VMEM((tokens, width), jnp.float32)],
            compiler_params=params(),
            cost_estimate=pl.CostEstimate(
                flops=2 * tokens * d_width * (high - low) * width,
                bytes_accessed=2 * d_width * (high - low) * width,
                transcendentals=0,
            ),
            name="partial",
        )(meta, here, rows, down_weight, held)
        pieces.append(lax.psum_scatter(piece, "seq", scatter_dimension=0, tiled=True))
    hidden_grad = jnp.concatenate(pieces, axis=1)

    grad_send = pl.pallas_call(
        functools.partial(grad_kernel, *sizes),
        out_shape=jax.ShapeDtypeStruct((spans, block, block), jnp.bfloat16),
        in_specs=[smem(), smem(), vmem(), vmem()],
        out_specs=vmem(),
        compiler_params=params(),
        name="tile_grad",
    )(meta, here, hidden_cols, rows)
    grads = exchange(grad_send)
    tile = jax.ShapeDtypeStruct((slots, block, block), jnp.float32)
    new = pl.pallas_call(
        functools.partial(adam_kernel, spans, slots),
        out_shape=(tile, tile, tile),
        in_specs=[smem(), smem()] + [vmem()] * 4,
        out_specs=(vmem(), vmem(), vmem()),
        compiler_params=params(),
        name="adam",
    )(meta, here, grads, values[0, 0], moment_one[0, 0], moment_two[0, 0])
    return (hidden_grad,) + tuple(array[None, None] for array in new)


def offset_kernel(low, spans, slots, block, d_blocks, meta, here, rows, weight, held, out, total):
    step = pl.program_id(0) + low
    partial_step(step, spans, slots, block, d_blocks, meta, here, rows, weight, held, out, total)


def partial_step(
    step, spans, slots, block, d_blocks, meta, here, rows, weight, held, out, total
):
    width = weight.shape[0]
    total[...] = lax.dot_general(
        rows[...], weight[...], (((1,), (1,)), ((), ())), preferred_element_type=jnp.float32
    )
    me = here[0]
    count = region_count(meta, me, slots)
    before = jnp.int32(0)
    for region in range(spans):
        before = before + jnp.where(region < me, region_count(meta, region, slots), 0)
    for j in range(slots):
        tile = meta[me, j]
        f_start = lax.div(tile, d_blocks) * block - step * width

        @pl.when((j < count) & (f_start >= 0) & (f_start < width))
        def _():
            d_start = pl.multiple_of(lax.rem(tile, d_blocks) * block, block)
            place = pl.ds(pl.multiple_of(f_start, block), block)
            total[:, place] += lax.dot_general(
                rows[:, pl.ds(d_start, block)],
                held[lax.rem(before + j, spans)],
                (((1,), (1,)), ((), ())),
                preferred_element_type=jnp.float32,
            )

    out[...] = total[...].astype(out.dtype)


def solution(mesh):
    shards = P(("groups", "seq"), ("tensor", "dp"))
    tiles = P(("groups", "seq"), ("tensor", "dp"), None, None, None)
    lists = P(("groups", "seq"), ("tensor", "dp"), None)
    return jax.shard_map(
        per_device,
        mesh=mesh,
        in_specs=(
            shards,
            P(("groups", "tensor", "dp"), "seq"),
            P(("tensor", "dp"), "seq"),
            lists,
            lists,
            tiles,
            tiles,
            tiles,
        ),
        out_specs=(shards, tiles, tiles, tiles),
        check_vma=False,
    )
```

```python
import functools

import jax
import jax.numpy as jnp
from jax import lax
from jax.experimental import pallas as pl
from jax.experimental.pallas import tpu as pltpu
from jax.sharding import PartitionSpec as P

STEP = 100
BETA_ONE = 0.9
BETA_TWO = 0.999
RATE = 0.01
EPSILON = 1e-08
VMEM_LIMIT = 48 * 1024 * 1024
NT = (((1,), (1,)), ((), ()))
TN = (((0,), (0,)), ((), ()))


def vmem():
    return pl.BlockSpec(memory_space=pltpu.VMEM)


def smem():
    return pl.BlockSpec(memory_space=pltpu.SMEM)


def anywhere():
    return pl.BlockSpec(memory_space=pl.ANY)


def params():
    return pltpu.CompilerParams(vmem_limit_bytes=VMEM_LIMIT)


def wrap(index, size):
    return lax.rem(index + size, size)


def live_count(meta, region, slots):
    count = meta[region, slots]
    for slot in range(1, slots):
        count = count + meta[region, slots + slot]
    return count


def rank_before(meta, region, spans, slots):
    before = jnp.int32(0)
    for other in range(spans):
        before = before + jnp.where(other < region, live_count(meta, other, slots), 0)
    return before


def pick_kernel(spans, slots, block, d_blocks, meta, values, hidden, *outs):
    me = lax.axis_index("seq")
    for s in range(spans):
        region = lax.rem(me + s, spans)
        before = rank_before(meta, region, spans, slots)
        slot = wrap(me - lax.rem(before, spans), spans)
        live = slot < live_count(meta, region, slots)
        tile = values[jnp.minimum(lax.div(before + slot, spans), slots - 1)]
        outs[s][...] = jnp.where(live, tile, jnp.zeros_like(tile)).astype(jnp.bfloat16)
        for j in range(slots):
            start = pl.multiple_of(lax.div(meta[region, j], d_blocks) * block, block)
            outs[spans + s][j] = hidden[:, pl.ds(start, block)]


def chunk_place(chunk):
    tensors, cores = lax.axis_size("tensor"), lax.axis_size("dp")
    t_place = wrap(lax.div(chunk, cores) - lax.axis_index("tensor"), tensors)
    d_place = wrap(lax.rem(chunk, cores) - lax.axis_index("dp"), cores)
    return t_place * cores + d_place


def step_kernel(sizes, low, chunks_of, arrivals, meta, held, weight, *refs):
    spans, slots, block, d_blocks = sizes
    places = lax.axis_size("tensor") * lax.axis_size("dp")
    gathered, refs = refs[:places], refs[places:]
    arrived, refs = refs[: sum(arrivals)], refs[sum(arrivals) :]
    outs, (rows, total, sem) = refs[: len(chunks_of)], refs[len(chunks_of) :]
    step = pl.program_id(0)
    me = lax.axis_index("seq")
    chunk = gathered[0].shape[0]

    @pl.when(step == 0)
    def _():
        for k, chunk_of in enumerate(chunks_of):
            place = chunk_place(jnp.clip(chunk_of(me), 0, spans - 1))
            for p in range(places):

                @pl.when(place == p)
                def _():
                    copy = pltpu.make_async_copy(
                        gathered[p], rows.at[pl.ds(k * chunk, chunk)], sem
                    )
                    copy.start()
                    copy.wait()

    total[...] = lax.dot_general(rows[...], weight[...], NT, preferred_element_type=jnp.float32)
    width = weight.shape[0]
    count = live_count(meta, me, slots)
    before = rank_before(meta, me, spans, slots)
    for j in range(slots):
        tile = meta[me, j]
        f_start = lax.div(tile, d_blocks) * block - (step + low) * width

        @pl.when((j < count) & (f_start >= 0) & (f_start < width))
        def _():
            d_start = pl.multiple_of(lax.rem(tile, d_blocks) * block, block)
            place = pl.ds(pl.multiple_of(f_start, block), block)
            owner = lax.rem(before + j, spans)
            total[:, place] += lax.dot_general(
                rows[:, pl.ds(d_start, block)],
                held[wrap(me - owner, spans)],
                NT,
                preferred_element_type=jnp.float32,
            )

    at = 0
    for k, out in enumerate(outs):
        result = total[k * chunk : (k + 1) * chunk]
        for _ in range(arrivals[k]):
            result = result + arrived[at][...].astype(jnp.float32)
            at += 1
        out[...] = result.astype(out.dtype)


def step_call(sizes, low, high, width, chunks_of, arrived, meta, held, weight, gathered, dtype):
    chunk, d_width = gathered[0].shape
    many = len(chunks_of)
    columns = pl.BlockSpec((chunk, width), lambda i: (0, i))
    given = [array for group in arrived for array in group]
    return pl.pallas_call(
        functools.partial(step_kernel, sizes, low, chunks_of, [len(group) for group in arrived]),
        grid=(high - low,),
        out_shape=[jax.ShapeDtypeStruct((chunk, (high - low) * width), dtype)] * many,
        in_specs=[
            smem(),
            pl.BlockSpec(held.shape, lambda i: (0, 0, 0)),
            pl.BlockSpec((width, d_width), lambda i: (i + low, 0)),
        ]
        + [anywhere()] * len(gathered)
        + [columns] * len(given),
        out_specs=[columns] * many,
        scratch_shapes=[
            pltpu.VMEM((many * chunk, d_width), gathered[0].dtype),
            pltpu.VMEM((many * chunk, width), jnp.float32),
            pltpu.SemaphoreType.DMA,
        ],
        compiler_params=params(),
        cost_estimate=pl.CostEstimate(
            flops=2 * many * chunk * d_width * (high - low) * width,
            bytes_accessed=2 * d_width * (high - low) * width,
            transcendentals=0,
        ),
        name="partial",
    )(meta, held, weight, *gathered, *given)


def last_kernel(with_out, own, right, left, *refs):
    out = refs[-1]
    total = own[...] + right[...].astype(jnp.float32) + left[...].astype(jnp.float32)
    out[...] = total.astype(out.dtype)


def last_call(low, high, width, own, right, left, out, shape):
    chunk = own.shape[0]
    columns = pl.BlockSpec((chunk, width), lambda i: (0, i))
    return pl.pallas_call(
        functools.partial(last_kernel, out is not None),
        grid=(high - low,),
        out_shape=shape,
        in_specs=[columns] * 3 + ([] if out is None else [anywhere()]),
        out_specs=pl.BlockSpec((chunk, width), lambda i: (0, i + low)),
        input_output_aliases={} if out is None else {3: 0},
        compiler_params=params(),
        name="last_sum",
    )(own, right, left, *([] if out is None else [out]))


def grad_kernel(spans, slots, block, d_blocks, meta, *refs):
    places = lax.axis_size("tensor") * lax.axis_size("dp")
    hidden, refs = refs[:spans], refs[spans:]
    gathered, refs = refs[:places], refs[places:]
    outs, (cols,) = refs[:spans], refs[spans:]
    me = lax.axis_index("seq")
    tensors, cores = lax.axis_size("tensor"), lax.axis_size("dp")
    count = live_count(meta, me, slots)
    before = rank_before(meta, me, spans, slots)
    for s in range(spans):
        cols[s] = hidden[s][...]
    for s in range(spans):
        slot = wrap(lax.rem(me + s, spans) - lax.rem(before, spans), spans)
        outs[s][...] = jnp.zeros_like(outs[s])

        @pl.when(slot < count)
        def _():
            d_start = pl.multiple_of(lax.rem(meta[me, slot], d_blocks) * block, block)
            total = jnp.zeros((block, block), jnp.float32)
            for p in range(places):
                t_place = lax.rem(lax.axis_index("tensor") + p // cores, tensors)
                d_place = lax.rem(lax.axis_index("dp") + p % cores, cores)
                chunk = t_place * cores + d_place
                total = total + lax.dot_general(
                    cols[wrap(me - chunk, spans), slot],
                    gathered[p][:, pl.ds(d_start, block)],
                    TN,
                    preferred_element_type=jnp.float32,
                )
            outs[s][...] = total.astype(outs[s].dtype)


def adam_kernel(spans, slots, meta, *refs):
    arrived, refs = refs[:spans], refs[spans:]
    values, one, two, values_new, one_new, two_new, grads = refs
    me = lax.axis_index("seq")
    for s in range(spans):
        grads[s] = arrived[s][...]
    befores = [rank_before(meta, region, spans, slots) for region in range(spans)]
    total = befores[-1] + live_count(meta, spans - 1, slots)
    for owned in range(slots):
        rank = owned * spans + me
        source = jnp.int32(0)
        for region in range(1, spans):
            source = jnp.where(befores[region] <= rank, region, source)
        live = rank < total
        grad = grads[wrap(me - source, spans)].astype(jnp.float32)
        stored, old_one, old_two = values[owned], one[owned], two[owned]
        new_one = BETA_ONE * old_one + (1.0 - BETA_ONE) * grad
        new_two = BETA_TWO * old_two + (1.0 - BETA_TWO) * grad * grad
        stepped = (
            new_one
            / (1.0 - BETA_ONE**STEP)
            / (jnp.sqrt(new_two / (1.0 - BETA_TWO**STEP)) + EPSILON)
        )
        values_new[owned] = jnp.where(live, stored - RATE * stepped, stored)
        one_new[owned] = jnp.where(live, new_one, old_one)
        two_new[owned] = jnp.where(live, new_two, old_two)


def take_from(array, axis, places):
    size = lax.axis_size(axis)
    return lax.ppermute(array, axis, [((i + places) % size, i) for i in range(size)])


def exchange(pieces):
    return [pieces[0]] + [take_from(pieces[s], "seq", -s) for s in range(1, len(pieces))]


def gather_rows(own):
    gathered = []
    for t_place in range(lax.axis_size("tensor")):
        first = take_from(own, "tensor", t_place) if t_place else own
        gathered.append(first)
        for d_place in range(1, lax.axis_size("dp")):
            gathered.append(take_from(first, "dp", d_place))
    return gathered


def per_device(
    hidden_in, cotangent, down_weight, tile_ids, tile_live, values, moment_one, moment_two
):
    spans = lax.axis_size("seq")
    slots, block = values.shape[2], values.shape[3]
    f_width, d_width = down_weight.shape
    d_blocks, f_blocks = d_width // block, f_width // block
    chunk = hidden_in.shape[0]
    sizes = (spans, slots, block, d_blocks)

    gathered = gather_rows(cotangent)
    meta = jnp.concatenate([tile_ids[0], tile_live[0]], axis=1)
    meta = lax.all_gather(meta, "seq", axis=0, tiled=True)

    value_tile = jax.ShapeDtypeStruct((block, block), jnp.bfloat16)
    hidden_tiles = jax.ShapeDtypeStruct((slots, chunk, block), jnp.bfloat16)
    picked = pl.pallas_call(
        functools.partial(pick_kernel, *sizes),
        out_shape=[value_tile] * spans + [hidden_tiles] * spans,
        in_specs=[smem(), vmem(), vmem()],
        out_specs=[vmem()] * (2 * spans),
        compiler_params=params(),
        name="pick",
    )(meta, values[0, 0], hidden_in)
    held = jnp.stack(exchange(picked[:spans]))
    hidden_cols = exchange(picked[spans:])

    group = max(size for size in range(1, 3) if f_blocks % size == 0)
    width = group * block
    steps = f_blocks // group
    parts = max(count for count in (1, 2) if steps % count == 0)
    cuts = [steps * part // parts for part in range(parts + 1)]
    ranges = list(zip(cuts[:-1], cuts[1:]))
    half = spans // 2
    up, down = [[] for _ in ranges], [[] for _ in ranges]
    for t in range(1, spans):
        ups = lambda me, t=t: spans - t + me
        downs = lambda me, t=t: me + t - spans
        for part, (low, high) in enumerate(ranges):
            if t <= half:
                either = lambda me, ups=ups, downs=downs: jnp.where(me < half, ups(me), downs(me))
                chunks_of, arrived = [either], [up[part] + down[part]]
            else:
                chunks_of, arrived = [ups, downs], [up[part], down[part]]
            sums = step_call(
                sizes, low, high, width, chunks_of, arrived, meta, held, down_weight, gathered,
                jnp.bfloat16,
            )
            up[part] = [lax.ppermute(sums[0], "seq", [(z, z + 1) for z in range(t)])]
            down[part] = [
                lax.ppermute(sums[-1], "seq", [(spans - 1 - z, spans - 2 - z) for z in range(t)])
            ]

    send = pl.pallas_call(
        functools.partial(grad_kernel, *sizes),
        out_shape=[value_tile] * spans,
        in_specs=[smem()] + [vmem()] * (spans + len(gathered)),
        out_specs=[vmem()] * spans,
        scratch_shapes=[pltpu.VMEM((spans, slots, chunk, block), jnp.bfloat16)],
        compiler_params=params(),
        name="tile_grad",
    )(meta, *hidden_cols, *gathered)
    grads = exchange(send)
    tile = jax.ShapeDtypeStruct((slots, block, block), jnp.float32)
    new = pl.pallas_call(
        functools.partial(adam_kernel, spans, slots),
        out_shape=(tile, tile, tile),
        in_specs=[smem()] + [vmem()] * (spans + 3),
        out_specs=(vmem(), vmem(), vmem()),
        scratch_shapes=[pltpu.VMEM((spans, block, block), jnp.bfloat16)],
        compiler_params=params(),
        name="adam",
    )(meta, *grads, values[0, 0], moment_one[0, 0], moment_two[0, 0])

    hidden_grad = None
    shape = jax.ShapeDtypeStruct((chunk, f_width), jnp.bfloat16)
    for part, (low, high) in enumerate(ranges):
        (own,) = step_call(
            sizes, low, high, width, [lambda me: me], [[]], meta, held, down_weight, gathered,
            jnp.float32,
        )
        hidden_grad = last_call(
            low, high, width, own, up[part][0], down[part][0], hidden_grad, shape
        )
    return (hidden_grad,) + tuple(array[None, None] for array in new)


def solution(mesh):
    shards = P(("groups", "seq"), ("tensor", "dp"))
    tiles = P(("groups", "seq"), ("tensor", "dp"), None, None, None)
    lists = P(("groups", "seq"), ("tensor", "dp"), None)
    return jax.shard_map(
        per_device,
        mesh=mesh,
        in_specs=(
            shards,
            P(("groups", "tensor", "dp"), "seq"),
            P(("tensor", "dp"), "seq"),
            lists,
            lists,
            tiles,
            tiles,
            tiles,
        ),
        out_specs=(shards, tiles, tiles, tiles),
        check_vma=False,
    )
```

```python
import functools

import jax
import jax.numpy as jnp
from jax import lax
from jax.experimental import pallas as pl
from jax.experimental.pallas import tpu as pltpu
from jax.sharding import PartitionSpec as P

STEP = 100
BETA_ONE = 0.9
BETA_TWO = 0.999
RATE = 0.01
EPSILON = 1e-08
VMEM_LIMIT = 24 * 1024 * 1024
PARTS = 3
NT = (((1,), (1,)), ((), ()))
TN = (((0,), (0,)), ((), ()))


def vmem():
    return pl.BlockSpec(memory_space=pltpu.VMEM)


def smem():
    return pl.BlockSpec(memory_space=pltpu.SMEM)


def hbm():
    return pl.BlockSpec(memory_space=pltpu.HBM)


def stay(array):
    return pltpu.with_memory_space_constraint(array, pltpu.HBM)


def params():
    return pltpu.CompilerParams(vmem_limit_bytes=VMEM_LIMIT)


def wrap(index, size):
    return lax.rem(index + size, size)


def live_count(meta, region, slots):
    count = meta[region, slots]
    for slot in range(1, slots):
        count = count + meta[region, slots + slot]
    return count


def rank_before(meta, region, spans, slots):
    before = jnp.int32(0)
    for other in range(spans):
        before = before + jnp.where(other < region, live_count(meta, other, slots), 0)
    return before


def pick_kernel(spans, slots, block, d_blocks, meta, values, hidden, *refs):
    value_outs, hidden_outs = refs[:spans], refs[spans : 2 * spans]
    tiles, value_sems, hidden_sems = refs[2 * spans :]
    me = lax.axis_index("seq")
    lives, value_copies, hidden_copies = [], [], []
    for s in range(spans):
        region = lax.rem(me + s, spans)
        before = rank_before(meta, region, spans, slots)
        slot = wrap(me - lax.rem(before, spans), spans)
        lives.append(slot < live_count(meta, region, slots))
        owned = jnp.minimum(lax.div(before + slot, spans), slots - 1)
        copy = pltpu.make_async_copy(values.at[owned], tiles.at[s], value_sems.at[s])
        copy.start()
        value_copies.append(copy)
    for s in range(spans):
        region = lax.rem(me + s, spans)
        for j in range(slots):
            start = pl.multiple_of(lax.div(meta[region, j], d_blocks) * block, block)
            copy = pltpu.make_async_copy(
                hidden.at[:, pl.ds(start, block)], hidden_outs[s].at[j], hidden_sems.at[s, j]
            )
            copy.start()
            hidden_copies.append(copy)
    for s in range(spans):
        value_copies[s].wait()
        tile = tiles[s]
        value_outs[s][...] = jnp.where(lives[s], tile, jnp.zeros_like(tile)).astype(jnp.bfloat16)
    for copy in hidden_copies:
        copy.wait()


def chunk_at(place):
    tensors, cores = lax.axis_size("tensor"), lax.axis_size("dp")
    t_place = lax.rem(lax.axis_index("tensor") + place // cores, tensors)
    d_place = lax.rem(lax.axis_index("dp") + place % cores, cores)
    return t_place * cores + d_place


def matmul_kernel(sizes, low, first_part, meta, held, weight, *refs):
    spans, slots, block, d_blocks = sizes
    step = pl.program_id(0)
    if first_part:
        gathered, (out, first, rows, total, sem) = refs[:spans], refs[spans:]
        chunk = gathered[0].shape[0]

        @pl.when(step == 0)
        def _():
            copy = pltpu.make_async_copy(gathered[0], rows.at[pl.ds(0, chunk)], sem)
            copy.start()
            for p in range(1, spans):
                rows[p * chunk : (p + 1) * chunk] = gathered[p][...]
            copy.wait()

    else:
        rows, out, first, total = refs
        chunk = rows.shape[0] // spans
    me = lax.axis_index("seq")
    width = weight.shape[0]
    here = pl.ds(pl.multiple_of(step * width, width), width)
    total[...] = lax.dot_general(rows[...], weight[...], NT, preferred_element_type=jnp.float32)
    count = live_count(meta, me, slots)
    before = rank_before(meta, me, spans, slots)
    for j in range(slots):
        tile = meta[me, j]
        f_start = lax.div(tile, d_blocks) * block - (low + step) * width

        @pl.when((j < count) & (f_start >= 0) & (f_start < width))
        def _():
            d_start = pl.multiple_of(lax.rem(tile, d_blocks) * block, block)
            place = pl.ds(pl.multiple_of(f_start, block), block)
            owner = lax.rem(before + j, spans)
            total[:, place] += lax.dot_general(
                rows[:, pl.ds(d_start, block)],
                held[wrap(me - owner, spans)],
                NT,
                preferred_element_type=jnp.float32,
            )

    first_chunk = wrap(me - 1, spans)
    for p in range(spans):
        result = total[p * chunk : (p + 1) * chunk].astype(out.dtype)
        out[chunk_at(p), :, here] = result

        @pl.when(chunk_at(p) == first_chunk)
        def _():
            first[:, here] = result


def matmul_call(sizes, low, high, width, meta, held, weight, gathered, rows):
    spans = sizes[0]
    chunk, d_width = gathered[0].shape
    columns = (high - low) * width
    first_part = rows is None
    shapes = [
        jax.ShapeDtypeStruct((spans, chunk, columns), jnp.bfloat16),
        jax.ShapeDtypeStruct((chunk, columns), jnp.bfloat16),
    ]
    scratch = [pltpu.VMEM((spans * chunk, width), jnp.float32)]
    if first_part:
        shapes.append(jax.ShapeDtypeStruct((spans * chunk, d_width), gathered[0].dtype))
        scratch.append(pltpu.SemaphoreType.DMA)
    return pl.pallas_call(
        functools.partial(matmul_kernel, sizes, low, first_part),
        grid=(high - low,),
        out_shape=shapes,
        in_specs=[smem(), vmem(), pl.BlockSpec((width, d_width), lambda i: (i + low, 0))]
        + ([hbm()] + [vmem()] * (spans - 1) if first_part else [vmem()]),
        out_specs=[vmem()] * len(shapes),
        scratch_shapes=scratch,
        compiler_params=params(),
        cost_estimate=pl.CostEstimate(
            flops=2 * spans * chunk * d_width * columns,
            bytes_accessed=2 * d_width * columns,
            transcendentals=0,
        ),
        name="partial",
    )(
        meta,
        held,
        stay(weight),
        *([stay(gathered[0]), *gathered[1:]] if first_part else [rows]),
    )


def add_kernel(t, partials, arrived, out):
    spans = partials.shape[0]
    chunk = wrap(lax.axis_index("seq") - t, spans)
    result = partials[chunk].astype(jnp.float32) + arrived[...].astype(jnp.float32)
    out[...] = result.astype(out.dtype)


def add_call(t, partials, arrived):
    return pl.pallas_call(
        functools.partial(add_kernel, t),
        out_shape=jax.ShapeDtypeStruct(arrived.shape, arrived.dtype),
        in_specs=[vmem(), vmem()],
        out_specs=vmem(),
        compiler_params=params(),
        name="add",
    )(partials, arrived)


def last_kernel(low, partials, arrived, *refs):
    out, total, sem = refs[-3:]
    columns = partials.shape[2]
    result = partials[lax.axis_index("seq")].astype(jnp.float32) + arrived[...].astype(jnp.float32)
    total[...] = result.astype(out.dtype)
    copy = pltpu.make_async_copy(total, out.at[:, pl.ds(low, columns)], sem)
    copy.start()
    copy.wait()


def last_call(low, partials, arrived, out, shape):
    _, chunk, columns = partials.shape
    given = [] if out is None else [out]
    return pl.pallas_call(
        functools.partial(last_kernel, low),
        out_shape=shape,
        in_specs=[vmem()] * 2 + [hbm()] * len(given),
        out_specs=hbm(),
        scratch_shapes=[pltpu.VMEM((chunk, columns), shape.dtype), pltpu.SemaphoreType.DMA],
        input_output_aliases={2: 0} if given else {},
        compiler_params=params(),
        name="last_sum",
    )(partials, arrived, *given)


def grad_kernel(spans, slots, block, d_blocks, meta, *refs):
    places = lax.axis_size("tensor") * lax.axis_size("dp")
    hidden, refs = refs[:spans], refs[spans:]
    gathered, refs = refs[:places], refs[places:]
    outs, (cols,) = refs[:spans], refs[spans:]
    me = lax.axis_index("seq")
    count = live_count(meta, me, slots)
    before = rank_before(meta, me, spans, slots)
    for s in range(spans):
        cols[s] = hidden[s][...]
    for s in range(spans):
        slot = wrap(lax.rem(me + s, spans) - lax.rem(before, spans), spans)
        outs[s][...] = jnp.zeros_like(outs[s])

        @pl.when(slot < count)
        def _():
            d_start = pl.multiple_of(lax.rem(meta[me, slot], d_blocks) * block, block)
            total = jnp.zeros((block, block), jnp.float32)
            for p in range(places):
                chunk = chunk_at(p)
                total = total + lax.dot_general(
                    cols[wrap(me - chunk, spans), slot],
                    gathered[p][:, pl.ds(d_start, block)],
                    TN,
                    preferred_element_type=jnp.float32,
                )
            outs[s][...] = total.astype(outs[s].dtype)


def adam_kernel(spans, slots, meta, *refs):
    arrived, refs = refs[:spans], refs[spans:]
    values, one, two, values_new, one_new, two_new, grads = refs
    me = lax.axis_index("seq")
    for s in range(spans):
        grads[s] = arrived[s][...]
    befores = [rank_before(meta, region, spans, slots) for region in range(spans)]
    total = befores[-1] + live_count(meta, spans - 1, slots)
    for owned in range(slots):
        rank = owned * spans + me
        source = jnp.int32(0)
        for region in range(1, spans):
            source = jnp.where(befores[region] <= rank, region, source)
        live = rank < total
        grad = grads[wrap(me - source, spans)].astype(jnp.float32)
        stored, old_one, old_two = values[owned], one[owned], two[owned]
        new_one = BETA_ONE * old_one + (1.0 - BETA_ONE) * grad
        new_two = BETA_TWO * old_two + (1.0 - BETA_TWO) * grad * grad
        stepped = (
            new_one
            / (1.0 - BETA_ONE**STEP)
            / (jnp.sqrt(new_two / (1.0 - BETA_TWO**STEP)) + EPSILON)
        )
        values_new[owned] = jnp.where(live, stored - RATE * stepped, stored)
        one_new[owned] = jnp.where(live, new_one, old_one)
        two_new[owned] = jnp.where(live, new_two, old_two)


def take_from(array, axis, places):
    size = lax.axis_size(axis)
    return lax.ppermute(array, axis, [((i + places) % size, i) for i in range(size)])


def exchange(pieces):
    return [pieces[0]] + [take_from(pieces[s], "seq", -s) for s in range(1, len(pieces))]


def gather_rows(own, after):
    gathered = []
    for t_place in range(lax.axis_size("tensor")):
        first = take_from(own, "tensor", t_place) if t_place else own
        gathered.append(first)
        if t_place:
            first, _ = lax.optimization_barrier((first, after))
        for d_place in range(1, lax.axis_size("dp")):
            gathered.append(take_from(first, "dp", d_place))
    return gathered


def per_device(
    hidden_in, cotangent, down_weight, tile_ids, tile_live, values, moment_one, moment_two
):
    spans = lax.axis_size("seq")
    slots, block = values.shape[2], values.shape[3]
    f_width, d_width = down_weight.shape
    d_blocks, f_blocks = d_width // block, f_width // block
    chunk = hidden_in.shape[0]
    sizes = (spans, slots, block, d_blocks)

    meta = jnp.concatenate([tile_ids[0], tile_live[0]], axis=1)
    meta = lax.all_gather(meta, "seq", axis=0, tiled=True)

    value_tile = jax.ShapeDtypeStruct((block, block), jnp.bfloat16)
    hidden_tiles = jax.ShapeDtypeStruct((slots, chunk, block), jnp.bfloat16)
    picked = pl.pallas_call(
        functools.partial(pick_kernel, *sizes),
        out_shape=[value_tile] * spans + [hidden_tiles] * spans,
        in_specs=[smem(), hbm(), hbm()],
        out_specs=[vmem()] * (2 * spans),
        scratch_shapes=[
            pltpu.VMEM((spans, block, block), jnp.float32),
            pltpu.SemaphoreType.DMA((spans,)),
            pltpu.SemaphoreType.DMA((spans, slots)),
        ],
        compiler_params=params(),
        name="pick",
    )(meta, stay(values[0, 0]), stay(hidden_in))
    held = jnp.stack(exchange(picked[:spans]))
    hidden_cols = exchange(picked[spans:])
    gathered = gather_rows(cotangent, (held, hidden_cols[1]))

    group = max(size for size in range(1, 5) if f_blocks % size == 0)
    width = group * block
    steps = f_blocks // group
    cuts = [(steps * part + 1) // PARTS for part in range(PARTS + 1)]
    ranges = list(zip(cuts[:-1], cuts[1:]))
    partials, moving, rows = [], [], None
    for low, high in ranges:
        if len(partials) == 1:
            rows, hidden_cols = lax.optimization_barrier((rows, hidden_cols))
        if len(partials) == 2:
            moving[0] = add_call(2, partials[0], moving[0])
            rows, moving[0] = lax.optimization_barrier((rows, moving[0]))
        partial, first, *more = matmul_call(
            sizes, low, high, width, meta, held, down_weight, gathered, rows
        )
        rows = more[0] if more else rows
        partials.append(partial)
        moving.append(take_from(first, "seq", -1))
    for t in range(2, spans):
        for part in range(len(ranges)):
            if (t, part) != (2, 0):
                moving[part] = add_call(t, partials[part], moving[part])
            moving[part] = take_from(moving[part], "seq", -1)

    send = pl.pallas_call(
        functools.partial(grad_kernel, *sizes),
        out_shape=[value_tile] * spans,
        in_specs=[smem()] + [vmem()] * (spans + len(gathered)),
        out_specs=[vmem()] * spans,
        scratch_shapes=[pltpu.VMEM((spans, slots, chunk, block), jnp.bfloat16)],
        compiler_params=params(),
        name="tile_grad",
    )(meta, *hidden_cols, *gathered)
    grads = exchange(send)
    tile = jax.ShapeDtypeStruct((slots, block, block), jnp.float32)
    new = pl.pallas_call(
        functools.partial(adam_kernel, spans, slots),
        out_shape=(tile, tile, tile),
        in_specs=[smem()] + [vmem()] * (spans + 3),
        out_specs=(vmem(), vmem(), vmem()),
        scratch_shapes=[pltpu.VMEM((spans, block, block), jnp.bfloat16)],
        compiler_params=params(),
        name="adam",
    )(meta, *grads, values[0, 0], moment_one[0, 0], moment_two[0, 0])

    hidden_grad = None
    shape = jax.ShapeDtypeStruct((chunk, f_width), jnp.bfloat16)
    for part, (low, _) in enumerate(ranges):
        hidden_grad = last_call(
            low * width, partials[part], moving[part], hidden_grad, shape
        )
    return (hidden_grad,) + tuple(array[None, None] for array in new)


def solution(mesh):
    shards = P(("groups", "seq"), ("tensor", "dp"))
    tiles = P(("groups", "seq"), ("tensor", "dp"), None, None, None)
    lists = P(("groups", "seq"), ("tensor", "dp"), None)
    return jax.shard_map(
        per_device,
        mesh=mesh,
        in_specs=(
            shards,
            P(("groups", "tensor", "dp"), "seq"),
            P(("tensor", "dp"), "seq"),
            lists,
            lists,
            tiles,
            tiles,
            tiles,
        ),
        out_specs=(shards, tiles, tiles, tiles),
        check_vma=False,
    )
```

```python
import functools

import jax
import jax.numpy as jnp
from jax import lax
from jax.experimental import pallas as pl
from jax.experimental.pallas import tpu as pltpu
from jax.sharding import PartitionSpec as P

STEP = 100
BETA_ONE = 0.9
BETA_TWO = 0.999
RATE = 0.01
EPSILON = 1e-08
VMEM_LIMIT = 24 * 1024 * 1024
PARTS = 3
NT = (((1,), (1,)), ((), ()))
TN = (((0,), (0,)), ((), ()))


def vmem():
    return pl.BlockSpec(memory_space=pltpu.VMEM)


def smem():
    return pl.BlockSpec(memory_space=pltpu.SMEM)


def hbm():
    return pl.BlockSpec(memory_space=pltpu.HBM)


def stay(array):
    return pltpu.with_memory_space_constraint(array, pltpu.HBM)


def params():
    return pltpu.CompilerParams(vmem_limit_bytes=VMEM_LIMIT)


def wrap(index, size):
    return lax.rem(index + size, size)


class Lists:
    def __init__(self, rows, spans, slots):
        self.rows, self.spans, self.slots = rows, spans, slots
        self.me = lax.axis_index("seq")
        self.counts = []
        for s in range(spans):
            count = self.live(s, 0)
            for slot in range(1, slots):
                count = count + self.live(s, slot)
            self.counts.append(count)

    def tile(self, s, slot):
        ref, row = self.rows[s]
        return ref[row, slot]

    def live(self, s, slot):
        ref, row = self.rows[s]
        return ref[row, self.slots + slot]

    def region(self, s):
        return lax.rem(self.me + s, self.spans)

    def before(self, s):
        region, before = self.region(s), jnp.int32(0)
        for other in range(self.spans):
            before = before + jnp.where(self.region(other) < region, self.counts[other], 0)
        return before


def table_lists(table, spans, slots):
    return Lists([(table, s) for s in range(spans)], spans, slots)


def pick_kernel(spans, slots, block, d_blocks, *refs):
    metas, (values, hidden, table), refs = refs[:spans], refs[spans : spans + 3], refs[spans + 3 :]
    value_outs, hidden_outs = refs[:spans], refs[spans : 2 * spans]
    tiles, value_sems, hidden_sems = refs[2 * spans :]
    lists = Lists([(meta, 0) for meta in metas], spans, slots)
    lives, value_copies, hidden_copies = [], [], []
    for s in range(spans):
        before = lists.before(s)
        slot = wrap(lists.me - lax.rem(before, spans), spans)
        lives.append(slot < lists.counts[s])
        owned = jnp.minimum(lax.div(before + slot, spans), slots - 1)
        copy = pltpu.make_async_copy(values.at[owned], tiles.at[s], value_sems.at[s])
        copy.start()
        value_copies.append(copy)
    for s in range(spans):
        for j in range(slots):
            start = pl.multiple_of(lax.div(lists.tile(s, j), d_blocks) * block, block)
            copy = pltpu.make_async_copy(
                hidden.at[:, pl.ds(start, block)], hidden_outs[s].at[j], hidden_sems.at[s, j]
            )
            copy.start()
            hidden_copies.append(copy)
        for j in range(2 * slots):
            table[s, j] = metas[s][0, j]
    for s in range(spans):
        value_copies[s].wait()
        tile = tiles[s]
        value_outs[s][...] = jnp.where(lives[s], tile, jnp.zeros_like(tile)).astype(jnp.bfloat16)
    for copy in hidden_copies:
        copy.wait()


def lay_kernel(own, weight, *refs):
    others, (rows, first_weight, sems) = refs[:-3], refs[-3:]
    chunk = own.shape[0]
    weight_copy = pltpu.make_async_copy(
        weight.at[pl.ds(0, first_weight.shape[0])], first_weight, sems.at[0]
    )
    weight_copy.start()
    own_copy = pltpu.make_async_copy(own, rows.at[pl.ds(0, chunk)], sems.at[1])
    own_copy.start()
    for p, other in enumerate(others):
        rows[(p + 1) * chunk : (p + 2) * chunk] = other[...]
    own_copy.wait()
    weight_copy.wait()


def chunk_at(place):
    tensors, cores = lax.axis_size("tensor"), lax.axis_size("dp")
    t_place = lax.rem(lax.axis_index("tensor") + place // cores, tensors)
    d_place = lax.rem(lax.axis_index("dp") + place % cores, cores)
    return t_place * cores + d_place


def matmul_kernel(sizes, low, width, pieces, table, held, weight, *refs):
    spans, slots, block, d_blocks = sizes
    step = pl.program_id(0)
    if pieces > 1:
        given, (out, first, rows, total) = refs[:pieces], refs[pieces:]

        @pl.when(step == 0)
        def _():
            at = 0
            for piece in given:
                rows[at : at + piece.shape[0]] = piece[...]
                at += piece.shape[0]

    else:
        rows, out, first, total = refs
    chunk = rows.shape[0] // spans
    here = pl.ds(pl.multiple_of(step * width, width), width)
    weights = weight[here] if weight.shape[0] > width else weight[...]
    total[...] = lax.dot_general(rows[...], weights, NT, preferred_element_type=jnp.float32)
    lists = table_lists(table, spans, slots)
    before = lists.before(0)
    for j in range(slots):
        tile = lists.tile(0, j)
        f_start = lax.div(tile, d_blocks) * block - (low + step) * width

        @pl.when((j < lists.counts[0]) & (f_start >= 0) & (f_start < width))
        def _():
            d_start = pl.multiple_of(lax.rem(tile, d_blocks) * block, block)
            place = pl.ds(pl.multiple_of(f_start, block), block)
            owner = lax.rem(before + j, spans)
            total[:, place] += lax.dot_general(
                rows[:, pl.ds(d_start, block)],
                held[wrap(lists.me - owner, spans)],
                NT,
                preferred_element_type=jnp.float32,
            )

    first_chunk = wrap(lists.me - 1, spans)
    for p in range(spans):
        result = total[p * chunk : (p + 1) * chunk].astype(out.dtype)
        out[chunk_at(p), :, here] = result

        @pl.when(chunk_at(p) == first_chunk)
        def _():
            first[:, here] = result


def matmul_call(sizes, low, high, width, table, held, weight, pieces):
    spans = sizes[0]
    tokens, d_width = sum(piece.shape[0] for piece in pieces), weight.shape[1]
    columns = (high - low) * width
    shapes = [
        jax.ShapeDtypeStruct((spans, tokens // spans, columns), jnp.bfloat16),
        jax.ShapeDtypeStruct((tokens // spans, columns), jnp.bfloat16),
    ]
    if len(pieces) > 1:
        shapes.append(jax.ShapeDtypeStruct((tokens, d_width), pieces[0].dtype))
    if weight.shape[0] == columns:
        weight_spec = vmem()
    else:
        weight, weight_spec = stay(weight), pl.BlockSpec((width, d_width), lambda i: (i + low, 0))
    return pl.pallas_call(
        functools.partial(matmul_kernel, sizes, low, width, len(pieces)),
        grid=(high - low,),
        out_shape=shapes,
        in_specs=[smem(), vmem(), weight_spec] + [vmem()] * len(pieces),
        out_specs=[vmem()] * len(shapes),
        scratch_shapes=[pltpu.VMEM((tokens, width), jnp.float32)],
        compiler_params=params(),
        cost_estimate=pl.CostEstimate(
            flops=2 * tokens * d_width * columns,
            bytes_accessed=2 * d_width * columns,
            transcendentals=0,
        ),
        name="partial",
    )(table, held, weight, *pieces)


def add_kernel(t, partials, arrived, out):
    spans = partials.shape[0]
    chunk = wrap(lax.axis_index("seq") - t, spans)
    result = partials[chunk].astype(jnp.float32) + arrived[...].astype(jnp.float32)
    out[...] = result.astype(out.dtype)


def add_call(t, partials, arrived):
    return pl.pallas_call(
        functools.partial(add_kernel, t),
        out_shape=jax.ShapeDtypeStruct(arrived.shape, arrived.dtype),
        in_specs=[vmem(), vmem()],
        out_specs=vmem(),
        compiler_params=params(),
        name="add",
    )(partials, arrived)


def last_kernel(low, partials, arrived, *refs):
    out, total, sem = refs[-3:]
    columns = partials.shape[2]
    result = partials[lax.axis_index("seq")].astype(jnp.float32) + arrived[...].astype(jnp.float32)
    total[...] = result.astype(out.dtype)
    copy = pltpu.make_async_copy(total, out.at[:, pl.ds(low, columns)], sem)
    copy.start()
    copy.wait()


def last_call(low, partials, arrived, out, shape):
    _, chunk, columns = partials.shape
    given = [] if out is None else [out]
    return pl.pallas_call(
        functools.partial(last_kernel, low),
        out_shape=shape,
        in_specs=[vmem()] * 2 + [hbm()] * len(given),
        out_specs=hbm(),
        scratch_shapes=[pltpu.VMEM((chunk, columns), shape.dtype), pltpu.SemaphoreType.DMA],
        input_output_aliases={2: 0} if given else {},
        compiler_params=params(),
        name="last_sum",
    )(partials, arrived, *given)


def grad_kernel(spans, slots, block, d_blocks, table, rows, *refs):
    hidden, outs, (cols,) = refs[:spans], refs[spans : 2 * spans], refs[2 * spans :]
    lists = table_lists(table, spans, slots)
    before = lists.before(0)
    chunk = rows.shape[0] // spans
    for s in range(spans):
        cols[s] = hidden[s][...]
    for s in range(spans):
        slot = wrap(lists.region(s) - lax.rem(before, spans), spans)
        outs[s][...] = jnp.zeros_like(outs[s])

        @pl.when(slot < lists.counts[0])
        def _():
            d_start = pl.multiple_of(lax.rem(table[0, slot], d_blocks) * block, block)
            total = jnp.zeros((block, block), jnp.float32)
            for p in range(spans):
                total = total + lax.dot_general(
                    cols[wrap(lists.me - chunk_at(p), spans), slot],
                    rows[p * chunk : (p + 1) * chunk, pl.ds(d_start, block)],
                    TN,
                    preferred_element_type=jnp.float32,
                )
            outs[s][...] = total.astype(outs[s].dtype)


def grad_call(sizes, table, rows, hidden_cols):
    spans = sizes[0]
    slots, chunk, block = hidden_cols[0].shape
    return pl.pallas_call(
        functools.partial(grad_kernel, *sizes),
        out_shape=[jax.ShapeDtypeStruct((block, block), jnp.bfloat16)] * spans,
        in_specs=[smem()] + [vmem()] * (spans + 1),
        out_specs=[vmem()] * spans,
        scratch_shapes=[pltpu.VMEM((spans, slots, chunk, block), jnp.bfloat16)],
        compiler_params=params(),
        name="tile_grad",
    )(table, rows, *hidden_cols)


def adam_kernel(spans, slots, table, *refs):
    arrived, refs = refs[:spans], refs[spans:]
    values, one, two, values_new, one_new, two_new, grads = refs
    lists = table_lists(table, spans, slots)
    for s in range(spans):
        grads[s] = arrived[s][...]
    befores = [lists.before(s) for s in range(spans)]
    for owned in range(slots):
        rank = owned * spans + lists.me
        live, source = jnp.bool_(False), jnp.int32(0)
        for s in range(spans):
            holds = (befores[s] <= rank) & (rank < befores[s] + lists.counts[s])
            live, source = live | holds, jnp.where(holds, (spans - s) % spans, source)
        grad = grads[source].astype(jnp.float32)
        stored, old_one, old_two = values[owned], one[owned], two[owned]
        new_one = BETA_ONE * old_one + (1.0 - BETA_ONE) * grad
        new_two = BETA_TWO * old_two + (1.0 - BETA_TWO) * grad * grad
        stepped = (
            new_one
            / (1.0 - BETA_ONE**STEP)
            / (jnp.sqrt(new_two / (1.0 - BETA_TWO**STEP)) + EPSILON)
        )
        values_new[owned] = jnp.where(live, stored - RATE * stepped, stored)
        one_new[owned] = jnp.where(live, new_one, old_one)
        two_new[owned] = jnp.where(live, new_two, old_two)


def adam_call(sizes, table, grads, *states):
    spans, slots, block, _ = sizes
    tile = jax.ShapeDtypeStruct((slots, block, block), jnp.float32)
    return pl.pallas_call(
        functools.partial(adam_kernel, spans, slots),
        out_shape=(tile, tile, tile),
        in_specs=[smem()] + [vmem()] * (spans + 3),
        out_specs=(vmem(), vmem(), vmem()),
        scratch_shapes=[pltpu.VMEM((spans, block, block), jnp.bfloat16)],
        compiler_params=params(),
        name="adam",
    )(table, *grads, *[state[0, 0] for state in states])


def take_from(array, axis, places):
    size = lax.axis_size(axis)
    return lax.ppermute(array, axis, [((i + places) % size, i) for i in range(size)])


def exchange(pieces):
    return [pieces[0]] + [take_from(pieces[s], "seq", -s) for s in range(1, len(pieces))]


def per_device(
    hidden_in, cotangent, down_weight, tile_ids, tile_live, values, moment_one, moment_two
):
    spans, cores = lax.axis_size("seq"), lax.axis_size("dp")
    slots, block = values.shape[2], values.shape[3]
    f_width, d_width = down_weight.shape
    d_blocks, f_blocks = d_width // block, f_width // block
    chunk = hidden_in.shape[0]
    sizes = (spans, slots, block, d_blocks)
    group = max(size for size in range(1, 5) if f_blocks % size == 0)
    width = group * block
    steps = f_blocks // group
    cuts = [(steps * part + 1) // PARTS for part in range(PARTS + 1)]
    ranges = list(zip(cuts[:-1], cuts[1:]))

    firsts = [take_from(cotangent, "tensor", t) for t in range(1, lax.axis_size("tensor"))]
    local = [take_from(cotangent, "dp", d) for d in range(1, cores)]
    meta = jnp.concatenate([tile_ids[0], tile_live[0]], axis=1)
    metas = [meta] + [take_from(meta, "seq", s) for s in range(1, spans)]

    value_tile = jax.ShapeDtypeStruct((block, block), jnp.bfloat16)
    hidden_tiles = jax.ShapeDtypeStruct((slots, chunk, block), jnp.bfloat16)
    table, *picked = pl.pallas_call(
        functools.partial(pick_kernel, *sizes),
        out_shape=[jax.ShapeDtypeStruct((spans, 2 * slots), jnp.int32)]
        + [value_tile] * spans
        + [hidden_tiles] * spans,
        in_specs=[smem()] * spans + [hbm(), hbm()],
        out_specs=[smem()] + [vmem()] * (2 * spans),
        scratch_shapes=[
            pltpu.VMEM((spans, block, block), jnp.float32),
            pltpu.SemaphoreType.DMA((spans,)),
            pltpu.SemaphoreType.DMA((spans, slots)),
        ],
        compiler_params=params(),
        name="pick",
    )(*metas, stay(values[0, 0]), stay(hidden_in))
    held = jnp.stack(exchange(picked[:spans]))
    hidden_cols = exchange(picked[spans:])

    local_rows, first_weight = pl.pallas_call(
        lay_kernel,
        out_shape=[
            jax.ShapeDtypeStruct((cores * chunk, d_width), cotangent.dtype),
            jax.ShapeDtypeStruct((ranges[0][1] * width, d_width), down_weight.dtype),
        ],
        in_specs=[hbm(), hbm()] + [vmem()] * (cores - 1),
        out_specs=[vmem(), vmem()],
        scratch_shapes=[pltpu.SemaphoreType.DMA((2,))],
        compiler_params=params(),
        name="lay",
    )(stay(cotangent), stay(down_weight), *local)

    firsts, *_ = lax.optimization_barrier((firsts, held, hidden_cols[1], local_rows, first_weight))
    pieces = [local_rows]
    for first in firsts:
        pieces += [first] + [take_from(first, "dp", d) for d in range(1, cores)]

    partials, moving = [], []
    for part, (low, high) in enumerate(ranges):
        if part == 1:
            rows, hidden_cols = lax.optimization_barrier((rows, hidden_cols))
        if part == 2:
            moving[0] = add_call(2, partials[0], moving[0])
            send = grad_call(sizes, table, rows, hidden_cols)
            rows, moving[0], send = lax.optimization_barrier((rows, moving[0], send))
        weight = down_weight if part else first_weight
        partial, first, *more = matmul_call(
            sizes, low, high, width, table, held, weight, [rows] if part else pieces
        )
        rows = more[0] if more else rows
        partials.append(partial)
        moving.append(take_from(first, "seq", -1))

    grads = exchange(send)
    for t in range(2, spans):
        for part in range(len(ranges)):
            if (t, part) == (2, 1):
                moving[part], grads = lax.optimization_barrier((moving[part], grads))
                new = adam_call(sizes, table, grads, values, moment_one, moment_two)
            if (t, part) == (spans - 1, 0):
                moving[part], new = lax.optimization_barrier((moving[part], new))
            if (t, part) != (2, 0):
                moving[part] = add_call(t, partials[part], moving[part])
            moving[part] = take_from(moving[part], "seq", -1)

    hidden_grad = None
    shape = jax.ShapeDtypeStruct((chunk, f_width), jnp.bfloat16)
    for part, (low, _) in enumerate(ranges):
        hidden_grad = last_call(low * width, partials[part], moving[part], hidden_grad, shape)
    return (hidden_grad,) + tuple(array[None, None] for array in new)


def solution(mesh):
    shards = P(("groups", "seq"), ("tensor", "dp"))
    tiles = P(("groups", "seq"), ("tensor", "dp"), None, None, None)
    lists = P(("groups", "seq"), ("tensor", "dp"), None)
    return jax.shard_map(
        per_device,
        mesh=mesh,
        in_specs=(
            shards,
            P(("groups", "tensor", "dp"), "seq"),
            P(("tensor", "dp"), "seq"),
            lists,
            lists,
            tiles,
            tiles,
            tiles,
        ),
        out_specs=(shards, tiles, tiles, tiles),
        check_vma=False,
    )
```

```python
import functools

import jax
import jax.numpy as jnp
from jax import lax
from jax.experimental import pallas as pl
from jax.experimental.pallas import tpu as pltpu
from jax.sharding import PartitionSpec as P

STEP = 100
BETA_ONE = 0.9
BETA_TWO = 0.999
RATE = 0.01
EPSILON = 1e-08
VMEM_LIMIT = 24 * 1024 * 1024
PARTS = 3
NT = (((1,), (1,)), ((), ()))
TN = (((0,), (0,)), ((), ()))


def vmem():
    return pl.BlockSpec(memory_space=pltpu.VMEM)


def smem():
    return pl.BlockSpec(memory_space=pltpu.SMEM)


def hbm():
    return pl.BlockSpec(memory_space=pltpu.HBM)


def stay(array):
    return pltpu.with_memory_space_constraint(array, pltpu.HBM)


def cost(count):
    return pl.CostEstimate(flops=count, bytes_accessed=2 * count, transcendentals=0)


def params():
    return pltpu.CompilerParams(vmem_limit_bytes=VMEM_LIMIT)


def wrap(index, size):
    return lax.rem(index + size, size)


def live_count(table, region, slots):
    count = table[region, slots]
    for slot in range(1, slots):
        count = count + table[region, slots + slot]
    return count


def rank_before(table, region, spans, slots):
    before = jnp.int32(0)
    for other in range(spans):
        before = before + jnp.where(other < region, live_count(table, other, slots), 0)
    return before


def early_kernel(values, hidden, values_half, hidden_here, stored, sems):
    value_copy = pltpu.make_async_copy(values, stored, sems.at[0])
    hidden_copy = pltpu.make_async_copy(hidden, hidden_here, sems.at[1])
    value_copy.start()
    hidden_copy.start()
    value_copy.wait()
    values_half[...] = stored[...].astype(values_half.dtype)
    hidden_copy.wait()


def pick_kernel(slots, block, d_blocks, table, hidden, *outs):
    spans = len(outs)
    me = lax.axis_index("seq")
    for s in range(spans):
        for j in range(slots):
            tile = table[lax.rem(me + s, spans), j]
            start = pl.multiple_of(lax.div(tile, d_blocks) * block, block)
            outs[s][j] = hidden[:, pl.ds(start, block)]


def lay_kernel(spans, slots, table, own, weight, *refs):
    others, stored, (rows, first_weight, held, sems) = (
        refs[: -4 - spans],
        refs[-4 - spans : -4],
        refs[-4:],
    )
    chunk = own.shape[0]
    weight_copy = pltpu.make_async_copy(
        weight.at[pl.ds(0, first_weight.shape[0])], first_weight, sems.at[0]
    )
    weight_copy.start()
    own_copy = pltpu.make_async_copy(own, rows.at[pl.ds(0, chunk)], sems.at[1])
    own_copy.start()
    for p, other in enumerate(others):
        rows[(p + 1) * chunk : (p + 2) * chunk] = other[...]
    me = lax.axis_index("seq")
    before = rank_before(table, me, spans, slots)
    for j in range(slots):
        rank = before + j
        owned = jnp.minimum(lax.div(rank, spans), slots - 1)
        place = wrap(lax.rem(rank, spans) - me, spans)
        for s in range(spans):

            @pl.when(place == s)
            def _():
                held[j] = stored[s][owned]

    own_copy.wait()
    weight_copy.wait()


def chunk_at(place):
    tensors, cores = lax.axis_size("tensor"), lax.axis_size("dp")
    t_place = lax.rem(lax.axis_index("tensor") + place // cores, tensors)
    d_place = lax.rem(lax.axis_index("dp") + place % cores, cores)
    return t_place * cores + d_place


def matmul_kernel(sizes, low, width, pieces, table, held, weight, *refs):
    spans, slots, block, d_blocks = sizes
    step = pl.program_id(0)
    if pieces > 1:
        given, (out, first, rows, total) = refs[:pieces], refs[pieces:]

        @pl.when(step == 0)
        def _():
            at = 0
            for piece in given:
                rows[at : at + piece.shape[0]] = piece[...]
                at += piece.shape[0]

    else:
        rows, out, first, total = refs
    chunk = rows.shape[0] // spans
    here = pl.ds(pl.multiple_of(step * width, width), width)
    weights = weight[here] if weight.shape[0] > width else weight[...]
    total[...] = lax.dot_general(rows[...], weights, NT, preferred_element_type=jnp.float32)
    me = lax.axis_index("seq")
    count = live_count(table, me, slots)
    for j in range(slots):
        tile = table[me, j]
        f_start = lax.div(tile, d_blocks) * block - (low + step) * width

        @pl.when((j < count) & (f_start >= 0) & (f_start < width))
        def _():
            d_start = pl.multiple_of(lax.rem(tile, d_blocks) * block, block)
            place = pl.ds(pl.multiple_of(f_start, block), block)
            total[:, place] += lax.dot_general(
                rows[:, pl.ds(d_start, block)],
                held[j],
                NT,
                preferred_element_type=jnp.float32,
            )

    first_chunk = wrap(me - 1, spans)
    for p in range(spans):
        result = total[p * chunk : (p + 1) * chunk].astype(out.dtype)
        out[chunk_at(p), :, here] = result

        @pl.when(chunk_at(p) == first_chunk)
        def _():
            first[:, here] = result


def matmul_call(sizes, low, high, width, table, held, weight, pieces):
    spans = sizes[0]
    tokens, d_width = sum(piece.shape[0] for piece in pieces), weight.shape[1]
    columns = (high - low) * width
    shapes = [
        jax.ShapeDtypeStruct((spans, tokens // spans, columns), jnp.bfloat16),
        jax.ShapeDtypeStruct((tokens // spans, columns), jnp.bfloat16),
    ]
    if len(pieces) > 1:
        shapes.append(jax.ShapeDtypeStruct((tokens, d_width), pieces[0].dtype))
    if weight.shape[0] == columns:
        weight_spec = vmem()
    else:
        weight, weight_spec = stay(weight), pl.BlockSpec((width, d_width), lambda i: (i + low, 0))
    return pl.pallas_call(
        functools.partial(matmul_kernel, sizes, low, width, len(pieces)),
        grid=(high - low,),
        out_shape=shapes,
        in_specs=[smem(), vmem(), weight_spec] + [vmem()] * len(pieces),
        out_specs=[vmem()] * len(shapes),
        scratch_shapes=[pltpu.VMEM((tokens, width), jnp.float32)],
        compiler_params=params(),
        cost_estimate=pl.CostEstimate(
            flops=2 * tokens * d_width * columns,
            bytes_accessed=2 * d_width * columns,
            transcendentals=0,
        ),
        name="partial",
    )(table, held, weight, *pieces)


def add_kernel(t, partials, arrived, out):
    spans = partials.shape[0]
    chunk = wrap(lax.axis_index("seq") - t, spans)
    result = partials[chunk].astype(jnp.float32) + arrived[...].astype(jnp.float32)
    out[...] = result.astype(out.dtype)


def add_call(t, partials, arrived):
    return pl.pallas_call(
        functools.partial(add_kernel, t),
        out_shape=jax.ShapeDtypeStruct(arrived.shape, arrived.dtype),
        in_specs=[vmem(), vmem()],
        out_specs=vmem(),
        compiler_params=params(),
        cost_estimate=cost(arrived.size),
        name="add",
    )(partials, arrived)


def last_kernel(low, partials, arrived, *refs):
    out, total, sem = refs[-3:]
    columns = partials.shape[2]
    result = partials[lax.axis_index("seq")].astype(jnp.float32) + arrived[...].astype(jnp.float32)
    total[...] = result.astype(out.dtype)
    copy = pltpu.make_async_copy(total, out.at[:, pl.ds(low, columns)], sem)
    copy.start()
    copy.wait()


def last_call(low, partials, arrived, out, shape):
    _, chunk, columns = partials.shape
    given = [] if out is None else [out]
    return pl.pallas_call(
        functools.partial(last_kernel, low),
        out_shape=shape,
        in_specs=[vmem()] * 2 + [hbm()] * len(given),
        out_specs=hbm(),
        scratch_shapes=[pltpu.VMEM((chunk, columns), shape.dtype), pltpu.SemaphoreType.DMA],
        input_output_aliases={2: 0} if given else {},
        compiler_params=params(),
        cost_estimate=cost(arrived.size),
        name="last_sum",
    )(partials, arrived, *given)


def grad_kernel(spans, slots, block, d_blocks, table, rows, *refs):
    hidden, outs, (cols,) = refs[:spans], refs[spans : 2 * spans], refs[2 * spans :]
    me = lax.axis_index("seq")
    count, before = live_count(table, me, slots), rank_before(table, me, spans, slots)
    chunk = rows.shape[0] // spans
    for s in range(spans):
        cols[s] = hidden[s][...]
    for s in range(spans):
        slot = wrap(lax.rem(me + s, spans) - lax.rem(before, spans), spans)
        outs[s][...] = jnp.zeros_like(outs[s])

        @pl.when(slot < count)
        def _():
            d_start = pl.multiple_of(lax.rem(table[me, slot], d_blocks) * block, block)
            total = jnp.zeros((block, block), jnp.float32)
            for p in range(spans):
                total = total + lax.dot_general(
                    cols[wrap(me - chunk_at(p), spans), slot],
                    rows[p * chunk : (p + 1) * chunk, pl.ds(d_start, block)],
                    TN,
                    preferred_element_type=jnp.float32,
                )
            outs[s][...] = total.astype(outs[s].dtype)


def grad_call(sizes, table, rows, hidden_cols):
    spans = sizes[0]
    slots, chunk, block = hidden_cols[0].shape
    return pl.pallas_call(
        functools.partial(grad_kernel, *sizes),
        out_shape=[jax.ShapeDtypeStruct((block, block), jnp.bfloat16)] * spans,
        in_specs=[smem()] + [vmem()] * (spans + 1),
        out_specs=[vmem()] * spans,
        scratch_shapes=[pltpu.VMEM((spans, slots, chunk, block), jnp.bfloat16)],
        compiler_params=params(),
        cost_estimate=cost(rows.size),
        name="tile_grad",
    )(table, rows, *hidden_cols)


def adam_kernel(spans, slots, table, *refs):
    arrived, refs = refs[:spans], refs[spans:]
    values, one, two, values_new, one_new, two_new, grads = refs
    me = lax.axis_index("seq")
    for s in range(spans):
        grads[s] = arrived[s][...]
    befores = [rank_before(table, region, spans, slots) for region in range(spans)]
    total = befores[-1] + live_count(table, spans - 1, slots)
    for owned in range(slots):
        rank = owned * spans + me
        source = jnp.int32(0)
        for region in range(1, spans):
            source = jnp.where(befores[region] <= rank, region, source)
        live = rank < total
        grad = grads[wrap(me - source, spans)].astype(jnp.float32)
        stored, old_one, old_two = values[owned], one[owned], two[owned]
        new_one = BETA_ONE * old_one + (1.0 - BETA_ONE) * grad
        new_two = BETA_TWO * old_two + (1.0 - BETA_TWO) * grad * grad
        stepped = (
            new_one
            / (1.0 - BETA_ONE**STEP)
            / (jnp.sqrt(new_two / (1.0 - BETA_TWO**STEP)) + EPSILON)
        )
        values_new[owned] = jnp.where(live, stored - RATE * stepped, stored)
        one_new[owned] = jnp.where(live, new_one, old_one)
        two_new[owned] = jnp.where(live, new_two, old_two)


def adam_call(sizes, table, grads, *states):
    spans, slots, block, _ = sizes
    tile = jax.ShapeDtypeStruct((slots, block, block), jnp.float32)
    return pl.pallas_call(
        functools.partial(adam_kernel, spans, slots),
        out_shape=(tile, tile, tile),
        in_specs=[smem()] + [vmem()] * (spans + 3),
        out_specs=(vmem(), vmem(), vmem()),
        scratch_shapes=[pltpu.VMEM((spans, block, block), jnp.bfloat16)],
        compiler_params=params(),
        cost_estimate=cost(slots * block * block),
        name="adam",
    )(table, *grads, *[state[0, 0] for state in states])


def take_from(array, axis, places):
    size = lax.axis_size(axis)
    return lax.ppermute(array, axis, [((i + places) % size, i) for i in range(size)])


def exchange(pieces):
    return [pieces[0]] + [take_from(pieces[s], "seq", -s) for s in range(1, len(pieces))]


def per_device(
    hidden_in, cotangent, down_weight, tile_ids, tile_live, values, moment_one, moment_two
):
    spans, cores = lax.axis_size("seq"), lax.axis_size("dp")
    slots, block = values.shape[2], values.shape[3]
    f_width, d_width = down_weight.shape
    d_blocks, f_blocks = d_width // block, f_width // block
    chunk = hidden_in.shape[0]
    sizes = (spans, slots, block, d_blocks)
    group = max(size for size in range(1, 5) if f_blocks % size == 0)
    width = group * block
    steps = f_blocks // group
    cuts = [(steps * part + 1) // PARTS for part in range(PARTS + 1)]
    ranges = list(zip(cuts[:-1], cuts[1:]))

    firsts = [take_from(cotangent, "tensor", t) for t in range(1, lax.axis_size("tensor"))]
    local = [take_from(cotangent, "dp", d) for d in range(1, cores)]

    values_half, hidden_here = pl.pallas_call(
        early_kernel,
        out_shape=[
            jax.ShapeDtypeStruct((slots, block, block), jnp.bfloat16),
            jax.ShapeDtypeStruct(hidden_in.shape, hidden_in.dtype),
        ],
        in_specs=[hbm(), hbm()],
        out_specs=[vmem(), vmem()],
        scratch_shapes=[
            pltpu.VMEM((slots, block, block), jnp.float32),
            pltpu.SemaphoreType.DMA((2,)),
        ],
        compiler_params=params(),
        cost_estimate=cost(hidden_in.size),
        name="early",
    )(stay(values[0, 0]), stay(hidden_in))
    stored = [values_half] + [take_from(values_half, "seq", s) for s in range(1, spans)]

    ids, values_half = lax.optimization_barrier((tile_ids[0], values_half))
    table = jnp.concatenate([ids, tile_live[0]], axis=1)
    table = lax.all_gather(table, "seq", axis=0, tiled=True)
    table, stored = lax.optimization_barrier((table, stored))
    picked = pl.pallas_call(
        functools.partial(pick_kernel, slots, block, d_blocks),
        out_shape=[jax.ShapeDtypeStruct((slots, chunk, block), jnp.bfloat16)] * spans,
        in_specs=[smem(), vmem()],
        out_specs=[vmem()] * spans,
        compiler_params=params(),
        cost_estimate=cost(hidden_in.size),
        name="pick",
    )(table, hidden_here)
    hidden_cols = exchange(picked)

    stored, hidden_cols[1] = lax.optimization_barrier((stored, hidden_cols[1]))
    local_rows, first_weight, held = pl.pallas_call(
        functools.partial(lay_kernel, spans, slots),
        out_shape=[
            jax.ShapeDtypeStruct((cores * chunk, d_width), cotangent.dtype),
            jax.ShapeDtypeStruct((ranges[0][1] * width, d_width), down_weight.dtype),
            jax.ShapeDtypeStruct((slots, block, block), jnp.bfloat16),
        ],
        in_specs=[smem(), hbm(), hbm()] + [vmem()] * (cores - 1 + spans),
        out_specs=[vmem()] * 3,
        scratch_shapes=[pltpu.SemaphoreType.DMA((2,))],
        compiler_params=params(),
        cost_estimate=cost(cores * chunk * d_width),
        name="lay",
    )(table, stay(cotangent), stay(down_weight), *local, *stored)

    firsts, picked = lax.optimization_barrier((firsts, picked))
    pieces = [local_rows]
    for first in firsts:
        pieces += [first] + [take_from(first, "dp", d) for d in range(1, cores)]

    partials, moving = [], []
    for part, (low, high) in enumerate(ranges):
        if part == 0:
            pieces, hidden_cols[-1] = lax.optimization_barrier((pieces, hidden_cols[-1]))
        if part == 1:
            rows, hidden_cols = lax.optimization_barrier((rows, hidden_cols))
        if part == 2:
            moving[0] = add_call(2, partials[0], moving[0])
            rows, moving[0] = lax.optimization_barrier((rows, moving[0]))
        weight = down_weight if part else first_weight
        partial, first, *more = matmul_call(
            sizes, low, high, width, table, held, weight, [rows] if part else pieces
        )
        rows = more[0] if more else rows
        partials.append(partial)
        moving.append(take_from(first, "seq", -1))

    grads = exchange(grad_call(sizes, table, rows, hidden_cols))
    for t in range(2, spans):
        for part in range(len(ranges)):
            if (t, part) == (spans - 1, len(ranges) - 1):
                moving[part], grads = lax.optimization_barrier((moving[part], grads))
            if (t, part) != (2, 0):
                moving[part] = add_call(t, partials[part], moving[part])
            moving[part] = take_from(moving[part], "seq", -1)

    new = adam_call(sizes, table, grads, values, moment_one, moment_two)

    hidden_grad = None
    shape = jax.ShapeDtypeStruct((chunk, f_width), jnp.bfloat16)
    for part, (low, _) in enumerate(ranges):
        hidden_grad = last_call(low * width, partials[part], moving[part], hidden_grad, shape)
    return (hidden_grad,) + tuple(array[None, None] for array in new)


def solution(mesh):
    shards = P(("groups", "seq"), ("tensor", "dp"))
    tiles = P(("groups", "seq"), ("tensor", "dp"), None, None, None)
    lists = P(("groups", "seq"), ("tensor", "dp"), None)
    return jax.shard_map(
        per_device,
        mesh=mesh,
        in_specs=(
            shards,
            P(("groups", "tensor", "dp"), "seq"),
            P(("tensor", "dp"), "seq"),
            lists,
            lists,
            tiles,
            tiles,
            tiles,
        ),
        out_specs=(shards, tiles, tiles, tiles),
        check_vma=False,
    )
```

```python
import functools

import jax
import jax.numpy as jnp
from jax import lax
from jax.experimental import pallas as pl
from jax.experimental.pallas import tpu as pltpu
from jax.sharding import PartitionSpec as P

STEP = 100
BETA_ONE = 0.9
BETA_TWO = 0.999
RATE = 0.01
EPSILON = 1e-08
VMEM_LIMIT = 24 * 1024 * 1024
PARTS = 3
RIDE = 1
WAIT = 2000
NT = (((1,), (1,)), ((), ()))
TN = (((0,), (0,)), ((), ()))


def vmem():
    return pl.BlockSpec(memory_space=pltpu.VMEM)


def smem():
    return pl.BlockSpec(memory_space=pltpu.SMEM)


def hbm():
    return pl.BlockSpec(memory_space=pltpu.HBM)


def stay(array):
    return pltpu.with_memory_space_constraint(array, pltpu.HBM)


def cost(count):
    return pl.CostEstimate(flops=count, bytes_accessed=2 * count, transcendentals=0)


def params():
    return pltpu.CompilerParams(vmem_limit_bytes=VMEM_LIMIT)


def wrap(index, size):
    return lax.rem(index + size, size)


def live_count(table, row, slots):
    count = table[row, 2 * slots]
    for slot in range(1, slots):
        count = count + table[row, 2 * slots + slot]
    return count


def rank_before(table, row, spans, slots):
    me = lax.axis_index("seq")
    before = jnp.int32(0)
    for other in range(spans):
        ahead = wrap(me - other, spans) < wrap(me - row, spans)
        before = before + jnp.where(ahead, live_count(table, other, slots), 0)
    return before


def early_kernel(d_blocks, ids, live, values, hidden, out, hidden_here, stored, sems):
    value_copy = pltpu.make_async_copy(values, stored, sems.at[0])
    hidden_copy = pltpu.make_async_copy(hidden, hidden_here, sems.at[1])
    value_copy.start()
    hidden_copy.start()
    slots, block, _ = stored.shape
    tail = (out.shape[0] - slots * block, block)
    lane = lax.broadcasted_iota(jnp.int32, tail, 1)
    lists = jnp.zeros(tail, jnp.int32)
    for j in range(slots):
        lists = jnp.where(lane == j, lax.div(ids[0, j], d_blocks), lists)
        lists = jnp.where(lane == slots + j, lax.rem(ids[0, j], d_blocks), lists)
        lists = jnp.where(lane == 2 * slots + j, live[0, j], lists)
    out[slots * block :] = lists.astype(jnp.float32).astype(out.dtype)
    value_copy.wait()
    for j in range(slots):
        out[j * block : (j + 1) * block] = stored[j].astype(out.dtype)
    hidden_copy.wait()


def pick_kernel(spans, slots, block, *refs):
    stored, hidden, table, outs = refs[:spans], refs[spans], refs[spans + 1], refs[spans + 2 : -2]
    lists, sem = refs[-2:]
    for s in range(spans):
        tail = stored[s][slots * block :].astype(jnp.float32).astype(jnp.int32)
        lists[s : s + 1] = tail[:1]
    copy = pltpu.make_async_copy(lists, table, sem)
    copy.start()
    copy.wait()
    for s in range(spans):
        for j in range(slots):
            start = pl.multiple_of(table[(spans - s) % spans, j] * block, block)
            outs[s][j] = hidden[:, pl.ds(start, block)]


def lay_kernel(own, weight, *refs):
    others, (rows, first_weight, sems) = refs[:-3], refs[-3:]
    chunk = own.shape[0]
    weight_copy = pltpu.make_async_copy(
        weight.at[pl.ds(0, first_weight.shape[0])], first_weight, sems.at[0]
    )
    weight_copy.start()
    own_copy = pltpu.make_async_copy(own, rows.at[pl.ds(0, chunk)], sems.at[1])
    own_copy.start()
    for p, other in enumerate(others):
        rows[(p + 1) * chunk : (p + 2) * chunk] = other[...]
    own_copy.wait()
    weight_copy.wait()


def chunk_at(place):
    tensors, cores = lax.axis_size("tensor"), lax.axis_size("dp")
    t_place = lax.rem(lax.axis_index("tensor") + place // cores, tensors)
    d_place = lax.rem(lax.axis_index("dp") + place % cores, cores)
    return t_place * cores + d_place


def matmul_kernel(sizes, low, width, counts, table, weight, *refs):
    spans, slots, block = sizes
    step = pl.program_id(0)
    me = lax.axis_index("seq")
    pieces, stores, riders = counts
    given, refs = refs[:pieces], refs[pieces:]
    stored, refs = refs[:stores], refs[stores:]
    riding, refs = refs[:riders], refs[riders:]
    if stores:
        out, first, rows, held, total = refs

        @pl.when(step == 0)
        def _():
            at = 0
            for piece in given:
                rows[at : at + piece.shape[0]] = piece[...]
                at += piece.shape[0]
            before = rank_before(table, 0, spans, slots)
            for j in range(slots):
                rank = before + j
                owned = jnp.minimum(lax.div(rank, spans), slots - 1)
                place = pl.ds(pl.multiple_of(owned * block, block), block)
                for s in range(spans):

                    @pl.when(lax.rem(rank, spans) == wrap(me - s, spans))
                    def _():
                        held[j] = stored[s][place]

    else:
        (rows, held), (out, first, total) = given, refs
    chunk = rows.shape[0] // spans
    here = pl.ds(pl.multiple_of(step * width, width), width)
    weights = weight[here] if weight.shape[0] > width else weight[...]
    total[...] = lax.dot_general(rows[...], weights, NT, preferred_element_type=jnp.float32)
    count = live_count(table, 0, slots)
    for j in range(slots):
        f_start = table[0, j] * block - (low + step) * width

        @pl.when((j < count) & (f_start >= 0) & (f_start < width))
        def _():
            d_start = pl.multiple_of(table[0, slots + j] * block, block)
            place = pl.ds(pl.multiple_of(f_start, block), block)
            total[:, place] += lax.dot_general(
                rows[:, pl.ds(d_start, block)], held[j], NT, preferred_element_type=jnp.float32
            )

    first_chunk = wrap(me - 1, spans)
    for p in range(spans):
        result = total[p * chunk : (p + 1) * chunk].astype(out.dtype)
        out[chunk_at(p), :, here] = result

        @pl.when(chunk_at(p) == first_chunk)
        def _():
            first[:, here] = result

    at = out.shape[2]
    for rider in riding:
        first[:, at : at + block] = rider[...]
        at += block


def matmul_call(sizes, low, high, width, table, weight, given, stored=(), riding=()):
    spans, slots, block = sizes
    tokens = sum(piece.shape[0] for piece in given) if stored else given[0].shape[0]
    d_width, columns = weight.shape[1], (high - low) * width
    half = jnp.bfloat16
    shapes = [
        jax.ShapeDtypeStruct((spans, tokens // spans, columns), half),
        jax.ShapeDtypeStruct((tokens // spans, columns + len(riding) * block), half),
    ]
    if stored:
        shapes.append(jax.ShapeDtypeStruct((tokens, d_width), half))
        shapes.append(jax.ShapeDtypeStruct((slots, block, block), half))
    if weight.shape[0] == columns:
        weight_spec = vmem()
    else:
        weight, weight_spec = stay(weight), pl.BlockSpec((width, d_width), lambda i: (i + low, 0))
    inputs = [*given, *stored, *riding]
    return pl.pallas_call(
        functools.partial(
            matmul_kernel, sizes, low, width, (len(given), len(stored), len(riding))
        ),
        grid=(high - low,),
        out_shape=shapes,
        in_specs=[smem(), weight_spec] + [vmem()] * len(inputs),
        out_specs=[vmem()] * len(shapes),
        scratch_shapes=[pltpu.VMEM((tokens, width), jnp.float32)],
        compiler_params=params(),
        cost_estimate=pl.CostEstimate(
            flops=2 * tokens * d_width * columns,
            bytes_accessed=2 * d_width * columns,
            transcendentals=0,
        ),
        name="partial",
    )(table, weight, *inputs)


def add_kernel(t, riders, partials, arrived, out, *mine):
    spans, _, columns = partials.shape
    chunk = wrap(lax.axis_index("seq") - t, spans)
    result = partials[chunk].astype(jnp.float32) + arrived[:, :columns].astype(jnp.float32)
    out[:, :columns] = result.astype(out.dtype)
    if riders:
        block = mine[0].shape[1]
        mine[0][...] = arrived[:, columns : columns + block]
        out[:, columns:] = arrived[:, columns + block :]


def add_call(t, partials, arrived, block):
    chunk, columns = partials.shape[1:]
    riders = (arrived.shape[1] - columns) // block
    shapes = [jax.ShapeDtypeStruct((chunk, arrived.shape[1] - min(riders, 1) * block), arrived.dtype)]
    if riders:
        shapes.append(jax.ShapeDtypeStruct((chunk, block), arrived.dtype))
    return pl.pallas_call(
        functools.partial(add_kernel, t, riders),
        out_shape=shapes,
        in_specs=[vmem(), vmem()],
        out_specs=[vmem()] * len(shapes),
        compiler_params=params(),
        cost_estimate=cost(arrived.size),
        name="add",
    )(partials, arrived)


def last_kernel(low, partials, arrived, *refs):
    out, total, sem = refs[-3:]
    columns = partials.shape[2]
    result = partials[lax.axis_index("seq")].astype(jnp.float32)
    result = result + arrived[:, :columns].astype(jnp.float32)
    total[...] = result.astype(out.dtype)
    copy = pltpu.make_async_copy(total, out.at[:, pl.ds(low, columns)], sem)
    copy.start()
    copy.wait()


def last_call(low, partials, arrived, out, shape):
    _, chunk, columns = partials.shape
    given = [] if out is None else [out]
    return pl.pallas_call(
        functools.partial(last_kernel, low),
        out_shape=shape,
        in_specs=[vmem()] * 2 + [hbm()] * len(given),
        out_specs=hbm(),
        scratch_shapes=[pltpu.VMEM((chunk, columns), shape.dtype), pltpu.SemaphoreType.DMA],
        input_output_aliases={2: 0} if given else {},
        compiler_params=params(),
        cost_estimate=cost(arrived.size),
        name="last_sum",
    )(partials, arrived, *given)


def grad_kernel(spans, slots, block, table, rows, *refs):
    hidden, outs, (cols,) = refs[:spans], refs[spans : 2 * spans], refs[2 * spans :]
    me = lax.axis_index("seq")
    count, before = live_count(table, 0, slots), rank_before(table, 0, spans, slots)
    chunk = rows.shape[0] // spans
    for s in range(spans):
        cols[s] = hidden[s][...]
    for s in range(spans):
        slot = wrap(lax.rem(me + s, spans) - lax.rem(before, spans), spans)
        outs[s][...] = jnp.zeros_like(outs[s])

        @pl.when(slot < count)
        def _():
            d_start = pl.multiple_of(table[0, slots + slot] * block, block)
            total = jnp.zeros((block, block), jnp.float32)
            for p in range(spans):
                total = total + lax.dot_general(
                    cols[wrap(me - chunk_at(p), spans), slot],
                    rows[p * chunk : (p + 1) * chunk, pl.ds(d_start, block)],
                    TN,
                    preferred_element_type=jnp.float32,
                )
            outs[s][...] = total.astype(outs[s].dtype)


def grad_call(sizes, table, rows, hidden_cols):
    spans = sizes[0]
    slots, chunk, block = hidden_cols[0].shape
    return pl.pallas_call(
        functools.partial(grad_kernel, *sizes),
        out_shape=[jax.ShapeDtypeStruct((block, block), jnp.bfloat16)] * spans,
        in_specs=[smem()] + [vmem()] * (spans + 1),
        out_specs=[vmem()] * spans,
        scratch_shapes=[pltpu.VMEM((spans, slots, chunk, block), jnp.bfloat16)],
        compiler_params=params(),
        cost_estimate=cost(WAIT * rows.size),
        name="tile_grad",
    )(table, rows, *hidden_cols)


def adam_kernel(spans, slots, columns, table, *refs):
    arrived, refs = refs[:spans], refs[spans:]
    values, one, two, values_new, one_new, two_new, grads = refs
    me = lax.axis_index("seq")
    for s in range(spans - 1):
        grads[s] = arrived[s][...]
    grads[spans - 1] = arrived[-1][:, columns:]
    befores = [rank_before(table, s, spans, slots) for s in range(spans)]
    counts = [live_count(table, s, slots) for s in range(spans)]
    for owned in range(slots):
        rank = owned * spans + me
        source, live = jnp.int32(0), jnp.int32(0)
        for s in range(spans):
            holds = (befores[s] <= rank) & (rank < befores[s] + counts[s])
            source, live = jnp.where(holds, s, source), jnp.where(holds, 1, live)
        grad = grads[source].astype(jnp.float32)
        stored, old_one, old_two = values[owned], one[owned], two[owned]
        new_one = BETA_ONE * old_one + (1.0 - BETA_ONE) * grad
        new_two = BETA_TWO * old_two + (1.0 - BETA_TWO) * grad * grad
        stepped = (
            new_one
            / (1.0 - BETA_ONE**STEP)
            / (jnp.sqrt(new_two / (1.0 - BETA_TWO**STEP)) + EPSILON)
        )
        values_new[owned] = jnp.where(live > 0, stored - RATE * stepped, stored)
        one_new[owned] = jnp.where(live > 0, new_one, old_one)
        two_new[owned] = jnp.where(live > 0, new_two, old_two)


def adam_call(sizes, columns, table, grads, *states):
    spans, slots, block = sizes
    tile = jax.ShapeDtypeStruct((slots, block, block), jnp.float32)
    return pl.pallas_call(
        functools.partial(adam_kernel, spans, slots, columns),
        out_shape=(tile, tile, tile),
        in_specs=[smem()] + [vmem()] * (spans + 3),
        out_specs=(vmem(), vmem(), vmem()),
        scratch_shapes=[pltpu.VMEM((spans, block, block), jnp.bfloat16)],
        compiler_params=params(),
        cost_estimate=cost(slots * block * block),
        name="adam",
    )(table, *grads, *[state[0, 0] for state in states])


def take_from(array, axis, places):
    size = lax.axis_size(axis)
    return lax.ppermute(array, axis, [((i + places) % size, i) for i in range(size)])


def exchange(pieces):
    return [pieces[0]] + [take_from(pieces[s], "seq", -s) for s in range(1, len(pieces))]


def per_device(
    hidden_in, cotangent, down_weight, tile_ids, tile_live, values, moment_one, moment_two
):
    spans, cores = lax.axis_size("seq"), lax.axis_size("dp")
    slots, block = values.shape[2], values.shape[3]
    f_width, d_width = down_weight.shape
    d_blocks, f_blocks = d_width // block, f_width // block
    chunk = hidden_in.shape[0]
    sizes = (spans, slots, block)
    group = max(size for size in range(1, 5) if f_blocks % size == 0)
    width = group * block
    steps = f_blocks // group
    cuts = [(steps * part + 2) // PARTS for part in range(PARTS + 1)]
    ranges = list(zip(cuts[:-1], cuts[1:]))

    firsts = [take_from(cotangent, "tensor", t) for t in range(1, lax.axis_size("tensor"))]
    local = [take_from(cotangent, "dp", d) for d in range(1, cores)]

    payload, hidden_here = pl.pallas_call(
        functools.partial(early_kernel, d_blocks),
        out_shape=[
            jax.ShapeDtypeStruct((slots * block + 16, block), jnp.bfloat16),
            jax.ShapeDtypeStruct(hidden_in.shape, hidden_in.dtype),
        ],
        in_specs=[smem(), smem(), hbm(), hbm()],
        out_specs=[vmem(), vmem()],
        scratch_shapes=[
            pltpu.VMEM((slots, block, block), jnp.float32),
            pltpu.SemaphoreType.DMA((2,)),
        ],
        compiler_params=params(),
        cost_estimate=cost(hidden_in.size),
        name="early",
    )(tile_ids[0], tile_live[0], stay(values[0, 0]), stay(hidden_in))
    stored = exchange([payload] * spans)
    local_rows, first_weight = pl.pallas_call(
        lay_kernel,
        out_shape=[
            jax.ShapeDtypeStruct((cores * chunk, d_width), cotangent.dtype),
            jax.ShapeDtypeStruct((ranges[0][1] * width, d_width), down_weight.dtype),
        ],
        in_specs=[hbm(), hbm()] + [vmem()] * (cores - 1),
        out_specs=[vmem(), vmem()],
        scratch_shapes=[pltpu.SemaphoreType.DMA((2,))],
        compiler_params=params(),
        cost_estimate=cost(cores * chunk * d_width),
        name="lay",
    )(stay(cotangent), stay(down_weight), *local)

    firsts, stored, local_rows, first_weight = lax.optimization_barrier(
        (firsts, stored, local_rows, first_weight)
    )
    pieces = [local_rows]
    for first in firsts:
        pieces += [first] + [take_from(first, "dp", d) for d in range(1, cores)]

    table, *picked = pl.pallas_call(
        functools.partial(pick_kernel, *sizes),
        out_shape=[jax.ShapeDtypeStruct((spans, block), jnp.int32)]
        + [jax.ShapeDtypeStruct((slots, chunk, block), jnp.bfloat16)] * spans,
        in_specs=[vmem()] * (spans + 1),
        out_specs=[smem()] + [vmem()] * spans,
        scratch_shapes=[pltpu.VMEM((spans, block), jnp.int32), pltpu.SemaphoreType.DMA],
        compiler_params=params(),
        cost_estimate=cost(hidden_in.size),
        name="pick",
    )(*stored, hidden_here)
    hidden_cols = exchange(picked)

    partials, moving, grads = [], [], None
    for part, (low, high) in enumerate(ranges):
        if part == 0:
            partial, first, rows, held = matmul_call(
                sizes, low, high, width, table, first_weight, pieces, stored
            )
        else:
            riding = []
            if part == RIDE:
                grads = grad_call(sizes, table, rows, hidden_cols)
                riding = grads[1:]
            else:
                moving[0] = add_call(2, partials[0], moving[0], block)[0]
                rows, moving[0] = lax.optimization_barrier((rows, moving[0]))
            partial, first = matmul_call(
                sizes, low, high, width, table, down_weight, [rows, held], riding=riding
            )
        partials.append(partial)
        moving.append(take_from(first, "seq", -1))

    tiles = [grads[0]]
    for t in range(2, spans):
        for part in range(len(ranges)):
            if (t, part) != (2, 0):
                moving[part], *mine = add_call(t, partials[part], moving[part], block)
                tiles += mine
            moving[part] = take_from(moving[part], "seq", -1)
    tiles.append(moving[RIDE])
    new = adam_call(
        sizes, partials[RIDE].shape[2], table, tiles, values, moment_one, moment_two
    )

    hidden_grad = None
    shape = jax.ShapeDtypeStruct((chunk, f_width), jnp.bfloat16)
    for part, (low, _) in enumerate(ranges):
        if part == len(ranges) - 1:
            moving[part], new = lax.optimization_barrier((moving[part], new))
        hidden_grad = last_call(low * width, partials[part], moving[part], hidden_grad, shape)
    return (hidden_grad,) + tuple(array[None, None] for array in new)


def solution(mesh):
    shards = P(("groups", "seq"), ("tensor", "dp"))
    tiles = P(("groups", "seq"), ("tensor", "dp"), None, None, None)
    lists = P(("groups", "seq"), ("tensor", "dp"), None)
    return jax.shard_map(
        per_device,
        mesh=mesh,
        in_specs=(
            shards,
            P(("groups", "tensor", "dp"), "seq"),
            P(("tensor", "dp"), "seq"),
            lists,
            lists,
            tiles,
            tiles,
            tiles,
        ),
        out_specs=(shards, tiles, tiles, tiles),
        check_vma=False,
    )
```

```python
import functools

import jax
import jax.numpy as jnp
from jax import lax
from jax.experimental import pallas as pl
from jax.experimental.pallas import tpu as pltpu
from jax.sharding import PartitionSpec as P

STEP = 100
BETA_ONE = 0.9
BETA_TWO = 0.999
RATE = 0.01
EPSILON = 1e-08
VMEM_LIMIT = 24 * 1024 * 1024
WAIT = 2000
LAG = 2
NT = (((1,), (1,)), ((), ()))
TN = (((0,), (0,)), ((), ()))


def vmem():
    return pl.BlockSpec(memory_space=pltpu.VMEM)


def smem():
    return pl.BlockSpec(memory_space=pltpu.SMEM)


def hbm():
    return pl.BlockSpec(memory_space=pltpu.HBM)


def stay(array):
    return pltpu.with_memory_space_constraint(array, pltpu.HBM)


def cost(count):
    return pl.CostEstimate(flops=count, bytes_accessed=2 * count, transcendentals=0)


def params():
    return pltpu.CompilerParams(vmem_limit_bytes=VMEM_LIMIT)


def wrap(index, size):
    return lax.rem(index + size, size)


def live_count(table, row, slots):
    count = table[row, 2 * slots]
    for slot in range(1, slots):
        count = count + table[row, 2 * slots + slot]
    return count


def rank_before(table, row, spans, slots):
    me = lax.axis_index("seq")
    before = jnp.int32(0)
    for other in range(spans):
        ahead = wrap(me - other, spans) < wrap(me - row, spans)
        before = before + jnp.where(ahead, live_count(table, other, slots), 0)
    return before


def early_kernel(values, hidden, values_half, hidden_here, stored, sems):
    value_copy = pltpu.make_async_copy(values, stored, sems.at[0])
    hidden_copy = pltpu.make_async_copy(hidden, hidden_here, sems.at[1])
    value_copy.start()
    hidden_copy.start()
    value_copy.wait()
    values_half[...] = stored[...].astype(values_half.dtype)
    hidden_copy.wait()


def pick_kernel(spans, slots, block, d_blocks, *refs):
    metas, (values, hidden, table), outs = refs[:spans], refs[spans : spans + 3], refs[spans + 3 :]
    me = lax.axis_index("seq")
    for s in range(spans):
        for j in range(slots):
            table[s, j] = lax.div(metas[s][0, j], d_blocks)
            table[s, slots + j] = lax.rem(metas[s][0, j], d_blocks)
            table[s, 2 * slots + j] = metas[s][0, slots + j]
    for s in range(spans):
        row = (spans - s) % spans
        before = rank_before(table, row, spans, slots)
        slot = wrap(me - lax.rem(before, spans), spans)
        tile = values[jnp.minimum(lax.div(before + slot, spans), slots - 1)]
        live = slot < live_count(table, row, slots)
        outs[s][...] = jnp.where(live, tile.astype(jnp.float32), 0.0).astype(tile.dtype)
        for j in range(slots):
            start = pl.multiple_of(table[row, j] * block, block)
            outs[spans + s][j] = hidden[:, pl.ds(start, block)]


def lay_kernel(own, weight, *refs):
    others, (rows, first_weight, sems) = refs[:-3], refs[-3:]
    chunk = own.shape[0]
    weight_copy = pltpu.make_async_copy(
        weight.at[pl.ds(0, first_weight.shape[0])], first_weight, sems.at[0]
    )
    weight_copy.start()
    own_copy = pltpu.make_async_copy(own, rows.at[pl.ds(0, chunk)], sems.at[1])
    own_copy.start()
    for p, other in enumerate(others):
        rows[(p + 1) * chunk : (p + 2) * chunk] = other[...]
    own_copy.wait()
    weight_copy.wait()


def chunk_at(place):
    tensors, cores = lax.axis_size("tensor"), lax.axis_size("dp")
    t_place = lax.rem(lax.axis_index("tensor") + place // cores, tensors)
    d_place = lax.rem(lax.axis_index("dp") + place % cores, cores)
    return t_place * cores + d_place


def matmul_kernel(sizes, low, width, firsts_of, stores, table, weight, *refs):
    spans, slots, block = sizes
    step = pl.program_id(0)
    me = lax.axis_index("seq")
    if stores:
        given, stored, (out, first, rows, held, total) = refs[: -stores - 5], refs[-stores - 5 : -5], refs[-5:]

        @pl.when(step == 0)
        def _():
            at = 0
            for piece in given:
                rows[at : at + piece.shape[0]] = piece[...]
                at += piece.shape[0]
            before = rank_before(table, 0, spans, slots)
            for j in range(slots):
                for s in range(spans):

                    @pl.when(lax.rem(before + j, spans) == wrap(me - s, spans))
                    def _():
                        held[j] = stored[s][...]

    else:
        rows, held, out, first, total = refs
    chunk = rows.shape[0] // spans
    here = pl.ds(pl.multiple_of(step * width, width), width)
    weights = weight[here] if weight.shape[0] > width else weight[...]
    total[...] = lax.dot_general(rows[...], weights, NT, preferred_element_type=jnp.float32)
    count = live_count(table, 0, slots)
    for j in range(slots):
        f_start = table[0, j] * block - (low + step) * width

        @pl.when((j < count) & (f_start >= 0) & (f_start < width))
        def _():
            d_start = pl.multiple_of(table[0, slots + j] * block, block)
            place = pl.ds(pl.multiple_of(f_start, block), block)
            total[:, place] += lax.dot_general(
                rows[:, pl.ds(d_start, block)], held[j], NT, preferred_element_type=jnp.float32
            )

    for p in range(spans):
        result = total[p * chunk : (p + 1) * chunk].astype(out.dtype)
        out[chunk_at(p), :, here] = result
        for k, first_chunk in enumerate(firsts_of(me)):

            @pl.when(chunk_at(p) == first_chunk)
            def _():
                first[k, :, here] = result


def matmul_call(sizes, low, high, width, firsts_of, table, weight, given, stored=()):
    spans, slots, block = sizes
    tokens = sum(piece.shape[0] for piece in given) if stored else given[0].shape[0]
    d_width, columns = weight.shape[1], (high - low) * width
    half = jnp.bfloat16
    shapes = [
        jax.ShapeDtypeStruct((spans, tokens // spans, columns), half),
        jax.ShapeDtypeStruct((len(firsts_of(0)), tokens // spans, columns), half),
    ]
    if stored:
        shapes.append(jax.ShapeDtypeStruct((tokens, d_width), half))
        shapes.append(jax.ShapeDtypeStruct((slots, block, block), half))
    if weight.shape[0] == columns:
        weight_spec = vmem()
    else:
        weight, weight_spec = stay(weight), pl.BlockSpec((width, d_width), lambda i: (i + low, 0))
    inputs = [*given, *stored]
    return pl.pallas_call(
        functools.partial(matmul_kernel, sizes, low, width, firsts_of, len(stored)),
        grid=(high - low,),
        out_shape=shapes,
        in_specs=[smem(), weight_spec] + [vmem()] * len(inputs),
        out_specs=[vmem()] * len(shapes),
        scratch_shapes=[pltpu.VMEM((tokens, width), jnp.float32)],
        compiler_params=params(),
        cost_estimate=pl.CostEstimate(
            flops=2 * tokens * d_width * columns,
            bytes_accessed=2 * d_width * columns,
            transcendentals=0,
        ),
        name="partial",
    )(table, weight, *inputs)


def add_kernel(chunks_of, partials, arrived, out):
    for k, chunk in enumerate(chunks_of(lax.axis_index("seq"))):
        result = partials[chunk].astype(jnp.float32) + arrived[k].astype(jnp.float32)
        out[k] = result.astype(out.dtype)


def add_call(chunks_of, partials, arrived):
    shape = (len(chunks_of(0)), *arrived.shape[1:])
    return pl.pallas_call(
        functools.partial(add_kernel, chunks_of),
        out_shape=jax.ShapeDtypeStruct(shape, arrived.dtype),
        in_specs=[vmem(), vmem()],
        out_specs=vmem(),
        compiler_params=params(),
        cost_estimate=cost(arrived.size),
        name="add",
    )(partials, arrived)


def last_kernel(low, places, partials, *refs):
    out, total, sem = refs[-3:]
    result = partials[lax.axis_index("seq")].astype(jnp.float32)
    for arrived, place in zip(refs, places):
        result = result + arrived[place].astype(jnp.float32)
    total[...] = result.astype(out.dtype)
    copy = pltpu.make_async_copy(total, out.at[:, pl.ds(low, total.shape[1])], sem)
    copy.start()
    copy.wait()


def last_call(low, partials, arrivals, out, shape):
    _, chunk, columns = partials.shape
    given = [] if out is None else [out]
    arrived, places = zip(*arrivals)
    return pl.pallas_call(
        functools.partial(last_kernel, low, places),
        out_shape=shape,
        in_specs=[vmem()] * (1 + len(arrived)) + [hbm()] * len(given),
        out_specs=hbm(),
        scratch_shapes=[pltpu.VMEM((chunk, columns), shape.dtype), pltpu.SemaphoreType.DMA],
        input_output_aliases={1 + len(arrived): 0} if given else {},
        compiler_params=params(),
        cost_estimate=cost(partials.size),
        name="last_sum",
    )(partials, *arrived, *given)


def grad_kernel(spans, slots, block, table, rows, *refs):
    hidden, outs, (cols,) = refs[:spans], refs[spans : 2 * spans], refs[2 * spans :]
    me = lax.axis_index("seq")
    count, before = live_count(table, 0, slots), rank_before(table, 0, spans, slots)
    chunk = rows.shape[0] // spans
    for s in range(spans):
        cols[s] = hidden[s][...]
    for s in range(spans):
        slot = wrap(lax.rem(me + s, spans) - lax.rem(before, spans), spans)
        outs[s][...] = jnp.zeros_like(outs[s])

        @pl.when(slot < count)
        def _():
            d_start = pl.multiple_of(table[0, slots + slot] * block, block)
            total = jnp.zeros((block, block), jnp.float32)
            for p in range(spans):
                total = total + lax.dot_general(
                    cols[wrap(me - chunk_at(p), spans), slot],
                    rows[p * chunk : (p + 1) * chunk, pl.ds(d_start, block)],
                    TN,
                    preferred_element_type=jnp.float32,
                )
            outs[s][...] = total.astype(outs[s].dtype)


def grad_call(sizes, table, rows, hidden_cols):
    spans = sizes[0]
    slots, chunk, block = hidden_cols[0].shape
    return pl.pallas_call(
        functools.partial(grad_kernel, *sizes),
        out_shape=[jax.ShapeDtypeStruct((block, block), jnp.bfloat16)] * spans,
        in_specs=[smem()] + [vmem()] * (spans + 1),
        out_specs=[vmem()] * spans,
        scratch_shapes=[pltpu.VMEM((spans, slots, chunk, block), jnp.bfloat16)],
        compiler_params=params(),
        cost_estimate=cost(WAIT * rows.size),
        name="tile_grad",
    )(table, rows, *hidden_cols)


def adam_kernel(spans, slots, table, *refs):
    arrived, refs = refs[:spans], refs[spans:]
    values, one, two, values_new, one_new, two_new, grads = refs
    me = lax.axis_index("seq")
    for s in range(spans):
        grads[s] = arrived[s][...]
    befores = [rank_before(table, s, spans, slots) for s in range(spans)]
    counts = [live_count(table, s, slots) for s in range(spans)]
    for owned in range(slots):
        rank = owned * spans + me
        source, live = jnp.int32(0), jnp.int32(0)
        for s in range(spans):
            holds = (befores[s] <= rank) & (rank < befores[s] + counts[s])
            source, live = jnp.where(holds, s, source), jnp.where(holds, 1, live)
        grad = grads[source].astype(jnp.float32)
        stored, old_one, old_two = values[owned], one[owned], two[owned]
        new_one = BETA_ONE * old_one + (1.0 - BETA_ONE) * grad
        new_two = BETA_TWO * old_two + (1.0 - BETA_TWO) * grad * grad
        stepped = (
            new_one
            / (1.0 - BETA_ONE**STEP)
            / (jnp.sqrt(new_two / (1.0 - BETA_TWO**STEP)) + EPSILON)
        )
        values_new[owned] = jnp.where(live > 0, stored - RATE * stepped, stored)
        one_new[owned] = jnp.where(live > 0, new_one, old_one)
        two_new[owned] = jnp.where(live > 0, new_two, old_two)


def adam_call(sizes, table, grads, *states):
    spans, slots, block = sizes
    tile = jax.ShapeDtypeStruct((slots, block, block), jnp.float32)
    return pl.pallas_call(
        functools.partial(adam_kernel, spans, slots),
        out_shape=(tile, tile, tile),
        in_specs=[smem()] + [vmem()] * (spans + 3),
        out_specs=(vmem(), vmem(), vmem()),
        scratch_shapes=[pltpu.VMEM((spans, block, block), jnp.bfloat16)],
        compiler_params=params(),
        cost_estimate=cost(slots * block * block),
        name="adam",
    )(table, *grads, *[state[0, 0] for state in states])


def take_from(array, axis, places):
    size = lax.axis_size(axis)
    return lax.ppermute(array, axis, [((i + places) % size, i) for i in range(size)])


def exchange(pieces):
    return [pieces[0]] + [take_from(pieces[s], "seq", -s) for s in range(1, len(pieces))]


class Ring:
    parts = [2, 3, 2]

    def __init__(self, spans):
        self.spans, self.steps = spans, spans - 1

    def first(self, me):
        return [wrap(me - 1, self.spans)]

    def move(self, step, sums):
        return take_from(sums, "seq", -1)

    def add(self, step, partials, moved):
        return add_call(lambda me: [wrap(me - step - 1, self.spans)], partials, moved[-1])

    def last(self, moved):
        return [(moved[-1], 0)]


class Line:
    parts = [2, 2, 2, 1]
    steps = 3

    def first(self, me):
        return [jnp.where(me < 2, 3, 0), jnp.where(me < 2, 2, 1)]

    def move(self, step, sums):
        pairs = [[(0, 1), (3, 2)], [(1, 2), (2, 1)], [(0, 1), (1, 0), (2, 3), (3, 2)]]
        return lax.ppermute(sums, "seq", pairs[step])

    def add(self, step, partials, moved):
        chunks_of = self.first if step == 1 else lambda me: [me + 1 - 2 * lax.rem(me, 2)]
        return add_call(chunks_of, partials, moved[-1])

    def last(self, moved):
        return [(moved[1], 1), (moved[2], 0)]


def per_device(
    hidden_in, cotangent, down_weight, tile_ids, tile_live, values, moment_one, moment_two
):
    spans, cores = lax.axis_size("seq"), lax.axis_size("dp")
    slots, block = values.shape[2], values.shape[3]
    f_width, d_width = down_weight.shape
    d_blocks, f_blocks = d_width // block, f_width // block
    chunk = hidden_in.shape[0]
    sizes = (spans, slots, block)
    group = max(size for size in range(1, 5) if f_blocks % size == 0)
    width = group * block
    plan = Line() if spans == 4 else Ring(spans)
    ends = [sum(plan.parts[:part]) for part in range(len(plan.parts) + 1)]
    cuts = [(f_blocks // group) * end // ends[-1] for end in ends]
    ranges = list(zip(cuts[:-1], cuts[1:]))

    firsts = [take_from(cotangent, "tensor", t) for t in range(1, lax.axis_size("tensor"))]
    local = [take_from(cotangent, "dp", d) for d in range(1, cores)]

    meta = jnp.concatenate([tile_ids[0], tile_live[0]], axis=1)
    metas = exchange([meta] * spans)
    values_half, hidden_here = pl.pallas_call(
        early_kernel,
        out_shape=[
            jax.ShapeDtypeStruct((slots, block, block), jnp.bfloat16),
            jax.ShapeDtypeStruct(hidden_in.shape, hidden_in.dtype),
        ],
        in_specs=[hbm(), hbm()],
        out_specs=[vmem(), vmem()],
        scratch_shapes=[
            pltpu.VMEM((slots, block, block), jnp.float32),
            pltpu.SemaphoreType.DMA((2,)),
        ],
        compiler_params=params(),
        cost_estimate=cost(hidden_in.size),
        name="early",
    )(stay(values[0, 0]), stay(hidden_in))
    local_rows, first_weight = pl.pallas_call(
        lay_kernel,
        out_shape=[
            jax.ShapeDtypeStruct((cores * chunk, d_width), cotangent.dtype),
            jax.ShapeDtypeStruct((ranges[0][1] * width, d_width), down_weight.dtype),
        ],
        in_specs=[hbm(), hbm()] + [vmem()] * (cores - 1),
        out_specs=[vmem(), vmem()],
        scratch_shapes=[pltpu.SemaphoreType.DMA((2,))],
        compiler_params=params(),
        cost_estimate=cost(cores * chunk * d_width),
        name="lay",
    )(stay(cotangent), stay(down_weight), *local)
    hidden_here, local_rows, first_weight = lax.optimization_barrier(
        (hidden_here, local_rows, first_weight)
    )
    table, *picked = pl.pallas_call(
        functools.partial(pick_kernel, *sizes, d_blocks),
        out_shape=[jax.ShapeDtypeStruct((spans, 3 * slots), jnp.int32)]
        + [jax.ShapeDtypeStruct((block, block), jnp.bfloat16)] * spans
        + [jax.ShapeDtypeStruct((slots, chunk, block), jnp.bfloat16)] * spans,
        in_specs=[smem()] * spans + [vmem(), vmem()],
        out_specs=[smem()] + [vmem()] * (2 * spans),
        compiler_params=params(),
        cost_estimate=cost(hidden_in.size),
        name="pick",
    )(*metas, values_half, hidden_here)
    stored = exchange(picked[:spans])
    hidden_cols = exchange(picked[spans:])

    firsts, stored = lax.optimization_barrier((firsts, stored))
    pieces = [local_rows]
    for first in firsts:
        pieces += [first] + [take_from(first, "dp", d) for d in range(1, cores)]

    partials, moved = [], []
    for part, (low, high) in enumerate(ranges):
        if part == 0:
            partial, first, rows, held = matmul_call(
                sizes, low, high, width, plan.first, table, first_weight, pieces, stored
            )
        else:
            if part == 2:
                send = grad_call(sizes, table, rows, hidden_cols)
                moved[0][-1], send = lax.optimization_barrier((moved[0][-1], send))
            if part > 1:
                sums = plan.add(1, partials[part - 2], moved[part - 2])
                rows, sums = lax.optimization_barrier((rows, sums))
                moved[part - 2].append(plan.move(1, sums))
            partial, first = matmul_call(
                sizes, low, high, width, plan.first, table, down_weight, [rows, held]
            )
        partials.append(partial)
        moved.append([plan.move(0, first)])

    grads = exchange(send)
    turn = partials[-1]
    todo = [(step, part) for step in range(1, plan.steps) for part in range(len(ranges))]
    todo = [(step, part) for step, part in todo if len(moved[part]) <= step]
    for step, part in sorted(todo, key=lambda item: (item[1] + LAG * item[0], -item[0])):
        if (step, part) == (plan.steps - 1, len(ranges) - 1):
            turn = (turn, grads)
        moved[part][-1], turn = lax.optimization_barrier((moved[part][-1], turn))
        turn = plan.add(step, partials[part], moved[part])
        moved[part].append(plan.move(step, turn))
    new = adam_call(sizes, table, grads, values, moment_one, moment_two)

    hidden_grad = None
    shape = jax.ShapeDtypeStruct((chunk, f_width), jnp.bfloat16)
    for part, (low, _) in enumerate(ranges):
        if part == len(ranges) - 1:
            moved[part][-1], new = lax.optimization_barrier((moved[part][-1], new))
        hidden_grad = last_call(
            low * width, partials[part], plan.last(moved[part]), hidden_grad, shape
        )
    return (hidden_grad,) + tuple(array[None, None] for array in new)


def solution(mesh):
    shards = P(("groups", "seq"), ("tensor", "dp"))
    tiles = P(("groups", "seq"), ("tensor", "dp"), None, None, None)
    lists = P(("groups", "seq"), ("tensor", "dp"), None)
    return jax.shard_map(
        per_device,
        mesh=mesh,
        in_specs=(
            shards,
            P(("groups", "tensor", "dp"), "seq"),
            P(("tensor", "dp"), "seq"),
            lists,
            lists,
            tiles,
            tiles,
            tiles,
        ),
        out_specs=(shards, tiles, tiles, tiles),
        check_vma=False,
    )
```

```python
import functools

import jax
import jax.numpy as jnp
from jax import lax
from jax.experimental import pallas as pl
from jax.experimental.pallas import tpu as pltpu
from jax.sharding import PartitionSpec as P

STEP = 100
BETA_ONE = 0.9
BETA_TWO = 0.999
RATE = 0.01
EPSILON = 1e-08
VMEM_LIMIT = 24 * 1024 * 1024
MATMUL = 4096
PARTS = (3, 2, 2)
RIDE = 2
NT = (((1,), (1,)), ((), ()))
TN = (((0,), (0,)), ((), ()))


def vmem():
    return pl.BlockSpec(memory_space=pltpu.VMEM)


def smem():
    return pl.BlockSpec(memory_space=pltpu.SMEM)


def hbm():
    return pl.BlockSpec(memory_space=pltpu.HBM)


def stay(array):
    return pltpu.with_memory_space_constraint(array, pltpu.HBM)


def cost(count):
    return pl.CostEstimate(flops=count, bytes_accessed=2 * count, transcendentals=0)


def params():
    return pltpu.CompilerParams(vmem_limit_bytes=VMEM_LIMIT)


def wrap(index, size):
    return lax.rem(index + size, size)


def live_count(table, row, slots):
    count = table[row, 2 * slots]
    for slot in range(1, slots):
        count = count + table[row, 2 * slots + slot]
    return count


def rank_before(table, row, spans, slots):
    me = lax.axis_index("seq")
    before = jnp.int32(0)
    for other in range(spans):
        ahead = wrap(me - other, spans) < wrap(me - row, spans)
        before = before + jnp.where(ahead, live_count(table, other, slots), 0)
    return before


def early_kernel(values, hidden, values_half, hidden_here, stored, sems):
    value_copy = pltpu.make_async_copy(values, stored, sems.at[0])
    hidden_copy = pltpu.make_async_copy(hidden, hidden_here, sems.at[1])
    value_copy.start()
    hidden_copy.start()
    value_copy.wait()
    values_half[...] = stored[...].astype(values_half.dtype)
    hidden_copy.wait()


def pick_kernel(spans, slots, block, d_blocks, *refs):
    metas, (values, hidden, table), outs = refs[:spans], refs[spans : spans + 3], refs[spans + 3 :]
    me = lax.axis_index("seq")
    for s in range(spans):
        for j in range(slots):
            table[s, j] = lax.div(metas[s][0, j], d_blocks)
            table[s, slots + j] = lax.rem(metas[s][0, j], d_blocks)
            table[s, 2 * slots + j] = metas[s][0, slots + j]
    for s in range(spans):
        row = (spans - s) % spans
        before = rank_before(table, row, spans, slots)
        slot = wrap(me - lax.rem(before, spans), spans)
        tile = values[jnp.minimum(lax.div(before + slot, spans), slots - 1)]
        live = slot < live_count(table, row, slots)
        outs[s][...] = jnp.where(live, tile.astype(jnp.float32), 0.0).astype(tile.dtype)
        for j in range(slots):
            start = pl.multiple_of(table[row, j] * block, block)
            outs[spans + s][j] = hidden[:, pl.ds(start, block)]


def lay_kernel(own, weight, *refs):
    others, (rows, first_weight, sems) = refs[:-3], refs[-3:]
    chunk = own.shape[0]
    weight_copy = pltpu.make_async_copy(
        weight.at[pl.ds(0, first_weight.shape[0])], first_weight, sems.at[0]
    )
    weight_copy.start()
    own_copy = pltpu.make_async_copy(own, rows.at[pl.ds(0, chunk)], sems.at[1])
    own_copy.start()
    for p, other in enumerate(others):
        rows[(p + 1) * chunk : (p + 2) * chunk] = other[...]
    own_copy.wait()
    weight_copy.wait()


def chunk_at(place):
    tensors, cores = lax.axis_size("tensor"), lax.axis_size("dp")
    t_place = lax.rem(lax.axis_index("tensor") + place // cores, tensors)
    d_place = lax.rem(lax.axis_index("dp") + place % cores, cores)
    return t_place * cores + d_place


def matmul_kernel(sizes, low, width, ends, stores, table, weight, *refs):
    spans, slots, block = sizes
    step = pl.program_id(0)
    me = lax.axis_index("seq")
    parts, total = len(ends), refs[-1]
    if stores:
        given, stored = refs[: -stores - 2 * parts - 3], refs[-stores - 2 * parts - 3 : -2 * parts - 3]
        outs, (rows, held) = refs[-2 * parts - 3 : -3], refs[-3:-1]

        @pl.when(step == 0)
        def _():
            at = 0
            for piece in given:
                rows[at : at + piece.shape[0]] = piece[...]
                at += piece.shape[0]
            before = rank_before(table, 0, spans, slots)
            for j in range(slots):
                for s in range(spans):

                    @pl.when(lax.rem(before + j, spans) == wrap(me - s, spans))
                    def _():
                        held[j] = stored[s][...]

    else:
        (rows, held), outs = refs[:2], refs[2:-1]
    chunk = rows.shape[0] // spans
    here = pl.ds(pl.multiple_of(step * width, width), width)
    weights = weight[here] if weight.shape[0] > width else weight[...]
    total[...] = lax.dot_general(rows[...], weights, NT, preferred_element_type=jnp.float32)
    count = live_count(table, 0, slots)
    for j in range(slots):
        f_start = table[0, j] * block - (low + step) * width

        @pl.when((j < count) & (f_start >= 0) & (f_start < width))
        def _():
            d_start = pl.multiple_of(table[0, slots + j] * block, block)
            place = pl.ds(pl.multiple_of(f_start, block), block)
            total[:, place] += lax.dot_general(
                rows[:, pl.ds(d_start, block)], held[j], NT, preferred_element_type=jnp.float32
            )

    for part, (begin, end) in enumerate(zip((0, *ends), ends)):

        @pl.when((step >= begin) & (step < end))
        def _():
            out, first = outs[2 * part : 2 * part + 2]
            here = pl.ds(pl.multiple_of((step - begin) * width, width), width)
            for p in range(spans):
                result = total[p * chunk : (p + 1) * chunk].astype(out.dtype)
                out[chunk_at(p), :, here] = result

                @pl.when(chunk_at(p) == wrap(me - 1, spans))
                def _():
                    first[:, here] = result


def matmul_call(sizes, low, ends, width, table, weight, given, stored=()):
    spans, slots, block = sizes
    tokens = sum(piece.shape[0] for piece in given) if stored else given[0].shape[0]
    d_width, chunk, half = weight.shape[1], tokens // spans, jnp.bfloat16
    shapes = []
    for begin, end in zip((0, *ends), ends):
        columns = (end - begin) * width
        shapes.append(jax.ShapeDtypeStruct((spans, chunk, columns), half))
        shapes.append(jax.ShapeDtypeStruct((chunk, columns), half))
    if stored:
        shapes.append(jax.ShapeDtypeStruct((tokens, d_width), half))
        shapes.append(jax.ShapeDtypeStruct((slots, block, block), half))
    if weight.shape[0] == ends[-1] * width:
        weight_spec = vmem()
    else:
        weight, weight_spec = stay(weight), pl.BlockSpec((width, d_width), lambda i: (i + low, 0))
    inputs = [*given, *stored]
    return pl.pallas_call(
        functools.partial(matmul_kernel, sizes, low, width, ends, len(stored)),
        grid=(ends[-1],),
        out_shape=shapes,
        in_specs=[smem(), weight_spec] + [vmem()] * len(inputs),
        out_specs=[vmem()] * len(shapes),
        scratch_shapes=[pltpu.VMEM((tokens, width), jnp.float32)],
        compiler_params=params(),
        cost_estimate=cost(MATMUL * tokens * ends[-1] * width),
        name="partial",
    )(table, weight, *inputs)


def attach_kernel(first, *refs):
    riders, out = refs[:-1], refs[-1]
    at = first.shape[1]
    out[:, :at] = first[...]
    for rider in riders:
        out[:, at : at + rider.shape[1]] = rider[...]
        at += rider.shape[1]


def attach_call(first, riders):
    chunk, columns = first.shape
    columns += sum(rider.shape[1] for rider in riders)
    return pl.pallas_call(
        attach_kernel,
        out_shape=jax.ShapeDtypeStruct((chunk, columns), first.dtype),
        in_specs=[vmem()] * (1 + len(riders)),
        out_specs=vmem(),
        compiler_params=params(),
        cost_estimate=cost(first.size),
        name="attach",
    )(first, *riders)


def add_kernel(t, riders, partials, arrived, out, *mine):
    spans, _, columns = partials.shape
    chunk = wrap(lax.axis_index("seq") - t, spans)
    result = partials[chunk].astype(jnp.float32) + arrived[:, :columns].astype(jnp.float32)
    out[:, :columns] = result.astype(out.dtype)
    if riders:
        block = mine[0].shape[1]
        mine[0][...] = arrived[:, columns : columns + block]
        out[:, columns:] = arrived[:, columns + block :]


def add_call(t, partials, arrived, block):
    chunk, columns = partials.shape[1:]
    riders = (arrived.shape[1] - columns) // block
    shapes = [jax.ShapeDtypeStruct((chunk, arrived.shape[1] - min(riders, 1) * block), arrived.dtype)]
    if riders:
        shapes.append(jax.ShapeDtypeStruct((chunk, block), arrived.dtype))
    return pl.pallas_call(
        functools.partial(add_kernel, t, riders),
        out_shape=shapes,
        in_specs=[vmem(), vmem()],
        out_specs=[vmem()] * len(shapes),
        compiler_params=params(),
        cost_estimate=cost(arrived.size),
        name="add",
    )(partials, arrived)


def last_kernel(low, partials, arrived, *refs):
    out, total, sem = refs[-3:]
    columns = total.shape[1]
    result = partials[lax.axis_index("seq")].astype(jnp.float32)
    result = result + arrived[:, :columns].astype(jnp.float32)
    total[...] = result.astype(out.dtype)
    copy = pltpu.make_async_copy(total, out.at[:, pl.ds(low, columns)], sem)
    copy.start()
    copy.wait()


def last_call(low, partials, arrived, out, shape):
    _, chunk, columns = partials.shape
    given = [] if out is None else [out]
    return pl.pallas_call(
        functools.partial(last_kernel, low),
        out_shape=shape,
        in_specs=[vmem()] * 2 + [hbm()] * len(given),
        out_specs=hbm(),
        scratch_shapes=[pltpu.VMEM((chunk, columns), shape.dtype), pltpu.SemaphoreType.DMA],
        input_output_aliases={2: 0} if given else {},
        compiler_params=params(),
        cost_estimate=cost(partials.size),
        name="last_sum",
    )(partials, arrived, *given)


def grad_kernel(spans, slots, block, table, rows, *refs):
    hidden, outs, (cols,) = refs[:spans], refs[spans : 2 * spans], refs[2 * spans :]
    me = lax.axis_index("seq")
    count, before = live_count(table, 0, slots), rank_before(table, 0, spans, slots)
    chunk = rows.shape[0] // spans
    for s in range(spans):
        cols[s] = hidden[s][...]
    for s in range(spans):
        slot = wrap(lax.rem(me + s, spans) - lax.rem(before, spans), spans)
        outs[s][...] = jnp.zeros_like(outs[s])

        @pl.when(slot < count)
        def _():
            d_start = pl.multiple_of(table[0, slots + slot] * block, block)
            total = jnp.zeros((block, block), jnp.float32)
            for p in range(spans):
                total = total + lax.dot_general(
                    cols[wrap(me - chunk_at(p), spans), slot],
                    rows[p * chunk : (p + 1) * chunk, pl.ds(d_start, block)],
                    TN,
                    preferred_element_type=jnp.float32,
                )
            outs[s][...] = total.astype(outs[s].dtype)


def grad_call(sizes, table, rows, hidden_cols):
    spans = sizes[0]
    slots, chunk, block = hidden_cols[0].shape
    return pl.pallas_call(
        functools.partial(grad_kernel, *sizes),
        out_shape=[jax.ShapeDtypeStruct((block, block), jnp.bfloat16)] * spans,
        in_specs=[smem()] + [vmem()] * (spans + 1),
        out_specs=[vmem()] * spans,
        scratch_shapes=[pltpu.VMEM((spans, slots, chunk, block), jnp.bfloat16)],
        compiler_params=params(),
        cost_estimate=cost(rows.size),
        name="tile_grad",
    )(table, rows, *hidden_cols)


def adam_kernel(spans, slots, columns, table, *refs):
    arrived, refs = refs[:spans], refs[spans:]
    values, one, two, values_new, one_new, two_new, grads = refs
    me = lax.axis_index("seq")
    for s in range(spans - 1):
        grads[s] = arrived[s][...]
    grads[spans - 1] = arrived[-1][:, columns:]
    befores = [rank_before(table, s, spans, slots) for s in range(spans)]
    counts = [live_count(table, s, slots) for s in range(spans)]
    for owned in range(slots):
        rank = owned * spans + me
        source, live = jnp.int32(0), jnp.int32(0)
        for s in range(spans):
            holds = (befores[s] <= rank) & (rank < befores[s] + counts[s])
            source, live = jnp.where(holds, s, source), jnp.where(holds, 1, live)
        grad = grads[source].astype(jnp.float32)
        stored, old_one, old_two = values[owned], one[owned], two[owned]
        new_one = BETA_ONE * old_one + (1.0 - BETA_ONE) * grad
        new_two = BETA_TWO * old_two + (1.0 - BETA_TWO) * grad * grad
        stepped = (
            new_one
            / (1.0 - BETA_ONE**STEP)
            / (jnp.sqrt(new_two / (1.0 - BETA_TWO**STEP)) + EPSILON)
        )
        values_new[owned] = jnp.where(live > 0, stored - RATE * stepped, stored)
        one_new[owned] = jnp.where(live > 0, new_one, old_one)
        two_new[owned] = jnp.where(live > 0, new_two, old_two)


def adam_call(sizes, columns, table, grads, *states):
    spans, slots, block = sizes
    tile = jax.ShapeDtypeStruct((slots, block, block), jnp.float32)
    return pl.pallas_call(
        functools.partial(adam_kernel, spans, slots, columns),
        out_shape=(tile, tile, tile),
        in_specs=[smem()] + [vmem()] * (spans + 3),
        out_specs=(vmem(), vmem(), vmem()),
        scratch_shapes=[pltpu.VMEM((spans, block, block), jnp.bfloat16)],
        compiler_params=params(),
        cost_estimate=cost(slots * block * block),
        name="adam",
    )(table, *grads, *[state[0, 0] for state in states])


def take_from(array, axis, places):
    size = lax.axis_size(axis)
    return lax.ppermute(array, axis, [((i + places) % size, i) for i in range(size)])


def exchange(pieces):
    return [pieces[0]] + [take_from(pieces[s], "seq", -s) for s in range(1, len(pieces))]


def per_device(
    hidden_in, cotangent, down_weight, tile_ids, tile_live, values, moment_one, moment_two
):
    spans, cores = lax.axis_size("seq"), lax.axis_size("dp")
    slots, block = values.shape[2], values.shape[3]
    f_width, d_width = down_weight.shape
    d_blocks, f_blocks = d_width // block, f_width // block
    chunk = hidden_in.shape[0]
    sizes = (spans, slots, block)
    group = max(size for size in range(1, 5) if f_blocks % size == 0)
    width = group * block
    ends = [sum(PARTS[:part]) for part in range(len(PARTS) + 1)]
    cuts = [(f_blocks // group) * end // ends[-1] for end in ends]
    ranges = list(zip(cuts[:-1], cuts[1:]))

    firsts = [take_from(cotangent, "tensor", t) for t in range(1, lax.axis_size("tensor"))]
    local = [take_from(cotangent, "dp", d) for d in range(1, cores)]

    meta = jnp.concatenate([tile_ids[0], tile_live[0]], axis=1)
    metas = exchange([meta] * spans)
    values_half, hidden_here = pl.pallas_call(
        early_kernel,
        out_shape=[
            jax.ShapeDtypeStruct((slots, block, block), jnp.bfloat16),
            jax.ShapeDtypeStruct(hidden_in.shape, hidden_in.dtype),
        ],
        in_specs=[hbm(), hbm()],
        out_specs=[vmem(), vmem()],
        scratch_shapes=[
            pltpu.VMEM((slots, block, block), jnp.float32),
            pltpu.SemaphoreType.DMA((2,)),
        ],
        compiler_params=params(),
        cost_estimate=cost(hidden_in.size),
        name="early",
    )(stay(values[0, 0]), stay(hidden_in))
    local_rows, first_weight = pl.pallas_call(
        lay_kernel,
        out_shape=[
            jax.ShapeDtypeStruct((cores * chunk, d_width), cotangent.dtype),
            jax.ShapeDtypeStruct((ranges[0][1] * width, d_width), down_weight.dtype),
        ],
        in_specs=[hbm(), hbm()] + [vmem()] * (cores - 1),
        out_specs=[vmem(), vmem()],
        scratch_shapes=[pltpu.SemaphoreType.DMA((2,))],
        compiler_params=params(),
        cost_estimate=cost(cores * chunk * d_width),
        name="lay",
    )(stay(cotangent), stay(down_weight), *local)
    hidden_here, local_rows, first_weight = lax.optimization_barrier(
        (hidden_here, local_rows, first_weight)
    )
    table, *picked = pl.pallas_call(
        functools.partial(pick_kernel, *sizes, d_blocks),
        out_shape=[jax.ShapeDtypeStruct((spans, 3 * slots), jnp.int32)]
        + [jax.ShapeDtypeStruct((block, block), jnp.bfloat16)] * spans
        + [jax.ShapeDtypeStruct((slots, chunk, block), jnp.bfloat16)] * spans,
        in_specs=[smem()] * spans + [vmem(), vmem()],
        out_specs=[smem()] + [vmem()] * (2 * spans),
        compiler_params=params(),
        cost_estimate=cost(hidden_in.size),
        name="pick",
    )(*metas, values_half, hidden_here)
    stored = exchange(picked[:spans])
    hidden_cols = exchange(picked[spans:])

    firsts, stored = lax.optimization_barrier((firsts, stored))
    pieces = [local_rows]
    for first in firsts:
        pieces += [first] + [take_from(first, "dp", d) for d in range(1, cores)]

    pieces = list(pieces)
    partial, first, rows, held = matmul_call(
        sizes, 0, (cuts[1],), width, table, first_weight, pieces, stored
    )
    later = tuple(cut - cuts[1] for cut in cuts[2:])
    more = matmul_call(sizes, cuts[1], later, width, table, down_weight, [rows, held])
    partials, begins = [partial, *more[::2]], [first, *more[1::2]]
    grads = grad_call(sizes, table, rows, hidden_cols)
    begins[RIDE] = attach_call(begins[RIDE], grads[1:])
    moving = [take_from(begin, "seq", -1) for begin in begins]

    tiles = [grads[0]]
    for t in range(2, spans):
        for part in range(len(ranges)):
            moving[part], *mine = add_call(t, partials[part], moving[part], block)
            tiles += mine
            moving[part] = take_from(moving[part], "seq", -1)
    tiles.append(moving[RIDE])
    columns = partials[RIDE].shape[2]
    new = adam_call(sizes, columns, table, tiles, values, moment_one, moment_two)

    hidden_grad = None
    shape = jax.ShapeDtypeStruct((chunk, f_width), jnp.bfloat16)
    for part, (low, _) in enumerate(ranges):
        if part == len(ranges) - 1:
            moving[part], new = lax.optimization_barrier((moving[part], new))
        hidden_grad = last_call(low * width, partials[part], moving[part], hidden_grad, shape)
    return (hidden_grad,) + tuple(array[None, None] for array in new)


def solution(mesh):
    shards = P(("groups", "seq"), ("tensor", "dp"))
    tiles = P(("groups", "seq"), ("tensor", "dp"), None, None, None)
    lists = P(("groups", "seq"), ("tensor", "dp"), None)
    return jax.shard_map(
        per_device,
        mesh=mesh,
        in_specs=(
            shards,
            P(("groups", "tensor", "dp"), "seq"),
            P(("tensor", "dp"), "seq"),
            lists,
            lists,
            tiles,
            tiles,
            tiles,
        ),
        out_specs=(shards, tiles, tiles, tiles),
        check_vma=False,
    )
```

```python
import functools

import jax
import jax.numpy as jnp
from jax import lax
from jax.experimental import pallas as pl
from jax.experimental.pallas import tpu as pltpu
from jax.sharding import PartitionSpec as P

STEP = 100
BETA_ONE = 0.9
BETA_TWO = 0.999
RATE = 0.01
EPSILON = 1e-08
VMEM_LIMIT = 24 * 1024 * 1024
MATMUL = 4096
PARTS = (3, 2, 2)
RIDE = 2
NT = (((1,), (1,)), ((), ()))
TN = (((0,), (0,)), ((), ()))


def vmem():
    return pl.BlockSpec(memory_space=pltpu.VMEM)


def smem():
    return pl.BlockSpec(memory_space=pltpu.SMEM)


def hbm():
    return pl.BlockSpec(memory_space=pltpu.HBM)


def stay(array):
    return pltpu.with_memory_space_constraint(array, pltpu.HBM)


def cost(count):
    return pl.CostEstimate(flops=count, bytes_accessed=2 * count, transcendentals=0)


def params():
    return pltpu.CompilerParams(vmem_limit_bytes=VMEM_LIMIT)


def wrap(index, size):
    return lax.rem(index + size, size)


def live_count(table, row, slots):
    count = table[row, 2 * slots]
    for slot in range(1, slots):
        count = count + table[row, 2 * slots + slot]
    return count


def rank_before(table, row, spans, slots):
    me = lax.axis_index("seq")
    before = jnp.int32(0)
    for other in range(spans):
        ahead = wrap(me - other, spans) < wrap(me - row, spans)
        before = before + jnp.where(ahead, live_count(table, other, slots), 0)
    return before


def early_kernel(values, hidden, values_half, hidden_here, stored, sems):
    value_copy = pltpu.make_async_copy(values, stored, sems.at[0])
    hidden_copy = pltpu.make_async_copy(hidden, hidden_here, sems.at[1])
    value_copy.start()
    hidden_copy.start()
    value_copy.wait()
    values_half[...] = stored[...].astype(values_half.dtype)
    hidden_copy.wait()


def pick_kernel(spans, slots, block, d_blocks, *refs):
    metas, (values, hidden, table), outs = refs[:spans], refs[spans : spans + 3], refs[spans + 3 :]
    me = lax.axis_index("seq")
    for s in range(spans):
        for j in range(slots):
            table[s, j] = lax.div(metas[s][0, j], d_blocks)
            table[s, slots + j] = lax.rem(metas[s][0, j], d_blocks)
            table[s, 2 * slots + j] = metas[s][0, slots + j]
    for s in range(spans):
        row = (spans - s) % spans
        before = rank_before(table, row, spans, slots)
        slot = wrap(me - lax.rem(before, spans), spans)
        tile = values[jnp.minimum(lax.div(before + slot, spans), slots - 1)]
        live = slot < live_count(table, row, slots)
        outs[s][slots] = jnp.where(live, tile.astype(jnp.float32), 0.0).astype(tile.dtype)
        for j in range(slots):
            start = pl.multiple_of(table[row, j] * block, block)
            outs[s][j] = hidden[:, pl.ds(start, block)]


def lay_kernel(own, weight, *refs):
    others, (rows, first_weight, sems) = refs[:-3], refs[-3:]
    chunk = own.shape[0]
    weight_copy = pltpu.make_async_copy(
        weight.at[pl.ds(0, first_weight.shape[0])], first_weight, sems.at[0]
    )
    weight_copy.start()
    own_copy = pltpu.make_async_copy(own, rows.at[pl.ds(0, chunk)], sems.at[1])
    own_copy.start()
    for p, other in enumerate(others):
        rows[(p + 1) * chunk : (p + 2) * chunk] = other[...]
    own_copy.wait()
    weight_copy.wait()


def chunk_at(place):
    tensors, cores = lax.axis_size("tensor"), lax.axis_size("dp")
    t_place = lax.rem(lax.axis_index("tensor") + place // cores, tensors)
    d_place = lax.rem(lax.axis_index("dp") + place % cores, cores)
    return t_place * cores + d_place


def early_matmul_kernel(width, weight, *refs):
    pieces, (out, rows) = refs[:-2], refs[-2:]
    step = pl.program_id(0)

    @pl.when(step == 0)
    def _():
        at = 0
        for piece in pieces:
            rows[at : at + piece.shape[0]] = piece[...]
            at += piece.shape[0]

    here = pl.ds(pl.multiple_of(step * width, width), width)
    out[:, here] = lax.dot_general(
        rows[...], weight[here], NT, preferred_element_type=jnp.float32
    )


def early_matmul_call(width, weight, pieces):
    tokens, (columns, d_width) = sum(piece.shape[0] for piece in pieces), weight.shape
    return pl.pallas_call(
        functools.partial(early_matmul_kernel, width),
        grid=(columns // width,),
        out_shape=[
            jax.ShapeDtypeStruct((tokens, columns), jnp.float32),
            jax.ShapeDtypeStruct((tokens, d_width), weight.dtype),
        ],
        in_specs=[vmem()] * (1 + len(pieces)),
        out_specs=[vmem()] * 2,
        compiler_params=params(),
        cost_estimate=cost(MATMUL * tokens * columns),
        name="partial",
    )(weight, *pieces)


def add_delta(table, rows, held, total, low):
    slots, block, _ = held.shape
    count = live_count(table, 0, slots)
    for j in range(slots):
        f_start = table[0, j] * block - low

        @pl.when((j < count) & (f_start >= 0) & (f_start < total.shape[1]))
        def _():
            d_start = pl.multiple_of(table[0, slots + j] * block, block)
            place = pl.ds(pl.multiple_of(f_start, block), block)
            total[:, place] += lax.dot_general(
                rows[:, pl.ds(d_start, block)], held[j], NT, preferred_element_type=jnp.float32
            )


def put_chunks(total, out, first, here):
    spans, chunk = out.shape[:2]
    me = lax.axis_index("seq")
    for p in range(spans):
        result = total[p * chunk : (p + 1) * chunk].astype(out.dtype)
        out[chunk_at(p), :, here] = result

        @pl.when(chunk_at(p) == wrap(me - 1, spans))
        def _():
            first[:, here] = result


def delta_kernel(spans, slots, block, table, early, rows, *refs):
    stored, (out, first, held, total) = refs[:spans], refs[spans:]
    me = lax.axis_index("seq")
    before = rank_before(table, 0, spans, slots)
    for j in range(slots):
        for s in range(spans):

            @pl.when(lax.rem(before + j, spans) == wrap(me - s, spans))
            def _():
                held[j] = stored[s][slots]

    total[...] = early[...]
    add_delta(table, rows, held, total, 0)
    put_chunks(total, out, first, pl.ds(0, total.shape[1]))


def delta_call(sizes, table, early, rows, stored):
    spans, slots, block = sizes
    tokens, columns = early.shape
    return pl.pallas_call(
        functools.partial(delta_kernel, *sizes),
        out_shape=[
            jax.ShapeDtypeStruct((spans, tokens // spans, columns), rows.dtype),
            jax.ShapeDtypeStruct((tokens // spans, columns), rows.dtype),
            jax.ShapeDtypeStruct((slots, block, block), rows.dtype),
        ],
        in_specs=[smem()] + [vmem()] * (2 + spans),
        out_specs=[vmem()] * 3,
        scratch_shapes=[pltpu.VMEM((tokens, columns), jnp.float32)],
        compiler_params=params(),
        cost_estimate=cost(early.size),
        name="delta",
    )(table, early, rows, *stored)


def matmul_kernel(low, ends, table, weight, rows, held, *refs):
    outs, total = refs[:-1], refs[-1]
    step, width = pl.program_id(0), weight.shape[0]
    total[...] = lax.dot_general(rows[...], weight[...], NT, preferred_element_type=jnp.float32)
    add_delta(table, rows, held, total, (low + step) * width)
    for part, (begin, end) in enumerate(zip((0, *ends), ends)):

        @pl.when((step >= begin) & (step < end))
        def _():
            here = pl.ds(pl.multiple_of((step - begin) * width, width), width)
            put_chunks(total, *outs[2 * part : 2 * part + 2], here)


def matmul_call(spans, low, ends, width, table, weight, rows, held):
    tokens, d_width = rows.shape
    shapes = []
    for begin, end in zip((0, *ends), ends):
        columns = (end - begin) * width
        shapes.append(jax.ShapeDtypeStruct((spans, tokens // spans, columns), rows.dtype))
        shapes.append(jax.ShapeDtypeStruct((tokens // spans, columns), rows.dtype))
    return pl.pallas_call(
        functools.partial(matmul_kernel, low, ends),
        grid=(ends[-1],),
        out_shape=shapes,
        in_specs=[
            smem(),
            pl.BlockSpec((width, d_width), lambda i: (i + low, 0)),
            vmem(),
            vmem(),
        ],
        out_specs=[vmem()] * len(shapes),
        scratch_shapes=[pltpu.VMEM((tokens, width), jnp.float32)],
        compiler_params=params(),
        cost_estimate=cost(MATMUL * tokens * ends[-1] * width),
        name="partial",
    )(table, stay(weight), rows, held)


def attach_kernel(first, *refs):
    riders, out = refs[:-1], refs[-1]
    at = first.shape[1]
    out[:, :at] = first[...]
    for rider in riders:
        out[:, at : at + rider.shape[1]] = rider[...]
        at += rider.shape[1]


def attach_call(first, riders):
    chunk, columns = first.shape
    columns += sum(rider.shape[1] for rider in riders)
    return pl.pallas_call(
        attach_kernel,
        out_shape=jax.ShapeDtypeStruct((chunk, columns), first.dtype),
        in_specs=[vmem()] * (1 + len(riders)),
        out_specs=vmem(),
        compiler_params=params(),
        cost_estimate=cost(first.size),
        name="attach",
    )(first, *riders)


def add_kernel(t, riders, partials, arrived, out, *mine):
    spans, _, columns = partials.shape
    chunk = wrap(lax.axis_index("seq") - t, spans)
    result = partials[chunk].astype(jnp.float32) + arrived[:, :columns].astype(jnp.float32)
    out[:, :columns] = result.astype(out.dtype)
    if riders:
        block = mine[0].shape[1]
        mine[0][...] = arrived[:, columns : columns + block]
        out[:, columns:] = arrived[:, columns + block :]


def add_call(t, partials, arrived, block):
    chunk, columns = partials.shape[1:]
    riders = (arrived.shape[1] - columns) // block
    shapes = [jax.ShapeDtypeStruct((chunk, arrived.shape[1] - min(riders, 1) * block), arrived.dtype)]
    if riders:
        shapes.append(jax.ShapeDtypeStruct((chunk, block), arrived.dtype))
    return pl.pallas_call(
        functools.partial(add_kernel, t, riders),
        out_shape=shapes,
        in_specs=[vmem(), vmem()],
        out_specs=[vmem()] * len(shapes),
        compiler_params=params(),
        cost_estimate=cost(arrived.size),
        name="add",
    )(partials, arrived)


def last_kernel(low, partials, arrived, *refs):
    out, total, sem = refs[-3:]
    columns = total.shape[1]
    result = partials[lax.axis_index("seq")].astype(jnp.float32)
    result = result + arrived[:, :columns].astype(jnp.float32)
    total[...] = result.astype(out.dtype)
    copy = pltpu.make_async_copy(total, out.at[:, pl.ds(low, columns)], sem)
    copy.start()
    copy.wait()


def last_call(low, partials, arrived, out, shape):
    _, chunk, columns = partials.shape
    given = [] if out is None else [out]
    return pl.pallas_call(
        functools.partial(last_kernel, low),
        out_shape=shape,
        in_specs=[vmem()] * 2 + [hbm()] * len(given),
        out_specs=hbm(),
        scratch_shapes=[pltpu.VMEM((chunk, columns), shape.dtype), pltpu.SemaphoreType.DMA],
        input_output_aliases={2: 0} if given else {},
        compiler_params=params(),
        cost_estimate=cost(partials.size),
        name="last_sum",
    )(partials, arrived, *given)


def grad_kernel(spans, slots, block, table, rows, *refs):
    hidden, outs, (cols,) = refs[:spans], refs[spans : 2 * spans], refs[2 * spans :]
    me = lax.axis_index("seq")
    count, before = live_count(table, 0, slots), rank_before(table, 0, spans, slots)
    chunk = rows.shape[0] // spans
    for s in range(spans):
        cols[s] = hidden[s][:slots]
    for s in range(spans):
        slot = wrap(lax.rem(me + s, spans) - lax.rem(before, spans), spans)
        outs[s][...] = jnp.zeros_like(outs[s])

        @pl.when(slot < count)
        def _():
            d_start = pl.multiple_of(table[0, slots + slot] * block, block)
            total = jnp.zeros((block, block), jnp.float32)
            for p in range(spans):
                total = total + lax.dot_general(
                    cols[wrap(me - chunk_at(p), spans), slot],
                    rows[p * chunk : (p + 1) * chunk, pl.ds(d_start, block)],
                    TN,
                    preferred_element_type=jnp.float32,
                )
            outs[s][...] = total.astype(outs[s].dtype)


def grad_call(sizes, table, rows, hidden_cols):
    spans = sizes[0]
    slots, chunk, block = hidden_cols[0].shape
    slots -= 1
    return pl.pallas_call(
        functools.partial(grad_kernel, *sizes),
        out_shape=[jax.ShapeDtypeStruct((block, block), jnp.bfloat16)] * spans,
        in_specs=[smem()] + [vmem()] * (spans + 1),
        out_specs=[vmem()] * spans,
        scratch_shapes=[pltpu.VMEM((spans, slots, chunk, block), jnp.bfloat16)],
        compiler_params=params(),
        cost_estimate=cost(rows.size),
        name="tile_grad",
    )(table, rows, *hidden_cols)


def adam_kernel(spans, slots, columns, table, *refs):
    arrived, refs = refs[:spans], refs[spans:]
    values, one, two, values_new, one_new, two_new, grads = refs
    me = lax.axis_index("seq")
    for s in range(spans - 1):
        grads[s] = arrived[s][...]
    grads[spans - 1] = arrived[-1][:, columns:]
    befores = [rank_before(table, s, spans, slots) for s in range(spans)]
    counts = [live_count(table, s, slots) for s in range(spans)]
    for owned in range(slots):
        rank = owned * spans + me
        source, live = jnp.int32(0), jnp.int32(0)
        for s in range(spans):
            holds = (befores[s] <= rank) & (rank < befores[s] + counts[s])
            source, live = jnp.where(holds, s, source), jnp.where(holds, 1, live)
        grad = grads[source].astype(jnp.float32)
        stored, old_one, old_two = values[owned], one[owned], two[owned]
        new_one = BETA_ONE * old_one + (1.0 - BETA_ONE) * grad
        new_two = BETA_TWO * old_two + (1.0 - BETA_TWO) * grad * grad
        stepped = (
            new_one
            / (1.0 - BETA_ONE**STEP)
            / (jnp.sqrt(new_two / (1.0 - BETA_TWO**STEP)) + EPSILON)
        )
        values_new[owned] = jnp.where(live > 0, stored - RATE * stepped, stored)
        one_new[owned] = jnp.where(live > 0, new_one, old_one)
        two_new[owned] = jnp.where(live > 0, new_two, old_two)


def adam_call(sizes, columns, table, grads, *states):
    spans, slots, block = sizes
    tile = jax.ShapeDtypeStruct((slots, block, block), jnp.float32)
    return pl.pallas_call(
        functools.partial(adam_kernel, spans, slots, columns),
        out_shape=(tile, tile, tile),
        in_specs=[smem()] + [vmem()] * (spans + 3),
        out_specs=(vmem(), vmem(), vmem()),
        scratch_shapes=[pltpu.VMEM((spans, block, block), jnp.bfloat16)],
        compiler_params=params(),
        cost_estimate=cost(slots * block * block),
        name="adam",
    )(table, *grads, *[state[0, 0] for state in states])


def take_from(array, axis, places):
    size = lax.axis_size(axis)
    return lax.ppermute(array, axis, [((i + places) % size, i) for i in range(size)])


def exchange(pieces):
    return [pieces[0]] + [take_from(pieces[s], "seq", -s) for s in range(1, len(pieces))]


def per_device(
    hidden_in, cotangent, down_weight, tile_ids, tile_live, values, moment_one, moment_two
):
    spans, cores = lax.axis_size("seq"), lax.axis_size("dp")
    slots, block = values.shape[2], values.shape[3]
    f_width, d_width = down_weight.shape
    d_blocks, f_blocks = d_width // block, f_width // block
    chunk = hidden_in.shape[0]
    sizes = (spans, slots, block)
    group = max(size for size in range(1, 5) if f_blocks % size == 0)
    width = group * block
    ends = [sum(PARTS[:part]) for part in range(len(PARTS) + 1)]
    cuts = [(f_blocks // group) * end // ends[-1] for end in ends]
    ranges = list(zip(cuts[:-1], cuts[1:]))

    firsts = [take_from(cotangent, "tensor", t) for t in range(1, lax.axis_size("tensor"))]
    local = [take_from(cotangent, "dp", d) for d in range(1, cores)]

    meta = jnp.concatenate([tile_ids[0], tile_live[0]], axis=1)
    metas = exchange([meta] * spans)
    values_half, hidden_here = pl.pallas_call(
        early_kernel,
        out_shape=[
            jax.ShapeDtypeStruct((slots, block, block), jnp.bfloat16),
            jax.ShapeDtypeStruct(hidden_in.shape, hidden_in.dtype),
        ],
        in_specs=[hbm(), hbm()],
        out_specs=[vmem(), vmem()],
        scratch_shapes=[
            pltpu.VMEM((slots, block, block), jnp.float32),
            pltpu.SemaphoreType.DMA((2,)),
        ],
        compiler_params=params(),
        cost_estimate=cost(hidden_in.size),
        name="early",
    )(stay(values[0, 0]), stay(hidden_in))
    local_rows, first_weight = pl.pallas_call(
        lay_kernel,
        out_shape=[
            jax.ShapeDtypeStruct((cores * chunk, d_width), cotangent.dtype),
            jax.ShapeDtypeStruct((ranges[0][1] * width, d_width), down_weight.dtype),
        ],
        in_specs=[hbm(), hbm()] + [vmem()] * (cores - 1),
        out_specs=[vmem(), vmem()],
        scratch_shapes=[pltpu.SemaphoreType.DMA((2,))],
        compiler_params=params(),
        cost_estimate=cost(cores * chunk * d_width),
        name="lay",
    )(stay(cotangent), stay(down_weight), *local)
    table, *picked = pl.pallas_call(
        functools.partial(pick_kernel, *sizes, d_blocks),
        out_shape=[jax.ShapeDtypeStruct((spans, 3 * slots), jnp.int32)]
        + [jax.ShapeDtypeStruct((slots + 1, chunk, block), jnp.bfloat16)] * spans,
        in_specs=[smem()] * spans + [vmem(), vmem()],
        out_specs=[smem()] + [vmem()] * spans,
        compiler_params=params(),
        cost_estimate=cost(hidden_in.size),
        name="pick",
    )(*metas, values_half, hidden_here)
    crossed = exchange(picked)

    firsts, crossed[1] = lax.optimization_barrier((firsts, crossed[1]))
    pieces = [local_rows]
    for first in firsts:
        pieces += [first] + [take_from(first, "dp", d) for d in range(1, cores)]

    early, rows = early_matmul_call(width, first_weight, pieces)
    partial, first, held = delta_call(sizes, table, early, rows, crossed)
    later = tuple(cut - cuts[1] for cut in cuts[2:])
    more = matmul_call(spans, cuts[1], later, width, table, down_weight, rows, held)
    partials, begins = [partial, *more[::2]], [first, *more[1::2]]
    grads = grad_call(sizes, table, rows, crossed)
    begins[RIDE] = attach_call(begins[RIDE], grads[1:])
    moving = [take_from(begin, "seq", -1) for begin in begins]

    tiles = [grads[0]]
    for t in range(2, spans):
        for part in range(len(ranges)):
            moving[part], *mine = add_call(t, partials[part], moving[part], block)
            tiles += mine
            moving[part] = take_from(moving[part], "seq", -1)
    tiles.append(moving[RIDE])
    columns = partials[RIDE].shape[2]
    new = adam_call(sizes, columns, table, tiles, values, moment_one, moment_two)

    hidden_grad = None
    shape = jax.ShapeDtypeStruct((chunk, f_width), jnp.bfloat16)
    for part, (low, _) in enumerate(ranges):
        if part == len(ranges) - 1:
            moving[part], new = lax.optimization_barrier((moving[part], new))
        hidden_grad = last_call(low * width, partials[part], moving[part], hidden_grad, shape)
    return (hidden_grad,) + tuple(array[None, None] for array in new)


def solution(mesh):
    shards = P(("groups", "seq"), ("tensor", "dp"))
    tiles = P(("groups", "seq"), ("tensor", "dp"), None, None, None)
    lists = P(("groups", "seq"), ("tensor", "dp"), None)
    return jax.shard_map(
        per_device,
        mesh=mesh,
        in_specs=(
            shards,
            P(("groups", "tensor", "dp"), "seq"),
            P(("tensor", "dp"), "seq"),
            lists,
            lists,
            tiles,
            tiles,
            tiles,
        ),
        out_specs=(shards, tiles, tiles, tiles),
        check_vma=False,
    )
```

```python
import functools

import jax
import jax.numpy as jnp
from jax import lax
from jax.experimental import pallas as pl
from jax.experimental.pallas import tpu as pltpu
from jax.sharding import PartitionSpec as P

STEP = 100
BETA_ONE = 0.9
BETA_TWO = 0.999
RATE = 0.01
EPSILON = 1e-08
VMEM_LIMIT = 24 * 1024 * 1024
MATMUL = 4096
EARLY = 1
PARTS = (2, 3, 2)
RIDE = 2
LAST = 0
NT = (((1,), (1,)), ((), ()))
TN = (((0,), (0,)), ((), ()))


def vmem():
    return pl.BlockSpec(memory_space=pltpu.VMEM)


def smem():
    return pl.BlockSpec(memory_space=pltpu.SMEM)


def hbm():
    return pl.BlockSpec(memory_space=pltpu.HBM)


def stay(array):
    return pltpu.with_memory_space_constraint(array, pltpu.HBM)


def cost(count):
    return pl.CostEstimate(flops=count, bytes_accessed=2 * count, transcendentals=0)


def params():
    return pltpu.CompilerParams(vmem_limit_bytes=VMEM_LIMIT)


def wrap(index, size):
    return lax.rem(index + size, size)


def live_count(table, row, slots):
    count = table[row, 2 * slots]
    for slot in range(1, slots):
        count = count + table[row, 2 * slots + slot]
    return count


def rank_before(table, row, spans, slots):
    me = lax.axis_index("seq")
    before = jnp.int32(0)
    for other in range(spans):
        ahead = wrap(me - other, spans) < wrap(me - row, spans)
        before = before + jnp.where(ahead, live_count(table, other, slots), 0)
    return before


def early_kernel(values, hidden, values_half, hidden_here, stored, sems):
    value_copy = pltpu.make_async_copy(values, stored, sems.at[0])
    hidden_copy = pltpu.make_async_copy(hidden, hidden_here, sems.at[1])
    value_copy.start()
    hidden_copy.start()
    value_copy.wait()
    values_half[...] = stored[...].astype(values_half.dtype)
    hidden_copy.wait()


def pick_kernel(spans, slots, block, d_blocks, *refs):
    metas, (values, hidden, table), outs = refs[:spans], refs[spans : spans + 3], refs[spans + 3 :]
    me = lax.axis_index("seq")
    for s in range(spans):
        for j in range(slots):
            table[s, j] = lax.div(metas[s][0, j], d_blocks)
            table[s, slots + j] = lax.rem(metas[s][0, j], d_blocks)
            table[s, 2 * slots + j] = metas[s][0, slots + j]
    for s in range(spans):
        row = (spans - s) % spans
        before = rank_before(table, row, spans, slots)
        slot = wrap(me - lax.rem(before, spans), spans)
        tile = values[jnp.minimum(lax.div(before + slot, spans), slots - 1)]
        live = slot < live_count(table, row, slots)
        outs[s][slots] = jnp.where(live, tile.astype(jnp.float32), 0.0).astype(tile.dtype)
        for j in range(slots):
            start = pl.multiple_of(table[row, j] * block, block)
            outs[s][j] = hidden[:, pl.ds(start, block)]


def lay_kernel(own, weight, *refs):
    others, (rows, first_weight, sems) = refs[:-3], refs[-3:]
    chunk = own.shape[0]
    weight_copy = pltpu.make_async_copy(
        weight.at[pl.ds(0, first_weight.shape[0])], first_weight, sems.at[0]
    )
    weight_copy.start()
    own_copy = pltpu.make_async_copy(own, rows.at[pl.ds(0, chunk)], sems.at[1])
    own_copy.start()
    for p, other in enumerate(others):
        rows[(p + 1) * chunk : (p + 2) * chunk] = other[...]
    own_copy.wait()
    weight_copy.wait()


def chunk_at(place):
    tensors, cores = lax.axis_size("tensor"), lax.axis_size("dp")
    t_place = lax.rem(lax.axis_index("tensor") + place // cores, tensors)
    d_place = lax.rem(lax.axis_index("dp") + place % cores, cores)
    return t_place * cores + d_place


def early_matmul_kernel(width, weight, *refs):
    pieces, (out, rows) = refs[:-2], refs[-2:]
    step = pl.program_id(0)

    @pl.when(step == 0)
    def _():
        at = 0
        for piece in pieces:
            rows[at : at + piece.shape[0]] = piece[...]
            at += piece.shape[0]

    here = pl.ds(pl.multiple_of(step * width, width), width)
    out[:, here] = lax.dot_general(
        rows[...], weight[here], NT, preferred_element_type=jnp.float32
    )


def early_matmul_call(width, weight, pieces):
    tokens, (columns, d_width) = sum(piece.shape[0] for piece in pieces), weight.shape
    return pl.pallas_call(
        functools.partial(early_matmul_kernel, width),
        grid=(columns // width,),
        out_shape=[
            jax.ShapeDtypeStruct((tokens, columns), jnp.float32),
            jax.ShapeDtypeStruct((tokens, d_width), weight.dtype),
        ],
        in_specs=[vmem()] * (1 + len(pieces)),
        out_specs=[vmem()] * 2,
        compiler_params=params(),
        cost_estimate=cost(EARLY * tokens * columns),
        name="partial",
    )(weight, *pieces)


def add_delta(table, rows, held, total, low):
    slots, block, _ = held.shape
    count = live_count(table, 0, slots)
    for j in range(slots):
        f_start = table[0, j] * block - low

        @pl.when((j < count) & (f_start >= 0) & (f_start < total.shape[1]))
        def _():
            d_start = pl.multiple_of(table[0, slots + j] * block, block)
            place = pl.ds(pl.multiple_of(f_start, block), block)
            total[:, place] += lax.dot_general(
                rows[:, pl.ds(d_start, block)], held[j], NT, preferred_element_type=jnp.float32
            )


def put_chunks(total, out, first, here):
    spans, chunk = out.shape[:2]
    me = lax.axis_index("seq")
    for p in range(spans):
        result = total[p * chunk : (p + 1) * chunk].astype(out.dtype)
        out[chunk_at(p), :, here] = result

        @pl.when(chunk_at(p) == wrap(me - 1, spans))
        def _():
            first[:, here] = result


def delta_kernel(spans, slots, block, table, early, rows, *refs):
    stored, (out, first, held, total) = refs[:spans], refs[spans:]
    me = lax.axis_index("seq")
    before = rank_before(table, 0, spans, slots)
    for j in range(slots):
        for s in range(spans):

            @pl.when(lax.rem(before + j, spans) == wrap(me - s, spans))
            def _():
                held[j] = stored[s][slots]

    total[...] = early[...]
    add_delta(table, rows, held, total, 0)
    put_chunks(total, out, first, pl.ds(0, total.shape[1]))


def delta_call(sizes, table, early, rows, stored):
    spans, slots, block = sizes
    tokens, columns = early.shape
    return pl.pallas_call(
        functools.partial(delta_kernel, *sizes),
        out_shape=[
            jax.ShapeDtypeStruct((spans, tokens // spans, columns), rows.dtype),
            jax.ShapeDtypeStruct((tokens // spans, columns), rows.dtype),
            jax.ShapeDtypeStruct((slots, block, block), rows.dtype),
        ],
        in_specs=[smem()] + [vmem()] * (2 + spans),
        out_specs=[vmem()] * 3,
        scratch_shapes=[pltpu.VMEM((tokens, columns), jnp.float32)],
        compiler_params=params(),
        cost_estimate=cost(early.size),
        name="delta",
    )(table, early, rows, *stored)


def matmul_kernel(low, ends, table, weight, rows, held, *refs):
    outs, total = refs[:-1], refs[-1]
    step, width = pl.program_id(0), weight.shape[0]
    total[...] = lax.dot_general(rows[...], weight[...], NT, preferred_element_type=jnp.float32)
    add_delta(table, rows, held, total, (low + step) * width)
    for part, (begin, end) in enumerate(zip((0, *ends), ends)):

        @pl.when((step >= begin) & (step < end))
        def _():
            here = pl.ds(pl.multiple_of((step - begin) * width, width), width)
            put_chunks(total, *outs[2 * part : 2 * part + 2], here)


def matmul_call(spans, low, ends, width, table, weight, rows, held):
    tokens, d_width = rows.shape
    shapes = []
    for begin, end in zip((0, *ends), ends):
        columns = (end - begin) * width
        shapes.append(jax.ShapeDtypeStruct((spans, tokens // spans, columns), rows.dtype))
        shapes.append(jax.ShapeDtypeStruct((tokens // spans, columns), rows.dtype))
    return pl.pallas_call(
        functools.partial(matmul_kernel, low, ends),
        grid=(ends[-1],),
        out_shape=shapes,
        in_specs=[
            smem(),
            pl.BlockSpec((width, d_width), lambda i: (i + low, 0)),
            vmem(),
            vmem(),
        ],
        out_specs=[vmem()] * len(shapes),
        scratch_shapes=[pltpu.VMEM((tokens, width), jnp.float32)],
        compiler_params=params(),
        cost_estimate=cost(MATMUL * tokens * ends[-1] * width),
        name="partial",
    )(table, stay(weight), rows, held)


def attach_kernel(first, *refs):
    riders, out = refs[:-1], refs[-1]
    at = first.shape[1]
    out[:, :at] = first[...]
    for rider in riders:
        out[:, at : at + rider.shape[1]] = rider[...]
        at += rider.shape[1]


def attach_call(first, riders):
    chunk, columns = first.shape
    columns += sum(rider.shape[1] for rider in riders)
    return pl.pallas_call(
        attach_kernel,
        out_shape=jax.ShapeDtypeStruct((chunk, columns), first.dtype),
        in_specs=[vmem()] * (1 + len(riders)),
        out_specs=vmem(),
        compiler_params=params(),
        cost_estimate=cost(first.size),
        name="attach",
    )(first, *riders)


def add_kernel(t, riders, partials, arrived, out, *mine):
    spans, _, columns = partials.shape
    chunk = wrap(lax.axis_index("seq") - t, spans)
    result = partials[chunk].astype(jnp.float32) + arrived[:, :columns].astype(jnp.float32)
    out[:, :columns] = result.astype(out.dtype)
    if riders:
        block = mine[0].shape[1]
        mine[0][...] = arrived[:, columns : columns + block]
        out[:, columns:] = arrived[:, columns + block :]


def add_call(t, partials, arrived, block):
    chunk, columns = partials.shape[1:]
    riders = (arrived.shape[1] - columns) // block
    shapes = [jax.ShapeDtypeStruct((chunk, arrived.shape[1] - min(riders, 1) * block), arrived.dtype)]
    if riders:
        shapes.append(jax.ShapeDtypeStruct((chunk, block), arrived.dtype))
    return pl.pallas_call(
        functools.partial(add_kernel, t, riders),
        out_shape=shapes,
        in_specs=[vmem(), vmem()],
        out_specs=[vmem()] * len(shapes),
        compiler_params=params(),
        cost_estimate=cost(arrived.size),
        name="add",
    )(partials, arrived)


def last_kernel(low, partials, arrived, *refs):
    out, total, sem = refs[-3:]
    columns = total.shape[1]
    result = partials[lax.axis_index("seq")].astype(jnp.float32)
    result = result + arrived[:, :columns].astype(jnp.float32)
    total[...] = result.astype(out.dtype)
    copy = pltpu.make_async_copy(total, out.at[:, pl.ds(low, columns)], sem)
    copy.start()
    copy.wait()


def last_call(low, partials, arrived, out, shape):
    _, chunk, columns = partials.shape
    given = [] if out is None else [out]
    return pl.pallas_call(
        functools.partial(last_kernel, low),
        out_shape=shape,
        in_specs=[vmem()] * 2 + [hbm()] * len(given),
        out_specs=hbm(),
        scratch_shapes=[pltpu.VMEM((chunk, columns), shape.dtype), pltpu.SemaphoreType.DMA],
        input_output_aliases={2: 0} if given else {},
        compiler_params=params(),
        cost_estimate=cost(partials.size),
        name="last_sum",
    )(partials, arrived, *given)


def grad_kernel(spans, slots, block, table, rows, *refs):
    hidden, outs, (cols,) = refs[:spans], refs[spans : 2 * spans], refs[2 * spans :]
    me = lax.axis_index("seq")
    count, before = live_count(table, 0, slots), rank_before(table, 0, spans, slots)
    chunk = rows.shape[0] // spans
    for s in range(spans):
        cols[s] = hidden[s][:slots]
    for s in range(spans):
        slot = wrap(lax.rem(me + s, spans) - lax.rem(before, spans), spans)
        outs[s][...] = jnp.zeros_like(outs[s])

        @pl.when(slot < count)
        def _():
            d_start = pl.multiple_of(table[0, slots + slot] * block, block)
            total = jnp.zeros((block, block), jnp.float32)
            for p in range(spans):
                total = total + lax.dot_general(
                    cols[wrap(me - chunk_at(p), spans), slot],
                    rows[p * chunk : (p + 1) * chunk, pl.ds(d_start, block)],
                    TN,
                    preferred_element_type=jnp.float32,
                )
            outs[s][...] = total.astype(outs[s].dtype)


def grad_call(sizes, table, rows, hidden_cols):
    spans = sizes[0]
    slots, chunk, block = hidden_cols[0].shape
    slots -= 1
    return pl.pallas_call(
        functools.partial(grad_kernel, *sizes),
        out_shape=[jax.ShapeDtypeStruct((block, block), jnp.bfloat16)] * spans,
        in_specs=[smem()] + [vmem()] * (spans + 1),
        out_specs=[vmem()] * spans,
        scratch_shapes=[pltpu.VMEM((spans, slots, chunk, block), jnp.bfloat16)],
        compiler_params=params(),
        cost_estimate=cost(rows.size),
        name="tile_grad",
    )(table, rows, *hidden_cols)


def adam_kernel(spans, slots, columns, table, *refs):
    arrived, refs = refs[:spans], refs[spans:]
    values, one, two, values_new, one_new, two_new, grads = refs
    me = lax.axis_index("seq")
    for s in range(spans - 1):
        grads[s] = arrived[s][...]
    grads[spans - 1] = arrived[-1][:, columns:]
    befores = [rank_before(table, s, spans, slots) for s in range(spans)]
    counts = [live_count(table, s, slots) for s in range(spans)]
    for owned in range(slots):
        rank = owned * spans + me
        source, live = jnp.int32(0), jnp.int32(0)
        for s in range(spans):
            holds = (befores[s] <= rank) & (rank < befores[s] + counts[s])
            source, live = jnp.where(holds, s, source), jnp.where(holds, 1, live)
        grad = grads[source].astype(jnp.float32)
        stored, old_one, old_two = values[owned], one[owned], two[owned]
        new_one = BETA_ONE * old_one + (1.0 - BETA_ONE) * grad
        new_two = BETA_TWO * old_two + (1.0 - BETA_TWO) * grad * grad
        stepped = (
            new_one
            / (1.0 - BETA_ONE**STEP)
            / (jnp.sqrt(new_two / (1.0 - BETA_TWO**STEP)) + EPSILON)
        )
        values_new[owned] = jnp.where(live > 0, stored - RATE * stepped, stored)
        one_new[owned] = jnp.where(live > 0, new_one, old_one)
        two_new[owned] = jnp.where(live > 0, new_two, old_two)


def adam_call(sizes, columns, table, grads, *states):
    spans, slots, block = sizes
    tile = jax.ShapeDtypeStruct((slots, block, block), jnp.float32)
    return pl.pallas_call(
        functools.partial(adam_kernel, spans, slots, columns),
        out_shape=(tile, tile, tile),
        in_specs=[smem()] + [vmem()] * (spans + 3),
        out_specs=(vmem(), vmem(), vmem()),
        scratch_shapes=[pltpu.VMEM((spans, block, block), jnp.bfloat16)],
        compiler_params=params(),
        cost_estimate=cost(slots * block * block),
        name="adam",
    )(table, *grads, *[state[0, 0] for state in states])


def take_from(array, axis, places):
    size = lax.axis_size(axis)
    return lax.ppermute(array, axis, [((i + places) % size, i) for i in range(size)])


def take_chunk(own, place):
    tensors, cores = lax.axis_size("tensor"), lax.axis_size("dp")
    t_place, d_place = divmod(place, cores)
    pairs = []
    for t in range(tensors):
        for d in range(cores):
            source = (t + t_place) % tensors * cores + (d + d_place) % cores
            pairs.append((source, t * cores + d))
    return lax.ppermute(own, ("tensor", "dp"), pairs)


def exchange(pieces):
    return [pieces[0]] + [take_from(pieces[s], "seq", -s) for s in range(1, len(pieces))]


def per_device(
    hidden_in, cotangent, down_weight, tile_ids, tile_live, values, moment_one, moment_two
):
    spans, cores = lax.axis_size("seq"), lax.axis_size("dp")
    slots, block = values.shape[2], values.shape[3]
    f_width, d_width = down_weight.shape
    d_blocks, f_blocks = d_width // block, f_width // block
    chunk = hidden_in.shape[0]
    sizes = (spans, slots, block)
    group = max(size for size in range(1, 5) if f_blocks % size == 0)
    width = group * block
    ends = [sum(PARTS[:part]) for part in range(len(PARTS) + 1)]
    cuts = [(f_blocks // group) * end // ends[-1] for end in ends]
    ranges = list(zip(cuts[:-1], cuts[1:]))

    local = [take_chunk(cotangent, place) for place in range(1, cores)]
    remote = [take_chunk(cotangent, place) for place in range(cores, spans)]

    meta = jnp.concatenate([tile_ids[0], tile_live[0]], axis=1)
    metas = exchange([meta] * spans)
    values_half, hidden_here = pl.pallas_call(
        early_kernel,
        out_shape=[
            jax.ShapeDtypeStruct((slots, block, block), jnp.bfloat16),
            jax.ShapeDtypeStruct(hidden_in.shape, hidden_in.dtype),
        ],
        in_specs=[hbm(), hbm()],
        out_specs=[vmem(), vmem()],
        scratch_shapes=[
            pltpu.VMEM((slots, block, block), jnp.float32),
            pltpu.SemaphoreType.DMA((2,)),
        ],
        compiler_params=params(),
        cost_estimate=cost(hidden_in.size),
        name="early",
    )(stay(values[0, 0]), stay(hidden_in))
    local_rows, first_weight = pl.pallas_call(
        lay_kernel,
        out_shape=[
            jax.ShapeDtypeStruct((cores * chunk, d_width), cotangent.dtype),
            jax.ShapeDtypeStruct((ranges[0][1] * width, d_width), down_weight.dtype),
        ],
        in_specs=[hbm(), hbm()] + [vmem()] * (cores - 1),
        out_specs=[vmem(), vmem()],
        scratch_shapes=[pltpu.SemaphoreType.DMA((2,))],
        compiler_params=params(),
        cost_estimate=cost(cores * chunk * d_width),
        name="lay",
    )(stay(cotangent), stay(down_weight), *local)
    table, *picked = pl.pallas_call(
        functools.partial(pick_kernel, *sizes, d_blocks),
        out_shape=[jax.ShapeDtypeStruct((spans, 3 * slots), jnp.int32)]
        + [jax.ShapeDtypeStruct((slots + 1, chunk, block), jnp.bfloat16)] * spans,
        in_specs=[smem()] * spans + [vmem(), vmem()],
        out_specs=[smem()] + [vmem()] * spans,
        compiler_params=params(),
        cost_estimate=cost(hidden_in.size),
        name="pick",
    )(*metas, values_half, hidden_here)
    crossed = exchange(picked)

    early, rows = early_matmul_call(width, first_weight, [local_rows, *remote])
    partial, first, held = delta_call(sizes, table, early, rows, crossed)
    partials, moving = [partial], [take_from(first, "seq", -1)]
    for part in range(1, len(ranges)):
        low, high = ranges[part]
        if part == RIDE:
            moving[0] = add_call(2, partials[0], moving[0], block)[0]
            rows, moving[0] = lax.optimization_barrier((rows, moving[0]))
        partial, first = matmul_call(
            spans, low, (high - low,), width, table, down_weight, rows, held
        )
        if part == RIDE:
            grads = grad_call(sizes, table, rows, crossed)
            first = attach_call(first, grads[1:])
        partials.append(partial)
        moving.append(take_from(first, "seq", -1))

    tiles = [grads[0]]
    for t in range(2, spans):
        for part in range(len(ranges)):
            if (t, part) != (2, 0):
                moving[part], *mine = add_call(t, partials[part], moving[part], block)
                tiles += mine
            moving[part] = take_from(moving[part], "seq", -1)
    tiles.append(moving[RIDE])
    columns = partials[RIDE].shape[2]
    new = adam_call(sizes, columns, table, tiles, values, moment_one, moment_two)

    hidden_grad = None
    shape = jax.ShapeDtypeStruct((chunk, f_width), jnp.bfloat16)
    order = [part for part in range(len(ranges)) if part != LAST] + [LAST]
    for part in order:
        if part == LAST:
            moving[part], new = lax.optimization_barrier((moving[part], new))
        hidden_grad = last_call(
            ranges[part][0] * width, partials[part], moving[part], hidden_grad, shape
        )
    return (hidden_grad,) + tuple(array[None, None] for array in new)


def solution(mesh):
    shards = P(("groups", "seq"), ("tensor", "dp"))
    tiles = P(("groups", "seq"), ("tensor", "dp"), None, None, None)
    lists = P(("groups", "seq"), ("tensor", "dp"), None)
    return jax.shard_map(
        per_device,
        mesh=mesh,
        in_specs=(
            shards,
            P(("groups", "tensor", "dp"), "seq"),
            P(("tensor", "dp"), "seq"),
            lists,
            lists,
            tiles,
            tiles,
            tiles,
        ),
        out_specs=(shards, tiles, tiles, tiles),
        check_vma=False,
    )
```

```python
import functools

import jax
import jax.numpy as jnp
from jax import lax
from jax.experimental import pallas as pl
from jax.experimental.pallas import tpu as pltpu
from jax.sharding import PartitionSpec as P

STEP = 100
BETA_ONE = 0.9
BETA_TWO = 0.999
RATE = 0.01
EPSILON = 1e-08
VMEM_LIMIT = 24 * 1024 * 1024
MATMUL = 4096
EARLY = 1
PARTS = (2, 3, 2)
RIDE = 2
LAST = 0
LAID = 2
NT = (((1,), (1,)), ((), ()))
TN = (((0,), (0,)), ((), ()))


def vmem():
    return pl.BlockSpec(memory_space=pltpu.VMEM)


def smem():
    return pl.BlockSpec(memory_space=pltpu.SMEM)


def hbm():
    return pl.BlockSpec(memory_space=pltpu.HBM)


def stay(array):
    return pltpu.with_memory_space_constraint(array, pltpu.HBM)


def cost(count):
    return pl.CostEstimate(flops=count, bytes_accessed=2 * count, transcendentals=0)


def params():
    return pltpu.CompilerParams(vmem_limit_bytes=VMEM_LIMIT)


def wrap(index, size):
    return lax.rem(index + size, size)


def live_count(table, row, slots):
    count = table[row, 2 * slots]
    for slot in range(1, slots):
        count = count + table[row, 2 * slots + slot]
    return count


def rank_before(table, row, spans, slots):
    me = lax.axis_index("seq")
    before = jnp.int32(0)
    for other in range(spans):
        ahead = wrap(me - other, spans) < wrap(me - row, spans)
        before = before + jnp.where(ahead, live_count(table, other, slots), 0)
    return before


def early_kernel(values, hidden, own, *refs):
    others, (values_half, hidden_here, rows, stored, sems) = refs[:-5], refs[-5:]
    chunk = own.shape[0]
    copies = [
        pltpu.make_async_copy(values, stored, sems.at[0]),
        pltpu.make_async_copy(hidden, hidden_here, sems.at[1]),
        pltpu.make_async_copy(own, rows.at[pl.ds(0, chunk)], sems.at[2]),
    ]
    for copy in copies:
        copy.start()
    for p, other in enumerate(others):
        rows[(p + 1) * chunk : (p + 2) * chunk] = other[...]
    copies[0].wait()
    values_half[...] = stored[...].astype(values_half.dtype)
    copies[1].wait()
    copies[2].wait()


def pick_kernel(spans, slots, block, d_blocks, *refs):
    metas, (values, hidden, table), outs = refs[:spans], refs[spans : spans + 3], refs[spans + 3 :]
    me = lax.axis_index("seq")
    for s in range(spans):
        for j in range(slots):
            table[s, j] = lax.div(metas[s][0, j], d_blocks)
            table[s, slots + j] = lax.rem(metas[s][0, j], d_blocks)
            table[s, 2 * slots + j] = metas[s][0, slots + j]
    for s in range(spans):
        row = (spans - s) % spans
        before = rank_before(table, row, spans, slots)
        slot = wrap(me - lax.rem(before, spans), spans)
        tile = values[jnp.minimum(lax.div(before + slot, spans), slots - 1)]
        live = slot < live_count(table, row, slots)
        outs[s][slots] = jnp.where(live, tile.astype(jnp.float32), 0.0).astype(tile.dtype)
        for j in range(slots):
            start = pl.multiple_of(table[row, j] * block, block)
            outs[s][j] = hidden[:, pl.ds(start, block)]


def lay_kernel(weight, first_weight, sem):
    copy = pltpu.make_async_copy(weight.at[pl.ds(0, first_weight.shape[0])], first_weight, sem)
    copy.start()
    copy.wait()


def chunk_at(place):
    tensors, cores = lax.axis_size("tensor"), lax.axis_size("dp")
    t_place = lax.rem(lax.axis_index("tensor") + place // cores, tensors)
    d_place = lax.rem(lax.axis_index("dp") + place % cores, cores)
    return t_place * cores + d_place


def early_matmul_kernel(width, weight, *refs):
    pieces, (out, rows) = refs[:-2], refs[-2:]
    step = pl.program_id(0)

    @pl.when(step == 0)
    def _():
        at = 0
        for piece in pieces:
            rows[at : at + piece.shape[0]] = piece[...]
            at += piece.shape[0]

    here = pl.ds(pl.multiple_of(step * width, width), width)
    out[:, here] = lax.dot_general(
        rows[...], weight[here], NT, preferred_element_type=jnp.float32
    )


def early_matmul_call(width, columns, weight, pieces):
    tokens, d_width = sum(piece.shape[0] for piece in pieces), weight.shape[1]
    return pl.pallas_call(
        functools.partial(early_matmul_kernel, width),
        grid=(columns // width,),
        out_shape=[
            jax.ShapeDtypeStruct((tokens, columns), jnp.float32),
            jax.ShapeDtypeStruct((tokens, d_width), weight.dtype),
        ],
        in_specs=[vmem()] * (1 + len(pieces)),
        out_specs=[vmem()] * 2,
        compiler_params=params(),
        cost_estimate=cost(EARLY * tokens * columns),
        name="partial",
    )(weight, *pieces)


def add_delta(table, rows, held, total, low):
    slots, block, _ = held.shape
    count = live_count(table, 0, slots)
    for j in range(slots):
        f_start = table[0, j] * block - low

        @pl.when((j < count) & (f_start >= 0) & (f_start < total.shape[1]))
        def _():
            d_start = pl.multiple_of(table[0, slots + j] * block, block)
            place = pl.ds(pl.multiple_of(f_start, block), block)
            total[:, place] += lax.dot_general(
                rows[:, pl.ds(d_start, block)], held[j], NT, preferred_element_type=jnp.float32
            )


def put_chunks(total, out, first, here):
    spans, chunk = out.shape[:2]
    me = lax.axis_index("seq")
    for p in range(spans):
        result = total[p * chunk : (p + 1) * chunk].astype(out.dtype)
        out[chunk_at(p), :, here] = result

        @pl.when(chunk_at(p) == wrap(me - 1, spans))
        def _():
            first[:, here] = result


def delta_kernel(spans, slots, block, table, early, rows, *refs):
    stored, (out, first, held, total) = refs[:spans], refs[spans:]
    me = lax.axis_index("seq")
    before = rank_before(table, 0, spans, slots)
    for j in range(slots):
        for s in range(spans):

            @pl.when(lax.rem(before + j, spans) == wrap(me - s, spans))
            def _():
                held[j] = stored[s][slots]

    total[...] = early[...]
    add_delta(table, rows, held, total, 0)
    put_chunks(total, out, first, pl.ds(0, total.shape[1]))


def delta_call(sizes, table, early, rows, stored):
    spans, slots, block = sizes
    tokens, columns = early.shape
    return pl.pallas_call(
        functools.partial(delta_kernel, *sizes),
        out_shape=[
            jax.ShapeDtypeStruct((spans, tokens // spans, columns), rows.dtype),
            jax.ShapeDtypeStruct((tokens // spans, columns), rows.dtype),
            jax.ShapeDtypeStruct((slots, block, block), rows.dtype),
        ],
        in_specs=[smem()] + [vmem()] * (2 + spans),
        out_specs=[vmem()] * 3,
        scratch_shapes=[pltpu.VMEM((tokens, columns), jnp.float32)],
        compiler_params=params(),
        cost_estimate=cost(early.size),
        name="delta",
    )(table, early, rows, *stored)


def matmul_kernel(low, ends, table, weight, rows, held, *refs):
    outs, total = refs[:-1], refs[-1]
    step, width = pl.program_id(0), total.shape[1]
    if weight.shape[0] == width:
        weights = weight[...]
    else:
        weights = weight[pl.ds(pl.multiple_of((low + step) * width, width), width)]
    total[...] = lax.dot_general(rows[...], weights, NT, preferred_element_type=jnp.float32)
    add_delta(table, rows, held, total, (low + step) * width)
    for part, (begin, end) in enumerate(zip((0, *ends), ends)):

        @pl.when((step >= begin) & (step < end))
        def _():
            here = pl.ds(pl.multiple_of((step - begin) * width, width), width)
            put_chunks(total, *outs[2 * part : 2 * part + 2], here)


def matmul_call(spans, low, ends, width, table, weight, in_vmem, rows, held):
    tokens, d_width = rows.shape
    if in_vmem:
        weight_spec = vmem()
    else:
        weight, weight_spec = stay(weight), pl.BlockSpec((width, d_width), lambda i: (i + low, 0))
    shapes = []
    for begin, end in zip((0, *ends), ends):
        columns = (end - begin) * width
        shapes.append(jax.ShapeDtypeStruct((spans, tokens // spans, columns), rows.dtype))
        shapes.append(jax.ShapeDtypeStruct((tokens // spans, columns), rows.dtype))
    return pl.pallas_call(
        functools.partial(matmul_kernel, low, ends),
        grid=(ends[-1],),
        out_shape=shapes,
        in_specs=[smem(), weight_spec, vmem(), vmem()],
        out_specs=[vmem()] * len(shapes),
        scratch_shapes=[pltpu.VMEM((tokens, width), jnp.float32)],
        compiler_params=params(),
        cost_estimate=cost(MATMUL * tokens * ends[-1] * width),
        name="partial",
    )(table, weight, rows, held)


def attach_kernel(first, *refs):
    riders, out = refs[:-1], refs[-1]
    at = first.shape[1]
    out[:, :at] = first[...]
    for rider in riders:
        out[:, at : at + rider.shape[1]] = rider[...]
        at += rider.shape[1]


def attach_call(first, riders):
    chunk, columns = first.shape
    columns += sum(rider.shape[1] for rider in riders)
    return pl.pallas_call(
        attach_kernel,
        out_shape=jax.ShapeDtypeStruct((chunk, columns), first.dtype),
        in_specs=[vmem()] * (1 + len(riders)),
        out_specs=vmem(),
        compiler_params=params(),
        cost_estimate=cost(first.size),
        name="attach",
    )(first, *riders)


def add_kernel(t, riders, partials, arrived, out, *mine):
    spans, _, columns = partials.shape
    chunk = wrap(lax.axis_index("seq") - t, spans)
    result = partials[chunk].astype(jnp.float32) + arrived[:, :columns].astype(jnp.float32)
    out[:, :columns] = result.astype(out.dtype)
    if riders:
        block = mine[0].shape[1]
        mine[0][...] = arrived[:, columns : columns + block]
        out[:, columns:] = arrived[:, columns + block :]


def add_call(t, partials, arrived, block):
    chunk, columns = partials.shape[1:]
    riders = (arrived.shape[1] - columns) // block
    shapes = [jax.ShapeDtypeStruct((chunk, arrived.shape[1] - min(riders, 1) * block), arrived.dtype)]
    if riders:
        shapes.append(jax.ShapeDtypeStruct((chunk, block), arrived.dtype))
    return pl.pallas_call(
        functools.partial(add_kernel, t, riders),
        out_shape=shapes,
        in_specs=[vmem(), vmem()],
        out_specs=[vmem()] * len(shapes),
        compiler_params=params(),
        cost_estimate=cost(arrived.size),
        name="add",
    )(partials, arrived)


def last_kernel(low, partials, arrived, *refs):
    out, total, sem = refs[-3:]
    columns = total.shape[1]
    result = partials[lax.axis_index("seq")].astype(jnp.float32)
    result = result + arrived[:, :columns].astype(jnp.float32)
    total[...] = result.astype(out.dtype)
    copy = pltpu.make_async_copy(total, out.at[:, pl.ds(low, columns)], sem)
    copy.start()
    copy.wait()


def last_call(low, partials, arrived, out, shape):
    _, chunk, columns = partials.shape
    given = [] if out is None else [out]
    return pl.pallas_call(
        functools.partial(last_kernel, low),
        out_shape=shape,
        in_specs=[vmem()] * 2 + [hbm()] * len(given),
        out_specs=hbm(),
        scratch_shapes=[pltpu.VMEM((chunk, columns), shape.dtype), pltpu.SemaphoreType.DMA],
        input_output_aliases={2: 0} if given else {},
        compiler_params=params(),
        cost_estimate=cost(partials.size),
        name="last_sum",
    )(partials, arrived, *given)


def grad_kernel(spans, slots, block, table, rows, *refs):
    hidden, outs, (cols,) = refs[:spans], refs[spans : 2 * spans], refs[2 * spans :]
    me = lax.axis_index("seq")
    count, before = live_count(table, 0, slots), rank_before(table, 0, spans, slots)
    chunk = rows.shape[0] // spans
    for s in range(spans):
        cols[s] = hidden[s][:slots]
    for s in range(spans):
        slot = wrap(lax.rem(me + s, spans) - lax.rem(before, spans), spans)
        outs[s][...] = jnp.zeros_like(outs[s])

        @pl.when(slot < count)
        def _():
            d_start = pl.multiple_of(table[0, slots + slot] * block, block)
            total = jnp.zeros((block, block), jnp.float32)
            for p in range(spans):
                total = total + lax.dot_general(
                    cols[wrap(me - chunk_at(p), spans), slot],
                    rows[p * chunk : (p + 1) * chunk, pl.ds(d_start, block)],
                    TN,
                    preferred_element_type=jnp.float32,
                )
            outs[s][...] = total.astype(outs[s].dtype)


def grad_call(sizes, table, rows, hidden_cols):
    spans = sizes[0]
    slots, chunk, block = hidden_cols[0].shape
    slots -= 1
    return pl.pallas_call(
        functools.partial(grad_kernel, *sizes),
        out_shape=[jax.ShapeDtypeStruct((block, block), jnp.bfloat16)] * spans,
        in_specs=[smem()] + [vmem()] * (spans + 1),
        out_specs=[vmem()] * spans,
        scratch_shapes=[pltpu.VMEM((spans, slots, chunk, block), jnp.bfloat16)],
        compiler_params=params(),
        cost_estimate=cost(rows.size),
        name="tile_grad",
    )(table, rows, *hidden_cols)


def adam_kernel(spans, slots, columns, table, *refs):
    arrived, refs = refs[:spans], refs[spans:]
    values, one, two, values_new, one_new, two_new, grads = refs
    me = lax.axis_index("seq")
    for s in range(spans - 1):
        grads[s] = arrived[s][...]
    grads[spans - 1] = arrived[-1][:, columns:]
    befores = [rank_before(table, s, spans, slots) for s in range(spans)]
    counts = [live_count(table, s, slots) for s in range(spans)]
    for owned in range(slots):
        rank = owned * spans + me
        source, live = jnp.int32(0), jnp.int32(0)
        for s in range(spans):
            holds = (befores[s] <= rank) & (rank < befores[s] + counts[s])
            source, live = jnp.where(holds, s, source), jnp.where(holds, 1, live)
        grad = grads[source].astype(jnp.float32)
        stored, old_one, old_two = values[owned], one[owned], two[owned]
        new_one = BETA_ONE * old_one + (1.0 - BETA_ONE) * grad
        new_two = BETA_TWO * old_two + (1.0 - BETA_TWO) * grad * grad
        stepped = (
            new_one
            / (1.0 - BETA_ONE**STEP)
            / (jnp.sqrt(new_two / (1.0 - BETA_TWO**STEP)) + EPSILON)
        )
        values_new[owned] = jnp.where(live > 0, stored - RATE * stepped, stored)
        one_new[owned] = jnp.where(live > 0, new_one, old_one)
        two_new[owned] = jnp.where(live > 0, new_two, old_two)


def adam_call(sizes, columns, table, grads, *states):
    spans, slots, block = sizes
    tile = jax.ShapeDtypeStruct((slots, block, block), jnp.float32)
    return pl.pallas_call(
        functools.partial(adam_kernel, spans, slots, columns),
        out_shape=(tile, tile, tile),
        in_specs=[smem()] + [vmem()] * (spans + 3),
        out_specs=(vmem(), vmem(), vmem()),
        scratch_shapes=[pltpu.VMEM((spans, block, block), jnp.bfloat16)],
        compiler_params=params(),
        cost_estimate=cost(slots * block * block),
        name="adam",
    )(table, *grads, *[state[0, 0] for state in states])


def take_from(array, axis, places):
    size = lax.axis_size(axis)
    return lax.ppermute(array, axis, [((i + places) % size, i) for i in range(size)])


def take_chunk(own, place):
    tensors, cores = lax.axis_size("tensor"), lax.axis_size("dp")
    t_place, d_place = divmod(place, cores)
    pairs = []
    for t in range(tensors):
        for d in range(cores):
            source = (t + t_place) % tensors * cores + (d + d_place) % cores
            pairs.append((source, t * cores + d))
    return lax.ppermute(own, ("tensor", "dp"), pairs)


def exchange(pieces):
    return [pieces[0]] + [take_from(pieces[s], "seq", -s) for s in range(1, len(pieces))]


def per_device(
    hidden_in, cotangent, down_weight, tile_ids, tile_live, values, moment_one, moment_two
):
    spans, cores = lax.axis_size("seq"), lax.axis_size("dp")
    slots, block = values.shape[2], values.shape[3]
    f_width, d_width = down_weight.shape
    d_blocks, f_blocks = d_width // block, f_width // block
    chunk = hidden_in.shape[0]
    sizes = (spans, slots, block)
    group = max(size for size in range(1, 5) if f_blocks % size == 0)
    width = group * block
    ends = [sum(PARTS[:part]) for part in range(len(PARTS) + 1)]
    cuts = [(f_blocks // group) * end // ends[-1] for end in ends]
    ranges = list(zip(cuts[:-1], cuts[1:]))

    local = [take_chunk(cotangent, place) for place in range(1, cores)]
    remote = [take_chunk(cotangent, place) for place in range(cores, spans)]

    meta = jnp.concatenate([tile_ids[0], tile_live[0]], axis=1)
    metas = exchange([meta] * spans)
    values_half, hidden_here, local_rows = pl.pallas_call(
        early_kernel,
        out_shape=[
            jax.ShapeDtypeStruct((slots, block, block), jnp.bfloat16),
            jax.ShapeDtypeStruct(hidden_in.shape, hidden_in.dtype),
            jax.ShapeDtypeStruct((cores * chunk, d_width), cotangent.dtype),
        ],
        in_specs=[hbm()] * 3 + [vmem()] * (cores - 1),
        out_specs=[vmem()] * 3,
        scratch_shapes=[
            pltpu.VMEM((slots, block, block), jnp.float32),
            pltpu.SemaphoreType.DMA((3,)),
        ],
        compiler_params=params(),
        cost_estimate=cost(hidden_in.size),
        name="early",
    )(stay(values[0, 0]), stay(hidden_in), stay(cotangent), *local)
    table, *picked = pl.pallas_call(
        functools.partial(pick_kernel, *sizes, d_blocks),
        out_shape=[jax.ShapeDtypeStruct((spans, 3 * slots), jnp.int32)]
        + [jax.ShapeDtypeStruct((slots + 1, chunk, block), jnp.bfloat16)] * spans,
        in_specs=[smem()] * spans + [vmem(), vmem()],
        out_specs=[smem()] + [vmem()] * spans,
        compiler_params=params(),
        cost_estimate=cost(hidden_in.size),
        name="pick",
    )(*metas, values_half, hidden_here)
    crossed = exchange(picked)

    laid = ranges[LAID - 1][1]
    first_weight = pl.pallas_call(
        lay_kernel,
        out_shape=jax.ShapeDtypeStruct((laid * width, d_width), down_weight.dtype),
        in_specs=[hbm()],
        out_specs=vmem(),
        scratch_shapes=[pltpu.SemaphoreType.DMA],
        compiler_params=params(),
        cost_estimate=cost(laid * width * d_width),
        name="lay",
    )(stay(down_weight))

    early, rows = early_matmul_call(
        width, ranges[0][1] * width, first_weight, [local_rows, *remote]
    )
    partial, first, held = delta_call(sizes, table, early, rows, crossed)
    partials, moving = [partial], [take_from(first, "seq", -1)]
    for part in range(1, len(ranges)):
        low, high = ranges[part]
        if part == RIDE:
            moving[0] = add_call(2, partials[0], moving[0], block)[0]
            rows, moving[0] = lax.optimization_barrier((rows, moving[0]))
        partial, first = matmul_call(
            spans,
            low,
            (high - low,),
            width,
            table,
            first_weight if part < LAID else down_weight,
            part < LAID,
            rows,
            held,
        )
        if part == RIDE:
            grads = grad_call(sizes, table, rows, crossed)
            first = attach_call(first, grads[1:])
        partials.append(partial)
        moving.append(take_from(first, "seq", -1))

    tiles = [grads[0]]
    for t in range(2, spans):
        for part in range(len(ranges)):
            if (t, part) != (2, 0):
                moving[part], *mine = add_call(t, partials[part], moving[part], block)
                tiles += mine
            moving[part] = take_from(moving[part], "seq", -1)
    tiles.append(moving[RIDE])
    columns = partials[RIDE].shape[2]

    hidden_grad = None
    shape = jax.ShapeDtypeStruct((chunk, f_width), jnp.bfloat16)
    order = [part for part in range(len(ranges)) if part != LAST] + [LAST]
    for part in order:
        if part == LAST:
            tiles[0], hidden_grad = lax.optimization_barrier((tiles[0], hidden_grad))
            new = adam_call(sizes, columns, table, tiles, values, moment_one, moment_two)
            moving[part], new = lax.optimization_barrier((moving[part], new))
        hidden_grad = last_call(
            ranges[part][0] * width, partials[part], moving[part], hidden_grad, shape
        )
    return (hidden_grad,) + tuple(array[None, None] for array in new)


def solution(mesh):
    shards = P(("groups", "seq"), ("tensor", "dp"))
    tiles = P(("groups", "seq"), ("tensor", "dp"), None, None, None)
    lists = P(("groups", "seq"), ("tensor", "dp"), None)
    return jax.shard_map(
        per_device,
        mesh=mesh,
        in_specs=(
            shards,
            P(("groups", "tensor", "dp"), "seq"),
            P(("tensor", "dp"), "seq"),
            lists,
            lists,
            tiles,
            tiles,
            tiles,
        ),
        out_specs=(shards, tiles, tiles, tiles),
        check_vma=False,
    )
```

```python
import functools

import jax
import jax.numpy as jnp
from jax import lax
from jax.experimental import pallas as pl
from jax.experimental.pallas import tpu as pltpu
from jax.sharding import PartitionSpec as P

STEP = 100
BETA_ONE = 0.9
BETA_TWO = 0.999
RATE = 0.01
EPSILON = 1e-08
VMEM_LIMIT = 24 * 1024 * 1024
MATMUL = 4096
EARLY = 1
AHEAD = 100000
PARTS = (2, 3, 2)
RIDE = 2
LAST = 0
LAID = 2
NT = (((1,), (1,)), ((), ()))
TN = (((0,), (0,)), ((), ()))


def vmem():
    return pl.BlockSpec(memory_space=pltpu.VMEM)


def smem():
    return pl.BlockSpec(memory_space=pltpu.SMEM)


def hbm():
    return pl.BlockSpec(memory_space=pltpu.HBM)


def stay(array):
    return pltpu.with_memory_space_constraint(array, pltpu.HBM)


def cost(count):
    return pl.CostEstimate(flops=count, bytes_accessed=2 * count, transcendentals=0)


def params():
    return pltpu.CompilerParams(vmem_limit_bytes=VMEM_LIMIT)


def wrap(index, size):
    return lax.rem(index + size, size)


def live_count(table, row, slots):
    count = table[row, 2 * slots]
    for slot in range(1, slots):
        count = count + table[row, 2 * slots + slot]
    return count


def rank_before(table, row, spans, slots):
    me = lax.axis_index("seq")
    before = jnp.int32(0)
    for other in range(spans):
        ahead = wrap(me - other, spans) < wrap(me - row, spans)
        before = before + jnp.where(ahead, live_count(table, other, slots), 0)
    return before


def early_kernel(values, hidden, own, *refs):
    others, (values_half, hidden_here, rows, stored, sems) = refs[:-5], refs[-5:]
    chunk = own.shape[0]
    copies = [
        pltpu.make_async_copy(values, stored, sems.at[0]),
        pltpu.make_async_copy(hidden, hidden_here, sems.at[1]),
        pltpu.make_async_copy(own, rows.at[pl.ds(0, chunk)], sems.at[2]),
    ]
    for copy in copies:
        copy.start()
    for p, other in enumerate(others):
        rows[(p + 1) * chunk : (p + 2) * chunk] = other[...]
    copies[0].wait()
    values_half[...] = stored[...].astype(values_half.dtype)
    copies[1].wait()
    copies[2].wait()


def pick_kernel(spans, slots, block, d_blocks, *refs):
    metas, (values, hidden, table), outs = refs[:spans], refs[spans : spans + 3], refs[spans + 3 :]
    me = lax.axis_index("seq")
    for s in range(spans):
        for j in range(slots):
            table[s, j] = lax.div(metas[s][0, j], d_blocks)
            table[s, slots + j] = lax.rem(metas[s][0, j], d_blocks)
            table[s, 2 * slots + j] = metas[s][0, slots + j]
    for s in range(spans):
        row = (spans - s) % spans
        before = rank_before(table, row, spans, slots)
        slot = wrap(me - lax.rem(before, spans), spans)
        tile = values[jnp.minimum(lax.div(before + slot, spans), slots - 1)]
        live = slot < live_count(table, row, slots)
        outs[s][slots] = jnp.where(live, tile.astype(jnp.float32), 0.0).astype(tile.dtype)
        for j in range(slots):
            start = pl.multiple_of(table[row, j] * block, block)
            outs[s][j] = hidden[:, pl.ds(start, block)]


def lay_kernel(weight, first_weight, sem):
    copy = pltpu.make_async_copy(weight.at[pl.ds(0, first_weight.shape[0])], first_weight, sem)
    copy.start()
    copy.wait()


def chunk_at(place):
    tensors, cores = lax.axis_size("tensor"), lax.axis_size("dp")
    t_place = lax.rem(lax.axis_index("tensor") + place // cores, tensors)
    d_place = lax.rem(lax.axis_index("dp") + place % cores, cores)
    return t_place * cores + d_place


def early_matmul_kernel(width, weight, *refs):
    pieces, (out, rows) = refs[:-2], refs[-2:]
    step = pl.program_id(0)

    @pl.when(step == 0)
    def _():
        at = 0
        for piece in pieces:
            rows[at : at + piece.shape[0]] = piece[...]
            at += piece.shape[0]

    here = pl.ds(pl.multiple_of(step * width, width), width)
    out[:, here] = lax.dot_general(
        rows[...], weight[here], NT, preferred_element_type=jnp.float32
    )


def early_matmul_call(width, columns, weight, pieces):
    tokens, d_width = sum(piece.shape[0] for piece in pieces), weight.shape[1]
    return pl.pallas_call(
        functools.partial(early_matmul_kernel, width),
        grid=(columns // width,),
        out_shape=[
            jax.ShapeDtypeStruct((tokens, columns), jnp.float32),
            jax.ShapeDtypeStruct((tokens, d_width), weight.dtype),
        ],
        in_specs=[vmem()] * (1 + len(pieces)),
        out_specs=[vmem()] * 2,
        compiler_params=params(),
        cost_estimate=cost(EARLY * tokens * columns),
        name="partial",
    )(weight, *pieces)


def add_delta(table, rows, held, total, low):
    slots, block, _ = held.shape
    count = live_count(table, 0, slots)
    for j in range(slots):
        f_start = table[0, j] * block - low

        @pl.when((j < count) & (f_start >= 0) & (f_start < total.shape[1]))
        def _():
            d_start = pl.multiple_of(table[0, slots + j] * block, block)
            place = pl.ds(pl.multiple_of(f_start, block), block)
            total[:, place] += lax.dot_general(
                rows[:, pl.ds(d_start, block)], held[j], NT, preferred_element_type=jnp.float32
            )


def put_chunks(total, out, first, here):
    spans, chunk = out.shape[:2]
    me = lax.axis_index("seq")
    for p in range(spans):
        result = total[p * chunk : (p + 1) * chunk].astype(out.dtype)
        out[chunk_at(p), :, here] = result

        @pl.when(chunk_at(p) == wrap(me - 1, spans))
        def _():
            first[:, here] = result


def delta_kernel(spans, slots, block, table, early, rows, *refs):
    stored, (out, first, held, total) = refs[:spans], refs[spans:]
    me = lax.axis_index("seq")
    before = rank_before(table, 0, spans, slots)
    for j in range(slots):
        for s in range(spans):

            @pl.when(lax.rem(before + j, spans) == wrap(me - s, spans))
            def _():
                held[j] = stored[s][slots]

    total[...] = early[...]
    add_delta(table, rows, held, total, 0)
    put_chunks(total, out, first, pl.ds(0, total.shape[1]))


def delta_call(sizes, table, early, rows, stored):
    spans, slots, block = sizes
    tokens, columns = early.shape
    return pl.pallas_call(
        functools.partial(delta_kernel, *sizes),
        out_shape=[
            jax.ShapeDtypeStruct((spans, tokens // spans, columns), rows.dtype),
            jax.ShapeDtypeStruct((tokens // spans, columns), rows.dtype),
            jax.ShapeDtypeStruct((slots, block, block), rows.dtype),
        ],
        in_specs=[smem()] + [vmem()] * (2 + spans),
        out_specs=[vmem()] * 3,
        scratch_shapes=[pltpu.VMEM((tokens, columns), jnp.float32)],
        compiler_params=params(),
        cost_estimate=cost(early.size),
        name="delta",
    )(table, early, rows, *stored)


def matmul_kernel(low, ends, table, weight, rows, held, *refs):
    outs, total = refs[:-1], refs[-1]
    step, width = pl.program_id(0), total.shape[1]
    if weight.shape[0] == width:
        weights = weight[...]
    else:
        weights = weight[pl.ds(pl.multiple_of((low + step) * width, width), width)]
    total[...] = lax.dot_general(rows[...], weights, NT, preferred_element_type=jnp.float32)
    add_delta(table, rows, held, total, (low + step) * width)
    for part, (begin, end) in enumerate(zip((0, *ends), ends)):

        @pl.when((step >= begin) & (step < end))
        def _():
            here = pl.ds(pl.multiple_of((step - begin) * width, width), width)
            put_chunks(total, *outs[2 * part : 2 * part + 2], here)


def matmul_call(spans, low, ends, width, table, weight, in_vmem, rows, held):
    tokens, d_width = rows.shape
    if in_vmem:
        weight_spec = vmem()
    else:
        weight, weight_spec = stay(weight), pl.BlockSpec((width, d_width), lambda i: (i + low, 0))
    shapes = []
    for begin, end in zip((0, *ends), ends):
        columns = (end - begin) * width
        shapes.append(jax.ShapeDtypeStruct((spans, tokens // spans, columns), rows.dtype))
        shapes.append(jax.ShapeDtypeStruct((tokens // spans, columns), rows.dtype))
    return pl.pallas_call(
        functools.partial(matmul_kernel, low, ends),
        grid=(ends[-1],),
        out_shape=shapes,
        in_specs=[smem(), weight_spec, vmem(), vmem()],
        out_specs=[vmem()] * len(shapes),
        scratch_shapes=[pltpu.VMEM((tokens, width), jnp.float32)],
        compiler_params=params(),
        cost_estimate=cost(MATMUL * tokens * ends[-1] * width),
        name="partial",
    )(table, weight, rows, held)


def attach_kernel(first, *refs):
    riders, out = refs[:-1], refs[-1]
    at = first.shape[1]
    out[:, :at] = first[...]
    for rider in riders:
        out[:, at : at + rider.shape[1]] = rider[...]
        at += rider.shape[1]


def attach_call(first, riders):
    chunk, columns = first.shape
    columns += sum(rider.shape[1] for rider in riders)
    return pl.pallas_call(
        attach_kernel,
        out_shape=jax.ShapeDtypeStruct((chunk, columns), first.dtype),
        in_specs=[vmem()] * (1 + len(riders)),
        out_specs=vmem(),
        compiler_params=params(),
        cost_estimate=cost(first.size),
        name="attach",
    )(first, *riders)


def add_kernel(t, riders, partials, arrived, out, *mine):
    spans, _, columns = partials.shape
    chunk = wrap(lax.axis_index("seq") - t, spans)
    result = partials[chunk].astype(jnp.float32) + arrived[:, :columns].astype(jnp.float32)
    out[:, :columns] = result.astype(out.dtype)
    if riders:
        block = mine[0].shape[1]
        mine[0][...] = arrived[:, columns : columns + block]
        out[:, columns:] = arrived[:, columns + block :]


def add_call(t, partials, arrived, block):
    chunk, columns = partials.shape[1:]
    riders = (arrived.shape[1] - columns) // block
    shapes = [jax.ShapeDtypeStruct((chunk, arrived.shape[1] - min(riders, 1) * block), arrived.dtype)]
    if riders:
        shapes.append(jax.ShapeDtypeStruct((chunk, block), arrived.dtype))
    return pl.pallas_call(
        functools.partial(add_kernel, t, riders),
        out_shape=shapes,
        in_specs=[vmem(), vmem()],
        out_specs=[vmem()] * len(shapes),
        compiler_params=params(),
        cost_estimate=cost(arrived.size),
        name="add",
    )(partials, arrived)


def last_kernel(low, partials, arrived, *refs):
    out, total, sem = refs[-3:]
    columns = total.shape[1]
    result = partials[lax.axis_index("seq")].astype(jnp.float32)
    result = result + arrived[:, :columns].astype(jnp.float32)
    total[...] = result.astype(out.dtype)
    copy = pltpu.make_async_copy(total, out.at[:, pl.ds(low, columns)], sem)
    copy.start()
    copy.wait()


def last_call(low, partials, arrived, out, shape):
    _, chunk, columns = partials.shape
    given = [] if out is None else [out]
    return pl.pallas_call(
        functools.partial(last_kernel, low),
        out_shape=shape,
        in_specs=[vmem()] * 2 + [hbm()] * len(given),
        out_specs=hbm(),
        scratch_shapes=[pltpu.VMEM((chunk, columns), shape.dtype), pltpu.SemaphoreType.DMA],
        input_output_aliases={2: 0} if given else {},
        compiler_params=params(),
        cost_estimate=cost(partials.size),
        name="last_sum",
    )(partials, arrived, *given)


def grad_kernel(spans, slots, block, table, rows, *refs):
    hidden, outs, (cols,) = refs[:spans], refs[spans : 2 * spans], refs[2 * spans :]
    me = lax.axis_index("seq")
    count, before = live_count(table, 0, slots), rank_before(table, 0, spans, slots)
    chunk = rows.shape[0] // spans
    for s in range(spans):
        cols[s] = hidden[s][:slots]
    for s in range(spans):
        slot = wrap(lax.rem(me + s, spans) - lax.rem(before, spans), spans)
        outs[s][...] = jnp.zeros_like(outs[s])

        @pl.when(slot < count)
        def _():
            d_start = pl.multiple_of(table[0, slots + slot] * block, block)
            total = jnp.zeros((block, block), jnp.float32)
            for p in range(spans):
                total = total + lax.dot_general(
                    cols[wrap(me - chunk_at(p), spans), slot],
                    rows[p * chunk : (p + 1) * chunk, pl.ds(d_start, block)],
                    TN,
                    preferred_element_type=jnp.float32,
                )
            outs[s][...] = total.astype(outs[s].dtype)


def grad_call(sizes, table, rows, hidden_cols):
    spans = sizes[0]
    slots, chunk, block = hidden_cols[0].shape
    slots -= 1
    return pl.pallas_call(
        functools.partial(grad_kernel, *sizes),
        out_shape=[jax.ShapeDtypeStruct((block, block), jnp.bfloat16)] * spans,
        in_specs=[smem()] + [vmem()] * (spans + 1),
        out_specs=[vmem()] * spans,
        scratch_shapes=[pltpu.VMEM((spans, slots, chunk, block), jnp.bfloat16)],
        compiler_params=params(),
        cost_estimate=cost(rows.size),
        name="tile_grad",
    )(table, rows, *hidden_cols)


def adam_kernel(spans, slots, columns, table, *refs):
    arrived, refs = refs[:spans], refs[spans:]
    values, one, two, values_new, one_new, two_new, grads = refs
    me = lax.axis_index("seq")
    for s in range(spans - 1):
        grads[s] = arrived[s][...]
    grads[spans - 1] = arrived[-1][:, columns:]
    befores = [rank_before(table, s, spans, slots) for s in range(spans)]
    counts = [live_count(table, s, slots) for s in range(spans)]
    for owned in range(slots):
        rank = owned * spans + me
        source, live = jnp.int32(0), jnp.int32(0)
        for s in range(spans):
            holds = (befores[s] <= rank) & (rank < befores[s] + counts[s])
            source, live = jnp.where(holds, s, source), jnp.where(holds, 1, live)
        grad = grads[source].astype(jnp.float32)
        stored, old_one, old_two = values[owned], one[owned], two[owned]
        new_one = BETA_ONE * old_one + (1.0 - BETA_ONE) * grad
        new_two = BETA_TWO * old_two + (1.0 - BETA_TWO) * grad * grad
        stepped = (
            new_one
            / (1.0 - BETA_ONE**STEP)
            / (jnp.sqrt(new_two / (1.0 - BETA_TWO**STEP)) + EPSILON)
        )
        values_new[owned] = jnp.where(live > 0, stored - RATE * stepped, stored)
        one_new[owned] = jnp.where(live > 0, new_one, old_one)
        two_new[owned] = jnp.where(live > 0, new_two, old_two)


def adam_call(sizes, columns, table, grads, *states):
    spans, slots, block = sizes
    tile = jax.ShapeDtypeStruct((slots, block, block), jnp.float32)
    return pl.pallas_call(
        functools.partial(adam_kernel, spans, slots, columns),
        out_shape=(tile, tile, tile),
        in_specs=[smem()] + [vmem()] * (spans + 3),
        out_specs=(vmem(), vmem(), vmem()),
        scratch_shapes=[pltpu.VMEM((spans, block, block), jnp.bfloat16)],
        compiler_params=params(),
        cost_estimate=cost(slots * block * block),
        name="adam",
    )(table, *grads, *[state[0, 0] for state in states])


def take_from(array, axis, places):
    size = lax.axis_size(axis)
    return lax.ppermute(array, axis, [((i + places) % size, i) for i in range(size)])


def take_chunk(own, place):
    tensors, cores = lax.axis_size("tensor"), lax.axis_size("dp")
    t_place, d_place = divmod(place, cores)
    pairs = []
    for t in range(tensors):
        for d in range(cores):
            source = (t + t_place) % tensors * cores + (d + d_place) % cores
            pairs.append((source, t * cores + d))
    return lax.ppermute(own, ("tensor", "dp"), pairs)


def exchange(pieces):
    return [pieces[0]] + [take_from(pieces[s], "seq", -s) for s in range(1, len(pieces))]


def per_device(
    hidden_in, cotangent, down_weight, tile_ids, tile_live, values, moment_one, moment_two
):
    spans, cores = lax.axis_size("seq"), lax.axis_size("dp")
    slots, block = values.shape[2], values.shape[3]
    f_width, d_width = down_weight.shape
    d_blocks, f_blocks = d_width // block, f_width // block
    chunk = hidden_in.shape[0]
    sizes = (spans, slots, block)
    group = max(size for size in range(1, 5) if f_blocks % size == 0)
    width = group * block
    ends = [sum(PARTS[:part]) for part in range(len(PARTS) + 1)]
    cuts = [(f_blocks // group) * end // ends[-1] for end in ends]
    ranges = list(zip(cuts[:-1], cuts[1:]))

    local = [take_chunk(cotangent, place) for place in range(1, cores)]
    firsts = [take_from(cotangent, "tensor", t) for t in range(1, lax.axis_size("tensor"))]

    meta = jnp.concatenate([tile_ids[0], tile_live[0]], axis=1)
    metas = exchange([meta] * spans)
    values_half, hidden_here, local_rows = pl.pallas_call(
        early_kernel,
        out_shape=[
            jax.ShapeDtypeStruct((slots, block, block), jnp.bfloat16),
            jax.ShapeDtypeStruct(hidden_in.shape, hidden_in.dtype),
            jax.ShapeDtypeStruct((cores * chunk, d_width), cotangent.dtype),
        ],
        in_specs=[hbm()] * 3 + [vmem()] * (cores - 1),
        out_specs=[vmem()] * 3,
        scratch_shapes=[
            pltpu.VMEM((slots, block, block), jnp.float32),
            pltpu.SemaphoreType.DMA((3,)),
        ],
        compiler_params=params(),
        cost_estimate=cost(hidden_in.size),
        name="early",
    )(stay(values[0, 0]), stay(hidden_in), stay(cotangent), *local)
    table, *picked = pl.pallas_call(
        functools.partial(pick_kernel, *sizes, d_blocks),
        out_shape=[jax.ShapeDtypeStruct((spans, 3 * slots), jnp.int32)]
        + [jax.ShapeDtypeStruct((slots + 1, chunk, block), jnp.bfloat16)] * spans,
        in_specs=[smem()] * spans + [vmem(), vmem()],
        out_specs=[smem()] + [vmem()] * spans,
        compiler_params=params(),
        cost_estimate=cost(hidden_in.size),
        name="pick",
    )(*metas, values_half, hidden_here)
    crossed = exchange(picked)

    laid = ranges[LAID - 1][1]
    first_weight = pl.pallas_call(
        lay_kernel,
        out_shape=jax.ShapeDtypeStruct((laid * width, d_width), down_weight.dtype),
        in_specs=[hbm()],
        out_specs=vmem(),
        scratch_shapes=[pltpu.SemaphoreType.DMA],
        compiler_params=params(),
        cost_estimate=cost(AHEAD * laid * width * d_width),
        name="lay",
    )(stay(down_weight))

    firsts, picked = lax.optimization_barrier((firsts, picked))
    remote = []
    for first in firsts:
        remote += [first] + [take_from(first, "dp", d) for d in range(1, cores)]
    early, rows = early_matmul_call(
        width, ranges[0][1] * width, first_weight, [local_rows, *remote]
    )
    partial, first, held = delta_call(sizes, table, early, rows, crossed)
    partials, moving = [partial], [take_from(first, "seq", -1)]
    for part in range(1, len(ranges)):
        low, high = ranges[part]
        if part == RIDE:
            moving[0] = add_call(2, partials[0], moving[0], block)[0]
            rows, moving[0] = lax.optimization_barrier((rows, moving[0]))
        partial, first = matmul_call(
            spans,
            low,
            (high - low,),
            width,
            table,
            first_weight if part < LAID else down_weight,
            part < LAID,
            rows,
            held,
        )
        if part == RIDE:
            grads = grad_call(sizes, table, rows, crossed)
            first = attach_call(first, grads[1:])
        partials.append(partial)
        moving.append(take_from(first, "seq", -1))

    tiles = [grads[0]]
    for t in range(2, spans):
        for part in range(len(ranges)):
            if (t, part) != (2, 0):
                moving[part], *mine = add_call(t, partials[part], moving[part], block)
                tiles += mine
            moving[part] = take_from(moving[part], "seq", -1)
    tiles.append(moving[RIDE])
    columns = partials[RIDE].shape[2]

    hidden_grad = None
    shape = jax.ShapeDtypeStruct((chunk, f_width), jnp.bfloat16)
    order = [part for part in range(len(ranges)) if part != LAST] + [LAST]
    for part in order:
        if part == LAST:
            tiles[0], hidden_grad = lax.optimization_barrier((tiles[0], hidden_grad))
            new = adam_call(sizes, columns, table, tiles, values, moment_one, moment_two)
            moving[part], new = lax.optimization_barrier((moving[part], new))
        hidden_grad = last_call(
            ranges[part][0] * width, partials[part], moving[part], hidden_grad, shape
        )
    return (hidden_grad,) + tuple(array[None, None] for array in new)


def solution(mesh):
    shards = P(("groups", "seq"), ("tensor", "dp"))
    tiles = P(("groups", "seq"), ("tensor", "dp"), None, None, None)
    lists = P(("groups", "seq"), ("tensor", "dp"), None)
    return jax.shard_map(
        per_device,
        mesh=mesh,
        in_specs=(
            shards,
            P(("groups", "tensor", "dp"), "seq"),
            P(("tensor", "dp"), "seq"),
            lists,
            lists,
            tiles,
            tiles,
            tiles,
        ),
        out_specs=(shards, tiles, tiles, tiles),
        check_vma=False,
    )
```

```python
import functools

import jax
import jax.numpy as jnp
from jax import lax
from jax.experimental import pallas as pl
from jax.experimental.pallas import tpu as pltpu
from jax.sharding import PartitionSpec as P

STEP = 100
BETA_ONE = 0.9
BETA_TWO = 0.999
RATE = 0.01
EPSILON = 1e-08
VMEM_LIMIT = 12 * 1024 * 1024
MATMUL = 4096
EARLY = 1
AHEAD = 5000
PARTS = (2, 3, 2)
RIDE = 2
LAST = 0
LAID = 2
NT = (((1,), (1,)), ((), ()))
TN = (((0,), (0,)), ((), ()))


def vmem():
    return pl.BlockSpec(memory_space=pltpu.VMEM)


def smem():
    return pl.BlockSpec(memory_space=pltpu.SMEM)


def hbm():
    return pl.BlockSpec(memory_space=pltpu.HBM)


def stay(array):
    return pltpu.with_memory_space_constraint(array, pltpu.HBM)


def cost(count):
    return pl.CostEstimate(flops=count, bytes_accessed=2 * count, transcendentals=0)


def params():
    return pltpu.CompilerParams(vmem_limit_bytes=VMEM_LIMIT)


def wrap(index, size):
    return lax.rem(index + size, size)


def live_count(table, row, slots):
    count = table[row, 2 * slots]
    for slot in range(1, slots):
        count = count + table[row, 2 * slots + slot]
    return count


def rank_before(table, row, spans, slots):
    me = lax.axis_index("seq")
    before = jnp.int32(0)
    for other in range(spans):
        ahead = wrap(me - other, spans) < wrap(me - row, spans)
        before = before + jnp.where(ahead, live_count(table, other, slots), 0)
    return before


def early_kernel(values, hidden, own, *refs):
    others, (values_half, hidden_here, rows, stored, sems) = refs[:-5], refs[-5:]
    chunk = own.shape[0]
    copies = [
        pltpu.make_async_copy(values, stored, sems.at[0]),
        pltpu.make_async_copy(hidden, hidden_here, sems.at[1]),
        pltpu.make_async_copy(own, rows.at[pl.ds(0, chunk)], sems.at[2]),
    ]
    for copy in copies:
        copy.start()
    for p, other in enumerate(others):
        rows[(p + 1) * chunk : (p + 2) * chunk] = other[...]
    copies[0].wait()
    values_half[...] = stored[...].astype(values_half.dtype)
    copies[1].wait()
    copies[2].wait()


def pick_kernel(spans, slots, block, d_blocks, *refs):
    metas, (values, hidden, table), outs = refs[:spans], refs[spans : spans + 3], refs[spans + 3 :]
    me = lax.axis_index("seq")
    for s in range(spans):
        for j in range(slots):
            table[s, j] = lax.div(metas[s][0, j], d_blocks)
            table[s, slots + j] = lax.rem(metas[s][0, j], d_blocks)
            table[s, 2 * slots + j] = metas[s][0, slots + j]
    for s in range(spans):
        row = (spans - s) % spans
        before = rank_before(table, row, spans, slots)
        slot = wrap(me - lax.rem(before, spans), spans)
        tile = values[jnp.minimum(lax.div(before + slot, spans), slots - 1)]
        live = slot < live_count(table, row, slots)
        outs[s][slots] = jnp.where(live, tile.astype(jnp.float32), 0.0).astype(tile.dtype)
        for j in range(slots):
            start = pl.multiple_of(table[row, j] * block, block)
            outs[s][j] = hidden[:, pl.ds(start, block)]


def lay_kernel(weight, first_weight, sem):
    copy = pltpu.make_async_copy(weight.at[pl.ds(0, first_weight.shape[0])], first_weight, sem)
    copy.start()
    copy.wait()


def chunk_at(place):
    tensors, cores = lax.axis_size("tensor"), lax.axis_size("dp")
    t_place = lax.rem(lax.axis_index("tensor") + place // cores, tensors)
    d_place = lax.rem(lax.axis_index("dp") + place % cores, cores)
    return t_place * cores + d_place


def early_matmul_kernel(width, weight, *refs):
    pieces, (out, rows) = refs[:-2], refs[-2:]
    step = pl.program_id(0)

    @pl.when(step == 0)
    def _():
        at = 0
        for piece in pieces:
            rows[at : at + piece.shape[0]] = piece[...]
            at += piece.shape[0]

    here = pl.ds(pl.multiple_of(step * width, width), width)
    out[:, here] = lax.dot_general(
        rows[...], weight[here], NT, preferred_element_type=jnp.float32
    )


def early_matmul_call(width, columns, weight, pieces):
    tokens, d_width = sum(piece.shape[0] for piece in pieces), weight.shape[1]
    return pl.pallas_call(
        functools.partial(early_matmul_kernel, width),
        grid=(columns // width,),
        out_shape=[
            jax.ShapeDtypeStruct((tokens, columns), jnp.float32),
            jax.ShapeDtypeStruct((tokens, d_width), weight.dtype),
        ],
        in_specs=[vmem()] * (1 + len(pieces)),
        out_specs=[vmem()] * 2,
        compiler_params=params(),
        cost_estimate=cost(EARLY * tokens * columns),
        name="partial",
    )(weight, *pieces)


def add_delta(table, rows, held, total, low):
    slots, block, _ = held.shape
    count = live_count(table, 0, slots)
    for j in range(slots):
        f_start = table[0, j] * block - low

        @pl.when((j < count) & (f_start >= 0) & (f_start < total.shape[1]))
        def _():
            d_start = pl.multiple_of(table[0, slots + j] * block, block)
            place = pl.ds(pl.multiple_of(f_start, block), block)
            total[:, place] += lax.dot_general(
                rows[:, pl.ds(d_start, block)], held[j], NT, preferred_element_type=jnp.float32
            )


def put_chunks(total, out, first, here):
    spans, chunk = out.shape[:2]
    me = lax.axis_index("seq")
    for p in range(spans):
        result = total[p * chunk : (p + 1) * chunk].astype(out.dtype)
        out[chunk_at(p), :, here] = result

        @pl.when(chunk_at(p) == wrap(me - 1, spans))
        def _():
            first[:, here] = result


def held_kernel(spans, slots, block, table, *refs):
    stored, held = refs[:-1], refs[-1]
    me = lax.axis_index("seq")
    before = rank_before(table, 0, spans, slots)
    for j in range(slots):
        for s in range(spans):

            @pl.when(lax.rem(before + j, spans) == wrap(me - s, spans))
            def _():
                held[j] = stored[s][slots]


def delta_kernel(sizes, low, stores, table, early, rows, *refs):
    given, (out, first, *more, total) = refs[:stores], refs[stores:]
    if stores > 1:
        (held,) = more
        held_kernel(*sizes, table, *given, held)
    else:
        (held,) = given
    total[...] = early[:, low : low + total.shape[1]]
    add_delta(table, rows, held, total, low)
    put_chunks(total, out, first, pl.ds(0, total.shape[1]))


def delta_call(sizes, low, high, table, early, rows, given):
    spans, slots, block = sizes
    tokens, columns = early.shape[0], high - low
    shapes = [
        jax.ShapeDtypeStruct((spans, tokens // spans, columns), rows.dtype),
        jax.ShapeDtypeStruct((tokens // spans, columns), rows.dtype),
    ]
    if len(given) > 1:
        shapes.append(jax.ShapeDtypeStruct((slots, block, block), rows.dtype))
    return pl.pallas_call(
        functools.partial(delta_kernel, sizes, low, len(given)),
        out_shape=shapes,
        in_specs=[smem()] + [vmem()] * (2 + len(given)),
        out_specs=[vmem()] * len(shapes),
        scratch_shapes=[pltpu.VMEM((tokens, columns), jnp.float32)],
        compiler_params=params(),
        cost_estimate=cost(early.size),
        name="delta",
    )(table, early, rows, *given)


def matmul_kernel(low, ends, table, weight, rows, held, *refs):
    outs, total = refs[:-1], refs[-1]
    step, width = pl.program_id(0), total.shape[1]
    total[...] = lax.dot_general(rows[...], weight[...], NT, preferred_element_type=jnp.float32)
    add_delta(table, rows, held, total, (low + step) * width)
    for part, (begin, end) in enumerate(zip((0, *ends), ends)):

        @pl.when((step >= begin) & (step < end))
        def _():
            here = pl.ds(pl.multiple_of((step - begin) * width, width), width)
            put_chunks(total, *outs[2 * part : 2 * part + 2], here)


def matmul_call(spans, low, ends, width, table, weight, rows, held):
    tokens, d_width = rows.shape
    weight_spec = pl.BlockSpec((width, d_width), lambda i: (i + low, 0))
    shapes = []
    for begin, end in zip((0, *ends), ends):
        columns = (end - begin) * width
        shapes.append(jax.ShapeDtypeStruct((spans, tokens // spans, columns), rows.dtype))
        shapes.append(jax.ShapeDtypeStruct((tokens // spans, columns), rows.dtype))
    return pl.pallas_call(
        functools.partial(matmul_kernel, low, ends),
        grid=(ends[-1],),
        out_shape=shapes,
        in_specs=[smem(), weight_spec, vmem(), vmem()],
        out_specs=[vmem()] * len(shapes),
        scratch_shapes=[pltpu.VMEM((tokens, width), jnp.float32)],
        compiler_params=params(),
        cost_estimate=cost(MATMUL * tokens * ends[-1] * width),
        name="partial",
    )(table, stay(weight), rows, held)


def attach_kernel(first, *refs):
    riders, out = refs[:-1], refs[-1]
    at = first.shape[1]
    out[:, :at] = first[...]
    for rider in riders:
        out[:, at : at + rider.shape[1]] = rider[...]
        at += rider.shape[1]


def attach_call(first, riders):
    chunk, columns = first.shape
    columns += sum(rider.shape[1] for rider in riders)
    return pl.pallas_call(
        attach_kernel,
        out_shape=jax.ShapeDtypeStruct((chunk, columns), first.dtype),
        in_specs=[vmem()] * (1 + len(riders)),
        out_specs=vmem(),
        compiler_params=params(),
        cost_estimate=cost(first.size),
        name="attach",
    )(first, *riders)


def add_kernel(t, riders, partials, arrived, out, *mine):
    spans, _, columns = partials.shape
    chunk = wrap(lax.axis_index("seq") - t, spans)
    result = partials[chunk].astype(jnp.float32) + arrived[:, :columns].astype(jnp.float32)
    out[:, :columns] = result.astype(out.dtype)
    if riders:
        block = mine[0].shape[1]
        mine[0][...] = arrived[:, columns : columns + block]
        out[:, columns:] = arrived[:, columns + block :]


def add_call(t, partials, arrived, block):
    chunk, columns = partials.shape[1:]
    riders = (arrived.shape[1] - columns) // block
    shapes = [jax.ShapeDtypeStruct((chunk, arrived.shape[1] - min(riders, 1) * block), arrived.dtype)]
    if riders:
        shapes.append(jax.ShapeDtypeStruct((chunk, block), arrived.dtype))
    return pl.pallas_call(
        functools.partial(add_kernel, t, riders),
        out_shape=shapes,
        in_specs=[vmem(), vmem()],
        out_specs=[vmem()] * len(shapes),
        compiler_params=params(),
        cost_estimate=cost(arrived.size),
        name="add",
    )(partials, arrived)


def last_kernel(low, partials, arrived, *refs):
    out, total, sem = refs[-3:]
    columns = total.shape[1]
    result = partials[lax.axis_index("seq")].astype(jnp.float32)
    result = result + arrived[:, :columns].astype(jnp.float32)
    total[...] = result.astype(out.dtype)
    copy = pltpu.make_async_copy(total, out.at[:, pl.ds(low, columns)], sem)
    copy.start()
    copy.wait()


def last_call(low, partials, arrived, out, shape):
    _, chunk, columns = partials.shape
    given = [] if out is None else [out]
    return pl.pallas_call(
        functools.partial(last_kernel, low),
        out_shape=shape,
        in_specs=[vmem()] * 2 + [hbm()] * len(given),
        out_specs=hbm(),
        scratch_shapes=[pltpu.VMEM((chunk, columns), shape.dtype), pltpu.SemaphoreType.DMA],
        input_output_aliases={2: 0} if given else {},
        compiler_params=params(),
        cost_estimate=cost(partials.size),
        name="last_sum",
    )(partials, arrived, *given)


def grad_kernel(spans, slots, block, table, rows, *refs):
    hidden, outs, (cols,) = refs[:spans], refs[spans : 2 * spans], refs[2 * spans :]
    me = lax.axis_index("seq")
    count, before = live_count(table, 0, slots), rank_before(table, 0, spans, slots)
    chunk = rows.shape[0] // spans
    for s in range(spans):
        cols[s] = hidden[s][:slots]
    for s in range(spans):
        slot = wrap(lax.rem(me + s, spans) - lax.rem(before, spans), spans)
        outs[s][...] = jnp.zeros_like(outs[s])

        @pl.when(slot < count)
        def _():
            d_start = pl.multiple_of(table[0, slots + slot] * block, block)
            total = jnp.zeros((block, block), jnp.float32)
            for p in range(spans):
                total = total + lax.dot_general(
                    cols[wrap(me - chunk_at(p), spans), slot],
                    rows[p * chunk : (p + 1) * chunk, pl.ds(d_start, block)],
                    TN,
                    preferred_element_type=jnp.float32,
                )
            outs[s][...] = total.astype(outs[s].dtype)


def grad_call(sizes, table, rows, hidden_cols):
    spans = sizes[0]
    slots, chunk, block = hidden_cols[0].shape
    slots -= 1
    return pl.pallas_call(
        functools.partial(grad_kernel, *sizes),
        out_shape=[jax.ShapeDtypeStruct((block, block), jnp.bfloat16)] * spans,
        in_specs=[smem()] + [vmem()] * (spans + 1),
        out_specs=[vmem()] * spans,
        scratch_shapes=[pltpu.VMEM((spans, slots, chunk, block), jnp.bfloat16)],
        compiler_params=params(),
        cost_estimate=cost(rows.size),
        name="tile_grad",
    )(table, rows, *hidden_cols)


def adam_kernel(spans, slots, columns, table, *refs):
    arrived, refs = refs[:spans], refs[spans:]
    values, one, two, values_new, one_new, two_new, grads = refs
    me = lax.axis_index("seq")
    for s in range(spans - 1):
        grads[s] = arrived[s][...]
    grads[spans - 1] = arrived[-1][:, columns:]
    befores = [rank_before(table, s, spans, slots) for s in range(spans)]
    counts = [live_count(table, s, slots) for s in range(spans)]
    for owned in range(slots):
        rank = owned * spans + me
        source, live = jnp.int32(0), jnp.int32(0)
        for s in range(spans):
            holds = (befores[s] <= rank) & (rank < befores[s] + counts[s])
            source, live = jnp.where(holds, s, source), jnp.where(holds, 1, live)
        grad = grads[source].astype(jnp.float32)
        stored, old_one, old_two = values[owned], one[owned], two[owned]
        new_one = BETA_ONE * old_one + (1.0 - BETA_ONE) * grad
        new_two = BETA_TWO * old_two + (1.0 - BETA_TWO) * grad * grad
        stepped = (
            new_one
            / (1.0 - BETA_ONE**STEP)
            / (jnp.sqrt(new_two / (1.0 - BETA_TWO**STEP)) + EPSILON)
        )
        values_new[owned] = jnp.where(live > 0, stored - RATE * stepped, stored)
        one_new[owned] = jnp.where(live > 0, new_one, old_one)
        two_new[owned] = jnp.where(live > 0, new_two, old_two)


def adam_call(sizes, columns, table, grads, *states):
    spans, slots, block = sizes
    tile = jax.ShapeDtypeStruct((slots, block, block), jnp.float32)
    return pl.pallas_call(
        functools.partial(adam_kernel, spans, slots, columns),
        out_shape=(tile, tile, tile),
        in_specs=[smem()] + [vmem()] * (spans + 3),
        out_specs=(vmem(), vmem(), vmem()),
        scratch_shapes=[pltpu.VMEM((spans, block, block), jnp.bfloat16)],
        compiler_params=params(),
        cost_estimate=cost(slots * block * block),
        name="adam",
    )(table, *grads, *[state[0, 0] for state in states])


def take_from(array, axis, places):
    size = lax.axis_size(axis)
    return lax.ppermute(array, axis, [((i + places) % size, i) for i in range(size)])


def take_chunk(own, place):
    tensors, cores = lax.axis_size("tensor"), lax.axis_size("dp")
    t_place, d_place = divmod(place, cores)
    pairs = []
    for t in range(tensors):
        for d in range(cores):
            source = (t + t_place) % tensors * cores + (d + d_place) % cores
            pairs.append((source, t * cores + d))
    return lax.ppermute(own, ("tensor", "dp"), pairs)


def exchange(pieces):
    return [pieces[0]] + [take_from(pieces[s], "seq", -s) for s in range(1, len(pieces))]


def per_device(
    hidden_in, cotangent, down_weight, tile_ids, tile_live, values, moment_one, moment_two
):
    spans, cores = lax.axis_size("seq"), lax.axis_size("dp")
    slots, block = values.shape[2], values.shape[3]
    f_width, d_width = down_weight.shape
    d_blocks, f_blocks = d_width // block, f_width // block
    chunk = hidden_in.shape[0]
    sizes = (spans, slots, block)
    group = max(size for size in range(1, 5) if f_blocks % size == 0)
    width = group * block
    ends = [sum(PARTS[:part]) for part in range(len(PARTS) + 1)]
    cuts = [(f_blocks // group) * end // ends[-1] for end in ends]
    ranges = list(zip(cuts[:-1], cuts[1:]))

    local = [take_chunk(cotangent, place) for place in range(1, cores)]
    firsts = [take_from(cotangent, "tensor", t) for t in range(1, lax.axis_size("tensor"))]

    meta = jnp.concatenate([tile_ids[0], tile_live[0]], axis=1)
    metas = exchange([meta] * spans)
    values_half, hidden_here, local_rows = pl.pallas_call(
        early_kernel,
        out_shape=[
            jax.ShapeDtypeStruct((slots, block, block), jnp.bfloat16),
            jax.ShapeDtypeStruct(hidden_in.shape, hidden_in.dtype),
            jax.ShapeDtypeStruct((cores * chunk, d_width), cotangent.dtype),
        ],
        in_specs=[hbm()] * 3 + [vmem()] * (cores - 1),
        out_specs=[vmem()] * 3,
        scratch_shapes=[
            pltpu.VMEM((slots, block, block), jnp.float32),
            pltpu.SemaphoreType.DMA((3,)),
        ],
        compiler_params=params(),
        cost_estimate=cost(hidden_in.size),
        name="early",
    )(stay(values[0, 0]), stay(hidden_in), stay(cotangent), *local)
    table, *picked = pl.pallas_call(
        functools.partial(pick_kernel, *sizes, d_blocks),
        out_shape=[jax.ShapeDtypeStruct((spans, 3 * slots), jnp.int32)]
        + [jax.ShapeDtypeStruct((slots + 1, chunk, block), jnp.bfloat16)] * spans,
        in_specs=[smem()] * spans + [vmem(), vmem()],
        out_specs=[smem()] + [vmem()] * spans,
        compiler_params=params(),
        cost_estimate=cost(hidden_in.size),
        name="pick",
    )(*metas, values_half, hidden_here)
    crossed = exchange(picked)

    laid = ranges[LAID - 1][1]
    first_weight = pl.pallas_call(
        lay_kernel,
        out_shape=jax.ShapeDtypeStruct((laid * width, d_width), down_weight.dtype),
        in_specs=[hbm()],
        out_specs=vmem(),
        scratch_shapes=[pltpu.SemaphoreType.DMA],
        compiler_params=params(),
        cost_estimate=cost(AHEAD * laid * width * d_width),
        name="lay",
    )(stay(down_weight))

    firsts, picked = lax.optimization_barrier((firsts, picked))
    remote = []
    for first in firsts:
        remote += [first] + [take_from(first, "dp", d) for d in range(1, cores)]
    early, rows = early_matmul_call(width, laid * width, first_weight, [local_rows, *remote])
    partials, moving, held = [], [], None
    for part, (low, high) in enumerate(ranges):
        if part < LAID:
            given = [held] if part else crossed
            partial, first, *more = delta_call(
                sizes, low * width, high * width, table, early, rows, given
            )
            held = more[0] if more else held
        else:
            moving[0] = add_call(2, partials[0], moving[0], block)[0]
            rows, moving[0] = lax.optimization_barrier((rows, moving[0]))
            partial, first = matmul_call(
                spans, low, (high - low,), width, table, down_weight, rows, held
            )
        if part == RIDE:
            grads = grad_call(sizes, table, rows, crossed)
            first = attach_call(first, grads[1:])
        partials.append(partial)
        moving.append(take_from(first, "seq", -1))

    tiles = [grads[0]]
    for t in range(2, spans):
        for part in range(len(ranges)):
            if (t, part) != (2, 0):
                moving[part], *mine = add_call(t, partials[part], moving[part], block)
                tiles += mine
            moving[part] = take_from(moving[part], "seq", -1)
    tiles.append(moving[RIDE])
    columns = partials[RIDE].shape[2]

    hidden_grad = None
    shape = jax.ShapeDtypeStruct((chunk, f_width), jnp.bfloat16)
    order = [part for part in range(len(ranges)) if part != LAST] + [LAST]
    for part in order:
        if part == LAST:
            tiles[0], hidden_grad = lax.optimization_barrier((tiles[0], hidden_grad))
            new = adam_call(sizes, columns, table, tiles, values, moment_one, moment_two)
            moving[part], new = lax.optimization_barrier((moving[part], new))
        hidden_grad = last_call(
            ranges[part][0] * width, partials[part], moving[part], hidden_grad, shape
        )
    return (hidden_grad,) + tuple(array[None, None] for array in new)


def solution(mesh):
    shards = P(("groups", "seq"), ("tensor", "dp"))
    tiles = P(("groups", "seq"), ("tensor", "dp"), None, None, None)
    lists = P(("groups", "seq"), ("tensor", "dp"), None)
    return jax.shard_map(
        per_device,
        mesh=mesh,
        in_specs=(
            shards,
            P(("groups", "tensor", "dp"), "seq"),
            P(("tensor", "dp"), "seq"),
            lists,
            lists,
            tiles,
            tiles,
            tiles,
        ),
        out_specs=(shards, tiles, tiles, tiles),
        check_vma=False,
    )
```

```python
import functools

import jax
import jax.numpy as jnp
from jax import lax
from jax.experimental import pallas as pl
from jax.experimental.pallas import tpu as pltpu
from jax.sharding import PartitionSpec as P

STEP = 100
BETA_ONE = 0.9
BETA_TWO = 0.999
RATE = 0.01
EPSILON = 1e-08
VMEM_LIMIT = 12 * 1024 * 1024
MATMUL = 4096
EARLY = 1
AHEAD = 5000
PARTS = (3, 2, 2)
RIDE = 2
LAST = 1
LAID = 2
NT = (((1,), (1,)), ((), ()))
TN = (((0,), (0,)), ((), ()))


def vmem():
    return pl.BlockSpec(memory_space=pltpu.VMEM)


def smem():
    return pl.BlockSpec(memory_space=pltpu.SMEM)


def hbm():
    return pl.BlockSpec(memory_space=pltpu.HBM)


def stay(array):
    return pltpu.with_memory_space_constraint(array, pltpu.HBM)


def cost(count):
    return pl.CostEstimate(flops=count, bytes_accessed=2 * count, transcendentals=0)


def params():
    return pltpu.CompilerParams(vmem_limit_bytes=VMEM_LIMIT)


def wrap(index, size):
    return lax.rem(index + size, size)


def live_count(table, row, slots):
    count = table[row, 2 * slots]
    for slot in range(1, slots):
        count = count + table[row, 2 * slots + slot]
    return count


def rank_before(table, row, spans, slots):
    me = lax.axis_index("seq")
    before = jnp.int32(0)
    for other in range(spans):
        ahead = wrap(me - other, spans) < wrap(me - row, spans)
        before = before + jnp.where(ahead, live_count(table, other, slots), 0)
    return before


def early_kernel(values, hidden, own, *refs):
    others, (values_half, hidden_here, rows, stored, sems) = refs[:-5], refs[-5:]
    chunk = own.shape[0]
    copies = [
        pltpu.make_async_copy(values, stored, sems.at[0]),
        pltpu.make_async_copy(hidden, hidden_here, sems.at[1]),
        pltpu.make_async_copy(own, rows.at[pl.ds(0, chunk)], sems.at[2]),
    ]
    for copy in copies:
        copy.start()
    for p, other in enumerate(others):
        rows[(p + 1) * chunk : (p + 2) * chunk] = other[...]
    copies[0].wait()
    values_half[...] = stored[...].astype(values_half.dtype)
    copies[1].wait()
    copies[2].wait()


def pick_kernel(spans, slots, block, d_blocks, *refs):
    metas, (values, hidden, table), outs = refs[:spans], refs[spans : spans + 3], refs[spans + 3 :]
    me = lax.axis_index("seq")
    for s in range(spans):
        for j in range(slots):
            table[s, j] = lax.div(metas[s][0, j], d_blocks)
            table[s, slots + j] = lax.rem(metas[s][0, j], d_blocks)
            table[s, 2 * slots + j] = metas[s][0, slots + j]
    for s in range(spans):
        row = (spans - s) % spans
        before = rank_before(table, row, spans, slots)
        slot = wrap(me - lax.rem(before, spans), spans)
        tile = values[jnp.minimum(lax.div(before + slot, spans), slots - 1)]
        live = slot < live_count(table, row, slots)
        outs[s][slots] = jnp.where(live, tile.astype(jnp.float32), 0.0).astype(tile.dtype)
        for j in range(slots):
            start = pl.multiple_of(table[row, j] * block, block)
            outs[s][j] = hidden[:, pl.ds(start, block)]


def lay_kernel(weight, first_weight, sem):
    copy = pltpu.make_async_copy(weight.at[pl.ds(0, first_weight.shape[0])], first_weight, sem)
    copy.start()
    copy.wait()


def chunk_at(place):
    tensors, cores = lax.axis_size("tensor"), lax.axis_size("dp")
    t_place = lax.rem(lax.axis_index("tensor") + place // cores, tensors)
    d_place = lax.rem(lax.axis_index("dp") + place % cores, cores)
    return t_place * cores + d_place


def early_matmul_kernel(width, weight, *refs):
    pieces, (out, rows) = refs[:-2], refs[-2:]
    step = pl.program_id(0)

    @pl.when(step == 0)
    def _():
        at = 0
        for piece in pieces:
            rows[at : at + piece.shape[0]] = piece[...]
            at += piece.shape[0]

    here = pl.ds(pl.multiple_of(step * width, width), width)
    out[:, here] = lax.dot_general(
        rows[...], weight[here], NT, preferred_element_type=jnp.float32
    )


def early_matmul_call(width, columns, weight, pieces):
    tokens, d_width = sum(piece.shape[0] for piece in pieces), weight.shape[1]
    return pl.pallas_call(
        functools.partial(early_matmul_kernel, width),
        grid=(columns // width,),
        out_shape=[
            jax.ShapeDtypeStruct((tokens, columns), jnp.float32),
            jax.ShapeDtypeStruct((tokens, d_width), weight.dtype),
        ],
        in_specs=[vmem()] * (1 + len(pieces)),
        out_specs=[vmem()] * 2,
        compiler_params=params(),
        cost_estimate=cost(EARLY * tokens * columns),
        name="partial",
    )(weight, *pieces)


def add_delta(table, rows, held, total, low):
    slots, block, _ = held.shape
    count = live_count(table, 0, slots)
    for j in range(slots):
        f_start = table[0, j] * block - low

        @pl.when((j < count) & (f_start >= 0) & (f_start < total.shape[1]))
        def _():
            d_start = pl.multiple_of(table[0, slots + j] * block, block)
            place = pl.ds(pl.multiple_of(f_start, block), block)
            total[:, place] += lax.dot_general(
                rows[:, pl.ds(d_start, block)], held[j], NT, preferred_element_type=jnp.float32
            )


def put_chunks(total, out, first, here):
    spans, chunk = out.shape[:2]
    me = lax.axis_index("seq")
    for p in range(spans):
        result = total[p * chunk : (p + 1) * chunk].astype(out.dtype)
        out[chunk_at(p), :, here] = result

        @pl.when(chunk_at(p) == wrap(me - 1, spans))
        def _():
            first[:, here] = result


def held_kernel(spans, slots, block, table, *refs):
    stored, held = refs[:-1], refs[-1]
    me = lax.axis_index("seq")
    before = rank_before(table, 0, spans, slots)
    for j in range(slots):
        for s in range(spans):

            @pl.when(lax.rem(before + j, spans) == wrap(me - s, spans))
            def _():
                held[j] = stored[s][slots]


def delta_kernel(sizes, low, stores, table, early, rows, *refs):
    given, (out, first, *more, total) = refs[:stores], refs[stores:]
    if stores > 1:
        (held,) = more
        held_kernel(*sizes, table, *given, held)
    else:
        (held,) = given
    total[...] = early[:, low : low + total.shape[1]]
    add_delta(table, rows, held, total, low)
    put_chunks(total, out, first, pl.ds(0, total.shape[1]))


def delta_call(sizes, low, high, table, early, rows, given):
    spans, slots, block = sizes
    tokens, columns = early.shape[0], high - low
    shapes = [
        jax.ShapeDtypeStruct((spans, tokens // spans, columns), rows.dtype),
        jax.ShapeDtypeStruct((tokens // spans, columns), rows.dtype),
    ]
    if len(given) > 1:
        shapes.append(jax.ShapeDtypeStruct((slots, block, block), rows.dtype))
    return pl.pallas_call(
        functools.partial(delta_kernel, sizes, low, len(given)),
        out_shape=shapes,
        in_specs=[smem()] + [vmem()] * (2 + len(given)),
        out_specs=[vmem()] * len(shapes),
        scratch_shapes=[pltpu.VMEM((tokens, columns), jnp.float32)],
        compiler_params=params(),
        cost_estimate=cost(early.size),
        name="delta",
    )(table, early, rows, *given)


def matmul_kernel(low, ends, table, weight, rows, held, *refs):
    outs, total = refs[:-1], refs[-1]
    step, width = pl.program_id(0), total.shape[1]
    total[...] = lax.dot_general(rows[...], weight[...], NT, preferred_element_type=jnp.float32)
    add_delta(table, rows, held, total, (low + step) * width)
    for part, (begin, end) in enumerate(zip((0, *ends), ends)):

        @pl.when((step >= begin) & (step < end))
        def _():
            here = pl.ds(pl.multiple_of((step - begin) * width, width), width)
            put_chunks(total, *outs[2 * part : 2 * part + 2], here)


def matmul_call(spans, low, ends, width, table, weight, rows, held):
    tokens, d_width = rows.shape
    weight_spec = pl.BlockSpec((width, d_width), lambda i: (i + low, 0))
    shapes = []
    for begin, end in zip((0, *ends), ends):
        columns = (end - begin) * width
        shapes.append(jax.ShapeDtypeStruct((spans, tokens // spans, columns), rows.dtype))
        shapes.append(jax.ShapeDtypeStruct((tokens // spans, columns), rows.dtype))
    return pl.pallas_call(
        functools.partial(matmul_kernel, low, ends),
        grid=(ends[-1],),
        out_shape=shapes,
        in_specs=[smem(), weight_spec, vmem(), vmem()],
        out_specs=[vmem()] * len(shapes),
        scratch_shapes=[pltpu.VMEM((tokens, width), jnp.float32)],
        compiler_params=params(),
        cost_estimate=cost(MATMUL * tokens * ends[-1] * width),
        name="partial",
    )(table, stay(weight), rows, held)


def attach_kernel(first, *refs):
    riders, out = refs[:-1], refs[-1]
    at = first.shape[1]
    out[:, :at] = first[...]
    for rider in riders:
        out[:, at : at + rider.shape[1]] = rider[...]
        at += rider.shape[1]


def attach_call(first, riders):
    chunk, columns = first.shape
    columns += sum(rider.shape[1] for rider in riders)
    return pl.pallas_call(
        attach_kernel,
        out_shape=jax.ShapeDtypeStruct((chunk, columns), first.dtype),
        in_specs=[vmem()] * (1 + len(riders)),
        out_specs=vmem(),
        compiler_params=params(),
        cost_estimate=cost(first.size),
        name="attach",
    )(first, *riders)


def add_kernel(t, riders, partials, arrived, out, *mine):
    spans, _, columns = partials.shape
    chunk = wrap(lax.axis_index("seq") - t, spans)
    result = partials[chunk].astype(jnp.float32) + arrived[:, :columns].astype(jnp.float32)
    out[:, :columns] = result.astype(out.dtype)
    if riders:
        block = mine[0].shape[1]
        mine[0][...] = arrived[:, columns : columns + block]
        out[:, columns:] = arrived[:, columns + block :]


def add_call(t, partials, arrived, block):
    chunk, columns = partials.shape[1:]
    riders = (arrived.shape[1] - columns) // block
    shapes = [jax.ShapeDtypeStruct((chunk, arrived.shape[1] - min(riders, 1) * block), arrived.dtype)]
    if riders:
        shapes.append(jax.ShapeDtypeStruct((chunk, block), arrived.dtype))
    return pl.pallas_call(
        functools.partial(add_kernel, t, riders),
        out_shape=shapes,
        in_specs=[vmem(), vmem()],
        out_specs=[vmem()] * len(shapes),
        compiler_params=params(),
        cost_estimate=cost(arrived.size),
        name="add",
    )(partials, arrived)


def last_kernel(low, partials, arrived, *refs):
    out, total, sem = refs[-3:]
    columns = total.shape[1]
    result = partials[lax.axis_index("seq")].astype(jnp.float32)
    result = result + arrived[:, :columns].astype(jnp.float32)
    total[...] = result.astype(out.dtype)
    copy = pltpu.make_async_copy(total, out.at[:, pl.ds(low, columns)], sem)
    copy.start()
    copy.wait()


def last_call(low, partials, arrived, out, shape):
    _, chunk, columns = partials.shape
    given = [] if out is None else [out]
    return pl.pallas_call(
        functools.partial(last_kernel, low),
        out_shape=shape,
        in_specs=[vmem()] * 2 + [hbm()] * len(given),
        out_specs=hbm(),
        scratch_shapes=[pltpu.VMEM((chunk, columns), shape.dtype), pltpu.SemaphoreType.DMA],
        input_output_aliases={2: 0} if given else {},
        compiler_params=params(),
        cost_estimate=cost(partials.size),
        name="last_sum",
    )(partials, arrived, *given)


def grad_kernel(spans, slots, block, table, rows, *refs):
    hidden, outs, (cols,) = refs[:spans], refs[spans : 2 * spans], refs[2 * spans :]
    me = lax.axis_index("seq")
    count, before = live_count(table, 0, slots), rank_before(table, 0, spans, slots)
    chunk = rows.shape[0] // spans
    for s in range(spans):
        cols[s] = hidden[s][:slots]
    for s in range(spans):
        slot = wrap(lax.rem(me + s, spans) - lax.rem(before, spans), spans)
        outs[s][...] = jnp.zeros_like(outs[s])

        @pl.when(slot < count)
        def _():
            d_start = pl.multiple_of(table[0, slots + slot] * block, block)
            total = jnp.zeros((block, block), jnp.float32)
            for p in range(spans):
                total = total + lax.dot_general(
                    cols[wrap(me - chunk_at(p), spans), slot],
                    rows[p * chunk : (p + 1) * chunk, pl.ds(d_start, block)],
                    TN,
                    preferred_element_type=jnp.float32,
                )
            outs[s][...] = total.astype(outs[s].dtype)


def grad_call(sizes, table, rows, hidden_cols):
    spans = sizes[0]
    slots, chunk, block = hidden_cols[0].shape
    slots -= 1
    return pl.pallas_call(
        functools.partial(grad_kernel, *sizes),
        out_shape=[jax.ShapeDtypeStruct((block, block), jnp.bfloat16)] * spans,
        in_specs=[smem()] + [vmem()] * (spans + 1),
        out_specs=[vmem()] * spans,
        scratch_shapes=[pltpu.VMEM((spans, slots, chunk, block), jnp.bfloat16)],
        compiler_params=params(),
        cost_estimate=cost(rows.size),
        name="tile_grad",
    )(table, rows, *hidden_cols)


def adam_kernel(spans, slots, columns, table, *refs):
    arrived, refs = refs[:spans], refs[spans:]
    values, one, two, values_new, one_new, two_new, grads = refs
    me = lax.axis_index("seq")
    for s in range(spans - 1):
        grads[s] = arrived[s][...]
    grads[spans - 1] = arrived[-1][:, columns:]
    befores = [rank_before(table, s, spans, slots) for s in range(spans)]
    counts = [live_count(table, s, slots) for s in range(spans)]
    for owned in range(slots):
        rank = owned * spans + me
        source, live = jnp.int32(0), jnp.int32(0)
        for s in range(spans):
            holds = (befores[s] <= rank) & (rank < befores[s] + counts[s])
            source, live = jnp.where(holds, s, source), jnp.where(holds, 1, live)
        grad = grads[source].astype(jnp.float32)
        stored, old_one, old_two = values[owned], one[owned], two[owned]
        new_one = BETA_ONE * old_one + (1.0 - BETA_ONE) * grad
        new_two = BETA_TWO * old_two + (1.0 - BETA_TWO) * grad * grad
        stepped = (
            new_one
            / (1.0 - BETA_ONE**STEP)
            / (jnp.sqrt(new_two / (1.0 - BETA_TWO**STEP)) + EPSILON)
        )
        values_new[owned] = jnp.where(live > 0, stored - RATE * stepped, stored)
        one_new[owned] = jnp.where(live > 0, new_one, old_one)
        two_new[owned] = jnp.where(live > 0, new_two, old_two)


def adam_call(sizes, columns, table, grads, *states):
    spans, slots, block = sizes
    tile = jax.ShapeDtypeStruct((slots, block, block), jnp.float32)
    return pl.pallas_call(
        functools.partial(adam_kernel, spans, slots, columns),
        out_shape=(tile, tile, tile),
        in_specs=[smem()] + [vmem()] * (spans + 3),
        out_specs=(vmem(), vmem(), vmem()),
        scratch_shapes=[pltpu.VMEM((spans, block, block), jnp.bfloat16)],
        compiler_params=params(),
        cost_estimate=cost(slots * block * block),
        name="adam",
    )(table, *grads, *[state[0, 0] for state in states])


def take_from(array, axis, places):
    size = lax.axis_size(axis)
    return lax.ppermute(array, axis, [((i + places) % size, i) for i in range(size)])


def take_chunk(own, place):
    tensors, cores = lax.axis_size("tensor"), lax.axis_size("dp")
    t_place, d_place = divmod(place, cores)
    pairs = []
    for t in range(tensors):
        for d in range(cores):
            source = (t + t_place) % tensors * cores + (d + d_place) % cores
            pairs.append((source, t * cores + d))
    return lax.ppermute(own, ("tensor", "dp"), pairs)


def exchange(pieces):
    return [pieces[0]] + [take_from(pieces[s], "seq", -s) for s in range(1, len(pieces))]


def per_device(
    hidden_in, cotangent, down_weight, tile_ids, tile_live, values, moment_one, moment_two
):
    spans, cores = lax.axis_size("seq"), lax.axis_size("dp")
    slots, block = values.shape[2], values.shape[3]
    f_width, d_width = down_weight.shape
    d_blocks, f_blocks = d_width // block, f_width // block
    chunk = hidden_in.shape[0]
    sizes = (spans, slots, block)
    group = max(size for size in range(1, 5) if f_blocks % size == 0)
    width = group * block
    ends = [sum(PARTS[:part]) for part in range(len(PARTS) + 1)]
    cuts = [(f_blocks // group) * end // ends[-1] for end in ends]
    ranges = list(zip(cuts[:-1], cuts[1:]))

    local = [take_chunk(cotangent, place) for place in range(1, cores)]
    firsts = [take_from(cotangent, "tensor", t) for t in range(1, lax.axis_size("tensor"))]

    meta = jnp.concatenate([tile_ids[0], tile_live[0]], axis=1)
    metas = exchange([meta] * spans)
    values_half, hidden_here, local_rows = pl.pallas_call(
        early_kernel,
        out_shape=[
            jax.ShapeDtypeStruct((slots, block, block), jnp.bfloat16),
            jax.ShapeDtypeStruct(hidden_in.shape, hidden_in.dtype),
            jax.ShapeDtypeStruct((cores * chunk, d_width), cotangent.dtype),
        ],
        in_specs=[hbm()] * 3 + [vmem()] * (cores - 1),
        out_specs=[vmem()] * 3,
        scratch_shapes=[
            pltpu.VMEM((slots, block, block), jnp.float32),
            pltpu.SemaphoreType.DMA((3,)),
        ],
        compiler_params=params(),
        cost_estimate=cost(hidden_in.size),
        name="early",
    )(stay(values[0, 0]), stay(hidden_in), stay(cotangent), *local)
    table, *picked = pl.pallas_call(
        functools.partial(pick_kernel, *sizes, d_blocks),
        out_shape=[jax.ShapeDtypeStruct((spans, 3 * slots), jnp.int32)]
        + [jax.ShapeDtypeStruct((slots + 1, chunk, block), jnp.bfloat16)] * spans,
        in_specs=[smem()] * spans + [vmem(), vmem()],
        out_specs=[smem()] + [vmem()] * spans,
        compiler_params=params(),
        cost_estimate=cost(hidden_in.size),
        name="pick",
    )(*metas, values_half, hidden_here)
    crossed = exchange(picked)

    laid = ranges[LAID - 1][1]
    first_weight = pl.pallas_call(
        lay_kernel,
        out_shape=jax.ShapeDtypeStruct((laid * width, d_width), down_weight.dtype),
        in_specs=[hbm()],
        out_specs=vmem(),
        scratch_shapes=[pltpu.SemaphoreType.DMA],
        compiler_params=params(),
        cost_estimate=cost(AHEAD * laid * width * d_width),
        name="lay",
    )(stay(down_weight))

    firsts, picked = lax.optimization_barrier((firsts, picked))
    remote = []
    for first in firsts:
        remote += [first] + [take_from(first, "dp", d) for d in range(1, cores)]
    early, rows = early_matmul_call(width, laid * width, first_weight, [local_rows, *remote])
    partials, moving, held = [], [], None
    for part, (low, high) in enumerate(ranges):
        if part < LAID:
            given = [held] if part else crossed
            partial, first, *more = delta_call(
                sizes, low * width, high * width, table, early, rows, given
            )
            held = more[0] if more else held
        else:
            partial, first = matmul_call(
                spans, low, (high - low,), width, table, down_weight, rows, held
            )
        if part == RIDE:
            grads = grad_call(sizes, table, rows, crossed)
            first = attach_call(first, grads[1:])
        partials.append(partial)
        moving.append(take_from(first, "seq", -1))

    tiles = [grads[0]]
    for t in range(2, spans):
        for part in range(len(ranges)):
            moving[part], *mine = add_call(t, partials[part], moving[part], block)
            tiles += mine
            moving[part] = take_from(moving[part], "seq", -1)
    tiles.append(moving[RIDE])
    columns = partials[RIDE].shape[2]

    hidden_grad = None
    shape = jax.ShapeDtypeStruct((chunk, f_width), jnp.bfloat16)
    order = [part for part in range(len(ranges)) if part != LAST] + [LAST]
    for part in order:
        if part == LAST:
            tiles[0], hidden_grad = lax.optimization_barrier((tiles[0], hidden_grad))
            new = adam_call(sizes, columns, table, tiles, values, moment_one, moment_two)
            moving[part], new = lax.optimization_barrier((moving[part], new))
        hidden_grad = last_call(
            ranges[part][0] * width, partials[part], moving[part], hidden_grad, shape
        )
    return (hidden_grad,) + tuple(array[None, None] for array in new)


def solution(mesh):
    shards = P(("groups", "seq"), ("tensor", "dp"))
    tiles = P(("groups", "seq"), ("tensor", "dp"), None, None, None)
    lists = P(("groups", "seq"), ("tensor", "dp"), None)
    return jax.shard_map(
        per_device,
        mesh=mesh,
        in_specs=(
            shards,
            P(("groups", "tensor", "dp"), "seq"),
            P(("tensor", "dp"), "seq"),
            lists,
            lists,
            tiles,
            tiles,
            tiles,
        ),
        out_specs=(shards, tiles, tiles, tiles),
        check_vma=False,
    )
```

```python
import functools

import jax
import jax.numpy as jnp
from jax import lax
from jax.experimental import pallas as pl
from jax.experimental.pallas import tpu as pltpu
from jax.sharding import PartitionSpec as P

STEP = 100
BETA_ONE = 0.9
BETA_TWO = 0.999
RATE = 0.01
EPSILON = 1e-08
VMEM_LIMIT = 12 * 1024 * 1024
MATMUL = 4096
EARLY = 1
AHEAD = 5000
PARTS = (3, 2, 2)
RIDE = 2
LAST = 1
LAID = 1
NT = (((1,), (1,)), ((), ()))
TN = (((0,), (0,)), ((), ()))


def vmem():
    return pl.BlockSpec(memory_space=pltpu.VMEM)


def smem():
    return pl.BlockSpec(memory_space=pltpu.SMEM)


def hbm():
    return pl.BlockSpec(memory_space=pltpu.HBM)


def stay(array):
    return pltpu.with_memory_space_constraint(array, pltpu.HBM)


def cost(count):
    return pl.CostEstimate(flops=count, bytes_accessed=2 * count, transcendentals=0)


def params():
    return pltpu.CompilerParams(vmem_limit_bytes=VMEM_LIMIT)


def wrap(index, size):
    return lax.rem(index + size, size)


def live_count(table, row, slots):
    count = table[row, 2 * slots]
    for slot in range(1, slots):
        count = count + table[row, 2 * slots + slot]
    return count


def rank_before(table, row, spans, slots):
    me = lax.axis_index("seq")
    before = jnp.int32(0)
    for other in range(spans):
        ahead = wrap(me - other, spans) < wrap(me - row, spans)
        before = before + jnp.where(ahead, live_count(table, other, slots), 0)
    return before


def early_kernel(values, hidden, own, *refs):
    others, (values_half, hidden_here, rows, stored, sems) = refs[:-5], refs[-5:]
    chunk = own.shape[0]
    copies = [
        pltpu.make_async_copy(values, stored, sems.at[0]),
        pltpu.make_async_copy(hidden, hidden_here, sems.at[1]),
        pltpu.make_async_copy(own, rows.at[pl.ds(0, chunk)], sems.at[2]),
    ]
    for copy in copies:
        copy.start()
    for p, other in enumerate(others):
        rows[(p + 1) * chunk : (p + 2) * chunk] = other[...]
    copies[0].wait()
    values_half[...] = stored[...].astype(values_half.dtype)
    copies[1].wait()
    copies[2].wait()


def pick_kernel(spans, slots, block, d_blocks, *refs):
    metas, (values, hidden, table), outs = refs[:spans], refs[spans : spans + 3], refs[spans + 3 :]
    me = lax.axis_index("seq")
    for s in range(spans):
        for j in range(slots):
            table[s, j] = lax.div(metas[s][0, j], d_blocks)
            table[s, slots + j] = lax.rem(metas[s][0, j], d_blocks)
            table[s, 2 * slots + j] = metas[s][0, slots + j]
    for s in range(spans):
        row = (spans - s) % spans
        before = rank_before(table, row, spans, slots)
        slot = wrap(me - lax.rem(before, spans), spans)
        tile = values[jnp.minimum(lax.div(before + slot, spans), slots - 1)]
        live = slot < live_count(table, row, slots)
        outs[s][slots] = jnp.where(live, tile.astype(jnp.float32), 0.0).astype(tile.dtype)
        for j in range(slots):
            start = pl.multiple_of(table[row, j] * block, block)
            outs[s][j] = hidden[:, pl.ds(start, block)]


def lay_kernel(weight, first_weight, sem):
    copy = pltpu.make_async_copy(weight.at[pl.ds(0, first_weight.shape[0])], first_weight, sem)
    copy.start()
    copy.wait()


def chunk_at(place):
    tensors, cores = lax.axis_size("tensor"), lax.axis_size("dp")
    t_place = lax.rem(lax.axis_index("tensor") + place // cores, tensors)
    d_place = lax.rem(lax.axis_index("dp") + place % cores, cores)
    return t_place * cores + d_place


def early_matmul_kernel(width, weight, *refs):
    pieces, (out, rows) = refs[:-2], refs[-2:]
    step = pl.program_id(0)

    @pl.when(step == 0)
    def _():
        at = 0
        for piece in pieces:
            rows[at : at + piece.shape[0]] = piece[...]
            at += piece.shape[0]

    here = pl.ds(pl.multiple_of(step * width, width), width)
    out[:, here] = lax.dot_general(
        rows[...], weight[here], NT, preferred_element_type=jnp.float32
    )


def early_matmul_call(width, columns, weight, pieces):
    tokens, d_width = sum(piece.shape[0] for piece in pieces), weight.shape[1]
    return pl.pallas_call(
        functools.partial(early_matmul_kernel, width),
        grid=(columns // width,),
        out_shape=[
            jax.ShapeDtypeStruct((tokens, columns), jnp.float32),
            jax.ShapeDtypeStruct((tokens, d_width), weight.dtype),
        ],
        in_specs=[vmem()] * (1 + len(pieces)),
        out_specs=[vmem()] * 2,
        compiler_params=params(),
        cost_estimate=cost(EARLY * tokens * columns),
        name="partial",
    )(weight, *pieces)


def add_delta(table, rows, held, total, low):
    slots, block, _ = held.shape
    count = live_count(table, 0, slots)
    for j in range(slots):
        f_start = table[0, j] * block - low

        @pl.when((j < count) & (f_start >= 0) & (f_start < total.shape[1]))
        def _():
            d_start = pl.multiple_of(table[0, slots + j] * block, block)
            place = pl.ds(pl.multiple_of(f_start, block), block)
            total[:, place] += lax.dot_general(
                rows[:, pl.ds(d_start, block)], held[j], NT, preferred_element_type=jnp.float32
            )


def put_chunks(total, out, first, here):
    spans, chunk = out.shape[:2]
    me = lax.axis_index("seq")
    for p in range(spans):
        result = total[p * chunk : (p + 1) * chunk].astype(out.dtype)
        out[chunk_at(p), :, here] = result

        @pl.when(chunk_at(p) == wrap(me - 1, spans))
        def _():
            first[:, here] = result


def held_kernel(spans, slots, block, table, *refs):
    stored, held = refs[:-1], refs[-1]
    me = lax.axis_index("seq")
    before = rank_before(table, 0, spans, slots)
    for j in range(slots):
        for s in range(spans):

            @pl.when(lax.rem(before + j, spans) == wrap(me - s, spans))
            def _():
                held[j] = stored[s][slots]


def delta_kernel(sizes, low, stores, table, early, rows, *refs):
    given, (out, first, *more, total) = refs[:stores], refs[stores:]
    if stores > 1:
        (held,) = more
        held_kernel(*sizes, table, *given, held)
    else:
        (held,) = given
    total[...] = early[:, low : low + total.shape[1]]
    add_delta(table, rows, held, total, low)
    put_chunks(total, out, first, pl.ds(0, total.shape[1]))


def delta_call(sizes, low, high, table, early, rows, given):
    spans, slots, block = sizes
    tokens, columns = early.shape[0], high - low
    shapes = [
        jax.ShapeDtypeStruct((spans, tokens // spans, columns), rows.dtype),
        jax.ShapeDtypeStruct((tokens // spans, columns), rows.dtype),
    ]
    if len(given) > 1:
        shapes.append(jax.ShapeDtypeStruct((slots, block, block), rows.dtype))
    return pl.pallas_call(
        functools.partial(delta_kernel, sizes, low, len(given)),
        out_shape=shapes,
        in_specs=[smem()] + [vmem()] * (2 + len(given)),
        out_specs=[vmem()] * len(shapes),
        scratch_shapes=[pltpu.VMEM((tokens, columns), jnp.float32)],
        compiler_params=params(),
        cost_estimate=cost(early.size),
        name="delta",
    )(table, early, rows, *given)


def matmul_kernel(low, ends, table, weight, rows, held, *refs):
    outs, total = refs[:-1], refs[-1]
    step, width = pl.program_id(0), total.shape[1]
    total[...] = lax.dot_general(rows[...], weight[...], NT, preferred_element_type=jnp.float32)
    add_delta(table, rows, held, total, (low + step) * width)
    for part, (begin, end) in enumerate(zip((0, *ends), ends)):

        @pl.when((step >= begin) & (step < end))
        def _():
            here = pl.ds(pl.multiple_of((step - begin) * width, width), width)
            put_chunks(total, *outs[2 * part : 2 * part + 2], here)


def matmul_call(spans, low, ends, width, table, weight, rows, held):
    tokens, d_width = rows.shape
    weight_spec = pl.BlockSpec((width, d_width), lambda i: (i + low, 0))
    shapes = []
    for begin, end in zip((0, *ends), ends):
        columns = (end - begin) * width
        shapes.append(jax.ShapeDtypeStruct((spans, tokens // spans, columns), rows.dtype))
        shapes.append(jax.ShapeDtypeStruct((tokens // spans, columns), rows.dtype))
    return pl.pallas_call(
        functools.partial(matmul_kernel, low, ends),
        grid=(ends[-1],),
        out_shape=shapes,
        in_specs=[smem(), weight_spec, vmem(), vmem()],
        out_specs=[vmem()] * len(shapes),
        scratch_shapes=[pltpu.VMEM((tokens, width), jnp.float32)],
        compiler_params=params(),
        cost_estimate=cost(MATMUL * tokens * ends[-1] * width),
        name="partial",
    )(table, stay(weight), rows, held)


def attach_kernel(first, *refs):
    riders, out = refs[:-1], refs[-1]
    at = first.shape[1]
    out[:, :at] = first[...]
    for rider in riders:
        out[:, at : at + rider.shape[1]] = rider[...]
        at += rider.shape[1]


def attach_call(first, riders):
    chunk, columns = first.shape
    columns += sum(rider.shape[1] for rider in riders)
    return pl.pallas_call(
        attach_kernel,
        out_shape=jax.ShapeDtypeStruct((chunk, columns), first.dtype),
        in_specs=[vmem()] * (1 + len(riders)),
        out_specs=vmem(),
        compiler_params=params(),
        cost_estimate=cost(first.size),
        name="attach",
    )(first, *riders)


def add_kernel(t, riders, partials, arrived, out, *mine):
    spans, _, columns = partials.shape
    chunk = wrap(lax.axis_index("seq") - t, spans)
    result = partials[chunk].astype(jnp.float32) + arrived[:, :columns].astype(jnp.float32)
    out[:, :columns] = result.astype(out.dtype)
    if riders:
        block = mine[0].shape[1]
        mine[0][...] = arrived[:, columns : columns + block]
        out[:, columns:] = arrived[:, columns + block :]


def add_call(t, partials, arrived, block):
    chunk, columns = partials.shape[1:]
    riders = (arrived.shape[1] - columns) // block
    shapes = [jax.ShapeDtypeStruct((chunk, arrived.shape[1] - min(riders, 1) * block), arrived.dtype)]
    if riders:
        shapes.append(jax.ShapeDtypeStruct((chunk, block), arrived.dtype))
    return pl.pallas_call(
        functools.partial(add_kernel, t, riders),
        out_shape=shapes,
        in_specs=[vmem(), vmem()],
        out_specs=[vmem()] * len(shapes),
        compiler_params=params(),
        cost_estimate=cost(arrived.size),
        name="add",
    )(partials, arrived)


def last_kernel(low, partials, arrived, *refs):
    out, total, sem = refs[-3:]
    columns = total.shape[1]
    result = partials[lax.axis_index("seq")].astype(jnp.float32)
    result = result + arrived[:, :columns].astype(jnp.float32)
    total[...] = result.astype(out.dtype)
    copy = pltpu.make_async_copy(total, out.at[:, pl.ds(low, columns)], sem)
    copy.start()
    copy.wait()


def last_call(low, partials, arrived, out, shape):
    _, chunk, columns = partials.shape
    given = [] if out is None else [out]
    return pl.pallas_call(
        functools.partial(last_kernel, low),
        out_shape=shape,
        in_specs=[vmem()] * 2 + [hbm()] * len(given),
        out_specs=hbm(),
        scratch_shapes=[pltpu.VMEM((chunk, columns), shape.dtype), pltpu.SemaphoreType.DMA],
        input_output_aliases={2: 0} if given else {},
        compiler_params=params(),
        cost_estimate=cost(partials.size),
        name="last_sum",
    )(partials, arrived, *given)


def grad_kernel(spans, slots, block, table, rows, *refs):
    hidden, outs, (cols,) = refs[:spans], refs[spans : 2 * spans], refs[2 * spans :]
    me = lax.axis_index("seq")
    count, before = live_count(table, 0, slots), rank_before(table, 0, spans, slots)
    chunk = rows.shape[0] // spans
    for s in range(spans):
        cols[s] = hidden[s][:slots]
    for s in range(spans):
        slot = wrap(lax.rem(me + s, spans) - lax.rem(before, spans), spans)
        outs[s][...] = jnp.zeros_like(outs[s])

        @pl.when(slot < count)
        def _():
            d_start = pl.multiple_of(table[0, slots + slot] * block, block)
            total = jnp.zeros((block, block), jnp.float32)
            for p in range(spans):
                total = total + lax.dot_general(
                    cols[wrap(me - chunk_at(p), spans), slot],
                    rows[p * chunk : (p + 1) * chunk, pl.ds(d_start, block)],
                    TN,
                    preferred_element_type=jnp.float32,
                )
            outs[s][...] = total.astype(outs[s].dtype)


def grad_call(sizes, table, rows, hidden_cols):
    spans = sizes[0]
    slots, chunk, block = hidden_cols[0].shape
    slots -= 1
    return pl.pallas_call(
        functools.partial(grad_kernel, *sizes),
        out_shape=[jax.ShapeDtypeStruct((block, block), jnp.bfloat16)] * spans,
        in_specs=[smem()] + [vmem()] * (spans + 1),
        out_specs=[vmem()] * spans,
        scratch_shapes=[pltpu.VMEM((spans, slots, chunk, block), jnp.bfloat16)],
        compiler_params=params(),
        cost_estimate=cost(rows.size),
        name="tile_grad",
    )(table, rows, *hidden_cols)


def adam_kernel(spans, slots, columns, table, *refs):
    arrived, refs = refs[:spans], refs[spans:]
    values, one, two, values_new, one_new, two_new, grads = refs
    me = lax.axis_index("seq")
    for s in range(spans - 1):
        grads[s] = arrived[s][...]
    grads[spans - 1] = arrived[-1][:, columns:]
    befores = [rank_before(table, s, spans, slots) for s in range(spans)]
    counts = [live_count(table, s, slots) for s in range(spans)]
    for owned in range(slots):
        rank = owned * spans + me
        source, live = jnp.int32(0), jnp.int32(0)
        for s in range(spans):
            holds = (befores[s] <= rank) & (rank < befores[s] + counts[s])
            source, live = jnp.where(holds, s, source), jnp.where(holds, 1, live)
        grad = grads[source].astype(jnp.float32)
        stored, old_one, old_two = values[owned], one[owned], two[owned]
        new_one = BETA_ONE * old_one + (1.0 - BETA_ONE) * grad
        new_two = BETA_TWO * old_two + (1.0 - BETA_TWO) * grad * grad
        stepped = (
            new_one
            / (1.0 - BETA_ONE**STEP)
            / (jnp.sqrt(new_two / (1.0 - BETA_TWO**STEP)) + EPSILON)
        )
        values_new[owned] = jnp.where(live > 0, stored - RATE * stepped, stored)
        one_new[owned] = jnp.where(live > 0, new_one, old_one)
        two_new[owned] = jnp.where(live > 0, new_two, old_two)


def adam_call(sizes, columns, table, grads, *states):
    spans, slots, block = sizes
    tile = jax.ShapeDtypeStruct((slots, block, block), jnp.float32)
    return pl.pallas_call(
        functools.partial(adam_kernel, spans, slots, columns),
        out_shape=(tile, tile, tile),
        in_specs=[smem()] + [vmem()] * (spans + 3),
        out_specs=(vmem(), vmem(), vmem()),
        scratch_shapes=[pltpu.VMEM((spans, block, block), jnp.bfloat16)],
        compiler_params=params(),
        cost_estimate=cost(slots * block * block),
        name="adam",
    )(table, *grads, *[state[0, 0] for state in states])


def take_from(array, axis, places):
    size = lax.axis_size(axis)
    return lax.ppermute(array, axis, [((i + places) % size, i) for i in range(size)])


def take_chunk(own, place):
    tensors, cores = lax.axis_size("tensor"), lax.axis_size("dp")
    t_place, d_place = divmod(place, cores)
    pairs = []
    for t in range(tensors):
        for d in range(cores):
            source = (t + t_place) % tensors * cores + (d + d_place) % cores
            pairs.append((source, t * cores + d))
    return lax.ppermute(own, ("tensor", "dp"), pairs)


def exchange(pieces):
    return [pieces[0]] + [take_from(pieces[s], "seq", -s) for s in range(1, len(pieces))]


def per_device(
    hidden_in, cotangent, down_weight, tile_ids, tile_live, values, moment_one, moment_two
):
    spans, cores = lax.axis_size("seq"), lax.axis_size("dp")
    slots, block = values.shape[2], values.shape[3]
    f_width, d_width = down_weight.shape
    d_blocks, f_blocks = d_width // block, f_width // block
    chunk = hidden_in.shape[0]
    sizes = (spans, slots, block)
    group = max(size for size in range(1, 5) if f_blocks % size == 0)
    width = group * block
    ends = [sum(PARTS[:part]) for part in range(len(PARTS) + 1)]
    cuts = [(f_blocks // group) * end // ends[-1] for end in ends]
    ranges = list(zip(cuts[:-1], cuts[1:]))

    local = [take_chunk(cotangent, place) for place in range(1, cores)]
    firsts = [take_from(cotangent, "tensor", t) for t in range(1, lax.axis_size("tensor"))]

    meta = jnp.concatenate([tile_ids[0], tile_live[0]], axis=1)
    metas = exchange([meta] * spans)
    values_half, hidden_here, local_rows = pl.pallas_call(
        early_kernel,
        out_shape=[
            jax.ShapeDtypeStruct((slots, block, block), jnp.bfloat16),
            jax.ShapeDtypeStruct(hidden_in.shape, hidden_in.dtype),
            jax.ShapeDtypeStruct((cores * chunk, d_width), cotangent.dtype),
        ],
        in_specs=[hbm()] * 3 + [vmem()] * (cores - 1),
        out_specs=[vmem()] * 3,
        scratch_shapes=[
            pltpu.VMEM((slots, block, block), jnp.float32),
            pltpu.SemaphoreType.DMA((3,)),
        ],
        compiler_params=params(),
        cost_estimate=cost(hidden_in.size),
        name="early",
    )(stay(values[0, 0]), stay(hidden_in), stay(cotangent), *local)
    table, *picked = pl.pallas_call(
        functools.partial(pick_kernel, *sizes, d_blocks),
        out_shape=[jax.ShapeDtypeStruct((spans, 3 * slots), jnp.int32)]
        + [jax.ShapeDtypeStruct((slots + 1, chunk, block), jnp.bfloat16)] * spans,
        in_specs=[smem()] * spans + [vmem(), vmem()],
        out_specs=[smem()] + [vmem()] * spans,
        compiler_params=params(),
        cost_estimate=cost(hidden_in.size),
        name="pick",
    )(*metas, values_half, hidden_here)
    crossed = exchange(picked)

    laid = ranges[LAID - 1][1]
    first_weight = pl.pallas_call(
        lay_kernel,
        out_shape=jax.ShapeDtypeStruct((laid * width, d_width), down_weight.dtype),
        in_specs=[hbm()],
        out_specs=vmem(),
        scratch_shapes=[pltpu.SemaphoreType.DMA],
        compiler_params=params(),
        cost_estimate=cost(AHEAD * laid * width * d_width),
        name="lay",
    )(stay(down_weight))

    firsts, picked = lax.optimization_barrier((firsts, picked))
    remote = []
    for first in firsts:
        remote += [first] + [take_from(first, "dp", d) for d in range(1, cores)]
    early, rows = early_matmul_call(width, laid * width, first_weight, [local_rows, *remote])
    partials, moving, held = [], [], None
    for part, (low, high) in enumerate(ranges):
        if part < LAID:
            given = [held] if part else crossed
            partial, first, *more = delta_call(
                sizes, low * width, high * width, table, early, rows, given
            )
            held = more[0] if more else held
        else:
            partial, first = matmul_call(
                spans, low, (high - low,), width, table, down_weight, rows, held
            )
        if part == RIDE:
            grads = grad_call(sizes, table, rows, crossed)
            first = attach_call(first, grads[1:])
        partials.append(partial)
        moving.append(take_from(first, "seq", -1))

    tiles = [grads[0]]
    for t in range(2, spans):
        for part in range(len(ranges)):
            moving[part], *mine = add_call(t, partials[part], moving[part], block)
            tiles += mine
            moving[part] = take_from(moving[part], "seq", -1)
    tiles.append(moving[RIDE])
    columns = partials[RIDE].shape[2]

    hidden_grad = None
    shape = jax.ShapeDtypeStruct((chunk, f_width), jnp.bfloat16)
    order = [part for part in range(len(ranges)) if part != LAST] + [LAST]
    for part in order:
        if part == LAST:
            tiles[0], hidden_grad = lax.optimization_barrier((tiles[0], hidden_grad))
            new = adam_call(sizes, columns, table, tiles, values, moment_one, moment_two)
            moving[part], new = lax.optimization_barrier((moving[part], new))
        hidden_grad = last_call(
            ranges[part][0] * width, partials[part], moving[part], hidden_grad, shape
        )
    return (hidden_grad,) + tuple(array[None, None] for array in new)


def solution(mesh):
    shards = P(("groups", "seq"), ("tensor", "dp"))
    tiles = P(("groups", "seq"), ("tensor", "dp"), None, None, None)
    lists = P(("groups", "seq"), ("tensor", "dp"), None)
    return jax.shard_map(
        per_device,
        mesh=mesh,
        in_specs=(
            shards,
            P(("groups", "tensor", "dp"), "seq"),
            P(("tensor", "dp"), "seq"),
            lists,
            lists,
            tiles,
            tiles,
            tiles,
        ),
        out_specs=(shards, tiles, tiles, tiles),
        check_vma=False,
    )
```

```python
import functools

import jax
import jax.numpy as jnp
from jax import lax
from jax.experimental import pallas as pl
from jax.experimental.pallas import tpu as pltpu
from jax.sharding import PartitionSpec as P

STEP = 100
BETA_ONE = 0.9
BETA_TWO = 0.999
RATE = 0.01
EPSILON = 1e-08
VMEM_LIMIT = 12 * 1024 * 1024
MATMUL = 4096
EARLY = 1
AHEAD = 5000
PARTS = (3, 2, 2)
RIDE = 2
LAST = 1
NT = (((1,), (1,)), ((), ()))
TN = (((0,), (0,)), ((), ()))


def vmem():
    return pl.BlockSpec(memory_space=pltpu.VMEM)


def smem():
    return pl.BlockSpec(memory_space=pltpu.SMEM)


def hbm():
    return pl.BlockSpec(memory_space=pltpu.HBM)


def stay(array):
    return pltpu.with_memory_space_constraint(array, pltpu.HBM)


def cost(count):
    return pl.CostEstimate(flops=count, bytes_accessed=2 * count, transcendentals=0)


def params():
    return pltpu.CompilerParams(vmem_limit_bytes=VMEM_LIMIT)


def wrap(index, size):
    return lax.rem(index + size, size)


def live_count(table, row, slots):
    count = table[row, 2 * slots]
    for slot in range(1, slots):
        count = count + table[row, 2 * slots + slot]
    return count


def rank_before(table, row, spans, slots):
    me = lax.axis_index("seq")
    before = jnp.int32(0)
    for other in range(spans):
        ahead = wrap(me - other, spans) < wrap(me - row, spans)
        before = before + jnp.where(ahead, live_count(table, other, slots), 0)
    return before


def early_kernel(values, hidden, own, *refs):
    others, (values_half, hidden_here, rows, stored, sems) = refs[:-5], refs[-5:]
    chunk = own.shape[0]
    copies = [
        pltpu.make_async_copy(values, stored, sems.at[0]),
        pltpu.make_async_copy(hidden, hidden_here, sems.at[1]),
        pltpu.make_async_copy(own, rows.at[pl.ds(0, chunk)], sems.at[2]),
    ]
    for copy in copies:
        copy.start()
    for p, other in enumerate(others):
        rows[(p + 1) * chunk : (p + 2) * chunk] = other[...]
    copies[0].wait()
    values_half[...] = stored[...].astype(values_half.dtype)
    copies[1].wait()
    copies[2].wait()


def pick_kernel(spans, slots, block, d_blocks, *refs):
    metas, (values, hidden, table), outs = refs[:spans], refs[spans : spans + 3], refs[spans + 3 :]
    me = lax.axis_index("seq")
    for s in range(spans):
        for j in range(slots):
            table[s, j] = lax.div(metas[s][0, j], d_blocks)
            table[s, slots + j] = lax.rem(metas[s][0, j], d_blocks)
            table[s, 2 * slots + j] = metas[s][0, slots + j]
    for s in range(spans):
        row = (spans - s) % spans
        before = rank_before(table, row, spans, slots)
        slot = wrap(me - lax.rem(before, spans), spans)
        tile = values[jnp.minimum(lax.div(before + slot, spans), slots - 1)]
        live = slot < live_count(table, row, slots)
        outs[s][slots] = jnp.where(live, tile.astype(jnp.float32), 0.0).astype(tile.dtype)
        for j in range(slots):
            start = pl.multiple_of(table[row, j] * block, block)
            outs[s][j] = hidden[:, pl.ds(start, block)]


def lay_kernel(weight, first_weight, sem):
    copy = pltpu.make_async_copy(weight.at[pl.ds(0, first_weight.shape[0])], first_weight, sem)
    copy.start()
    copy.wait()


def chunk_at(place):
    tensors, cores = lax.axis_size("tensor"), lax.axis_size("dp")
    t_place = lax.rem(lax.axis_index("tensor") + place // cores, tensors)
    d_place = lax.rem(lax.axis_index("dp") + place % cores, cores)
    return t_place * cores + d_place


def early_matmul_kernel(width, weight, *refs):
    pieces, (out, rows) = refs[:-2], refs[-2:]
    step = pl.program_id(0)

    @pl.when(step == 0)
    def _():
        at = 0
        for piece in pieces:
            rows[at : at + piece.shape[0]] = piece[...]
            at += piece.shape[0]

    here = pl.ds(pl.multiple_of(step * width, width), width)
    out[:, here] = lax.dot_general(
        rows[...], weight[here], NT, preferred_element_type=jnp.float32
    )


def early_matmul_call(width, columns, weight, pieces):
    tokens, d_width = sum(piece.shape[0] for piece in pieces), weight.shape[1]
    return pl.pallas_call(
        functools.partial(early_matmul_kernel, width),
        grid=(columns // width,),
        out_shape=[
            jax.ShapeDtypeStruct((tokens, columns), jnp.float32),
            jax.ShapeDtypeStruct((tokens, d_width), weight.dtype),
        ],
        in_specs=[vmem()] * (1 + len(pieces)),
        out_specs=[vmem()] * 2,
        compiler_params=params(),
        cost_estimate=cost(EARLY * tokens * columns),
        name="partial",
    )(weight, *pieces)


def add_delta(table, rows, held, total, low):
    slots, block, _ = held.shape
    count = live_count(table, 0, slots)
    for j in range(slots):
        f_start = table[0, j] * block - low

        @pl.when((j < count) & (f_start >= 0) & (f_start < total.shape[1]))
        def _():
            d_start = pl.multiple_of(table[0, slots + j] * block, block)
            place = pl.ds(pl.multiple_of(f_start, block), block)
            total[:, place] += lax.dot_general(
                rows[:, pl.ds(d_start, block)], held[j], NT, preferred_element_type=jnp.float32
            )


def put_chunks(total, out, first, here):
    spans, chunk = out.shape[:2]
    me = lax.axis_index("seq")
    for p in range(spans):
        result = total[p * chunk : (p + 1) * chunk].astype(out.dtype)
        out[chunk_at(p), :, here] = result

        @pl.when(chunk_at(p) == wrap(me - 1, spans))
        def _():
            first[:, here] = result


def begin_kernel(spans, slots, block, table, early, rows, *refs):
    stored, (first, held, total, chunk_rows) = refs[:spans], refs[spans:]
    me = lax.axis_index("seq")
    before = rank_before(table, 0, spans, slots)
    for j in range(slots):
        for s in range(spans):

            @pl.when(lax.rem(before + j, spans) == wrap(me - s, spans))
            def _():
                held[j] = stored[s][slots]

    chunk = first.shape[0]
    for p in range(spans):

        @pl.when(chunk_at(p) == wrap(me - 1, spans))
        def _():
            total[...] = early[p * chunk : (p + 1) * chunk]
            chunk_rows[...] = rows[p * chunk : (p + 1) * chunk]

    add_delta(table, chunk_rows, held, total, 0)
    first[...] = total[...].astype(first.dtype)


def begin_call(sizes, table, early, rows, stored):
    spans, slots, block = sizes
    (tokens, columns), d_width = early.shape, rows.shape[1]
    chunk = tokens // spans
    return pl.pallas_call(
        functools.partial(begin_kernel, *sizes),
        out_shape=[
            jax.ShapeDtypeStruct((chunk, columns), rows.dtype),
            jax.ShapeDtypeStruct((slots, block, block), rows.dtype),
        ],
        in_specs=[smem()] + [vmem()] * (2 + spans),
        out_specs=[vmem()] * 2,
        scratch_shapes=[
            pltpu.VMEM((chunk, columns), jnp.float32),
            pltpu.VMEM((chunk, d_width), rows.dtype),
        ],
        compiler_params=params(),
        cost_estimate=cost(chunk * columns),
        name="begin",
    )(table, early, rows, *stored)


def delta_kernel(table, early, rows, held, out, total):
    total[...] = early[...]
    add_delta(table, rows, held, total, 0)
    chunk = out.shape[1]
    for p in range(out.shape[0]):
        out[chunk_at(p)] = total[p * chunk : (p + 1) * chunk].astype(out.dtype)


def delta_call(spans, table, early, rows, held):
    tokens, columns = early.shape
    return pl.pallas_call(
        delta_kernel,
        out_shape=jax.ShapeDtypeStruct((spans, tokens // spans, columns), rows.dtype),
        in_specs=[smem()] + [vmem()] * 3,
        out_specs=vmem(),
        scratch_shapes=[pltpu.VMEM((tokens, columns), jnp.float32)],
        compiler_params=params(),
        cost_estimate=cost(early.size),
        name="delta",
    )(table, early, rows, held)


def matmul_kernel(low, ends, table, weight, rows, held, *refs):
    outs, total = refs[:-1], refs[-1]
    step, width = pl.program_id(0), total.shape[1]
    total[...] = lax.dot_general(rows[...], weight[...], NT, preferred_element_type=jnp.float32)
    add_delta(table, rows, held, total, (low + step) * width)
    for part, (begin, end) in enumerate(zip((0, *ends), ends)):

        @pl.when((step >= begin) & (step < end))
        def _():
            here = pl.ds(pl.multiple_of((step - begin) * width, width), width)
            put_chunks(total, *outs[2 * part : 2 * part + 2], here)


def matmul_call(spans, low, ends, width, table, weight, rows, held):
    tokens, d_width = rows.shape
    weight_spec = pl.BlockSpec((width, d_width), lambda i: (i + low, 0))
    shapes = []
    for begin, end in zip((0, *ends), ends):
        columns = (end - begin) * width
        shapes.append(jax.ShapeDtypeStruct((spans, tokens // spans, columns), rows.dtype))
        shapes.append(jax.ShapeDtypeStruct((tokens // spans, columns), rows.dtype))
    return pl.pallas_call(
        functools.partial(matmul_kernel, low, ends),
        grid=(ends[-1],),
        out_shape=shapes,
        in_specs=[smem(), weight_spec, vmem(), vmem()],
        out_specs=[vmem()] * len(shapes),
        scratch_shapes=[pltpu.VMEM((tokens, width), jnp.float32)],
        compiler_params=params(),
        cost_estimate=cost(MATMUL * tokens * ends[-1] * width),
        name="partial",
    )(table, stay(weight), rows, held)


def attach_kernel(first, *refs):
    riders, out = refs[:-1], refs[-1]
    at = first.shape[1]
    out[:, :at] = first[...]
    for rider in riders:
        out[:, at : at + rider.shape[1]] = rider[...]
        at += rider.shape[1]


def attach_call(first, riders):
    chunk, columns = first.shape
    columns += sum(rider.shape[1] for rider in riders)
    return pl.pallas_call(
        attach_kernel,
        out_shape=jax.ShapeDtypeStruct((chunk, columns), first.dtype),
        in_specs=[vmem()] * (1 + len(riders)),
        out_specs=vmem(),
        compiler_params=params(),
        cost_estimate=cost(first.size),
        name="attach",
    )(first, *riders)


def add_kernel(t, riders, partials, arrived, out, *mine):
    spans, _, columns = partials.shape
    chunk = wrap(lax.axis_index("seq") - t, spans)
    result = partials[chunk].astype(jnp.float32) + arrived[:, :columns].astype(jnp.float32)
    out[:, :columns] = result.astype(out.dtype)
    if riders:
        block = mine[0].shape[1]
        mine[0][...] = arrived[:, columns : columns + block]
        out[:, columns:] = arrived[:, columns + block :]


def add_call(t, partials, arrived, block):
    chunk, columns = partials.shape[1:]
    riders = (arrived.shape[1] - columns) // block
    shapes = [jax.ShapeDtypeStruct((chunk, arrived.shape[1] - min(riders, 1) * block), arrived.dtype)]
    if riders:
        shapes.append(jax.ShapeDtypeStruct((chunk, block), arrived.dtype))
    return pl.pallas_call(
        functools.partial(add_kernel, t, riders),
        out_shape=shapes,
        in_specs=[vmem(), vmem()],
        out_specs=[vmem()] * len(shapes),
        compiler_params=params(),
        cost_estimate=cost(arrived.size),
        name="add",
    )(partials, arrived)


def last_kernel(low, partials, arrived, *refs):
    out, total, sem = refs[-3:]
    columns = total.shape[1]
    result = partials[lax.axis_index("seq")].astype(jnp.float32)
    result = result + arrived[:, :columns].astype(jnp.float32)
    total[...] = result.astype(out.dtype)
    copy = pltpu.make_async_copy(total, out.at[:, pl.ds(low, columns)], sem)
    copy.start()
    copy.wait()


def last_call(low, partials, arrived, out, shape):
    _, chunk, columns = partials.shape
    given = [] if out is None else [out]
    return pl.pallas_call(
        functools.partial(last_kernel, low),
        out_shape=shape,
        in_specs=[vmem()] * 2 + [hbm()] * len(given),
        out_specs=hbm(),
        scratch_shapes=[pltpu.VMEM((chunk, columns), shape.dtype), pltpu.SemaphoreType.DMA],
        input_output_aliases={2: 0} if given else {},
        compiler_params=params(),
        cost_estimate=cost(partials.size),
        name="last_sum",
    )(partials, arrived, *given)


def grad_kernel(spans, slots, block, table, rows, *refs):
    hidden, outs, (cols,) = refs[:spans], refs[spans : 2 * spans], refs[2 * spans :]
    me = lax.axis_index("seq")
    count, before = live_count(table, 0, slots), rank_before(table, 0, spans, slots)
    chunk = rows.shape[0] // spans
    for s in range(spans):
        cols[s] = hidden[s][:slots]
    for s in range(spans):
        slot = wrap(lax.rem(me + s, spans) - lax.rem(before, spans), spans)
        outs[s][...] = jnp.zeros_like(outs[s])

        @pl.when(slot < count)
        def _():
            d_start = pl.multiple_of(table[0, slots + slot] * block, block)
            total = jnp.zeros((block, block), jnp.float32)
            for p in range(spans):
                total = total + lax.dot_general(
                    cols[wrap(me - chunk_at(p), spans), slot],
                    rows[p * chunk : (p + 1) * chunk, pl.ds(d_start, block)],
                    TN,
                    preferred_element_type=jnp.float32,
                )
            outs[s][...] = total.astype(outs[s].dtype)


def grad_call(sizes, table, rows, hidden_cols):
    spans = sizes[0]
    slots, chunk, block = hidden_cols[0].shape
    slots -= 1
    return pl.pallas_call(
        functools.partial(grad_kernel, *sizes),
        out_shape=[jax.ShapeDtypeStruct((block, block), jnp.bfloat16)] * spans,
        in_specs=[smem()] + [vmem()] * (spans + 1),
        out_specs=[vmem()] * spans,
        scratch_shapes=[pltpu.VMEM((spans, slots, chunk, block), jnp.bfloat16)],
        compiler_params=params(),
        cost_estimate=cost(rows.size),
        name="tile_grad",
    )(table, rows, *hidden_cols)


def adam_kernel(spans, slots, columns, table, *refs):
    arrived, refs = refs[:spans], refs[spans:]
    values, one, two, values_new, one_new, two_new, grads = refs
    me = lax.axis_index("seq")
    for s in range(spans - 1):
        grads[s] = arrived[s][...]
    grads[spans - 1] = arrived[-1][:, columns:]
    befores = [rank_before(table, s, spans, slots) for s in range(spans)]
    counts = [live_count(table, s, slots) for s in range(spans)]
    for owned in range(slots):
        rank = owned * spans + me
        source, live = jnp.int32(0), jnp.int32(0)
        for s in range(spans):
            holds = (befores[s] <= rank) & (rank < befores[s] + counts[s])
            source, live = jnp.where(holds, s, source), jnp.where(holds, 1, live)
        grad = grads[source].astype(jnp.float32)
        stored, old_one, old_two = values[owned], one[owned], two[owned]
        new_one = BETA_ONE * old_one + (1.0 - BETA_ONE) * grad
        new_two = BETA_TWO * old_two + (1.0 - BETA_TWO) * grad * grad
        stepped = (
            new_one
            / (1.0 - BETA_ONE**STEP)
            / (jnp.sqrt(new_two / (1.0 - BETA_TWO**STEP)) + EPSILON)
        )
        values_new[owned] = jnp.where(live > 0, stored - RATE * stepped, stored)
        one_new[owned] = jnp.where(live > 0, new_one, old_one)
        two_new[owned] = jnp.where(live > 0, new_two, old_two)


def adam_call(sizes, columns, table, grads, *states):
    spans, slots, block = sizes
    tile = jax.ShapeDtypeStruct((slots, block, block), jnp.float32)
    return pl.pallas_call(
        functools.partial(adam_kernel, spans, slots, columns),
        out_shape=(tile, tile, tile),
        in_specs=[smem()] + [vmem()] * (spans + 3),
        out_specs=(vmem(), vmem(), vmem()),
        scratch_shapes=[pltpu.VMEM((spans, block, block), jnp.bfloat16)],
        compiler_params=params(),
        cost_estimate=cost(slots * block * block),
        name="adam",
    )(table, *grads, *[state[0, 0] for state in states])


def take_from(array, axis, places):
    size = lax.axis_size(axis)
    return lax.ppermute(array, axis, [((i + places) % size, i) for i in range(size)])


def take_chunk(own, place):
    tensors, cores = lax.axis_size("tensor"), lax.axis_size("dp")
    t_place, d_place = divmod(place, cores)
    pairs = []
    for t in range(tensors):
        for d in range(cores):
            source = (t + t_place) % tensors * cores + (d + d_place) % cores
            pairs.append((source, t * cores + d))
    return lax.ppermute(own, ("tensor", "dp"), pairs)


def exchange(pieces):
    return [pieces[0]] + [take_from(pieces[s], "seq", -s) for s in range(1, len(pieces))]


def per_device(
    hidden_in, cotangent, down_weight, tile_ids, tile_live, values, moment_one, moment_two
):
    spans, cores = lax.axis_size("seq"), lax.axis_size("dp")
    slots, block = values.shape[2], values.shape[3]
    f_width, d_width = down_weight.shape
    d_blocks, f_blocks = d_width // block, f_width // block
    chunk = hidden_in.shape[0]
    sizes = (spans, slots, block)
    group = max(size for size in range(1, 5) if f_blocks % size == 0)
    width = group * block
    ends = [sum(PARTS[:part]) for part in range(len(PARTS) + 1)]
    cuts = [(f_blocks // group) * end // ends[-1] for end in ends]
    ranges = list(zip(cuts[:-1], cuts[1:]))

    local = [take_chunk(cotangent, place) for place in range(1, cores)]
    firsts = [take_from(cotangent, "tensor", t) for t in range(1, lax.axis_size("tensor"))]

    meta = jnp.concatenate([tile_ids[0], tile_live[0]], axis=1)
    metas = exchange([meta] * spans)
    values_half, hidden_here, local_rows = pl.pallas_call(
        early_kernel,
        out_shape=[
            jax.ShapeDtypeStruct((slots, block, block), jnp.bfloat16),
            jax.ShapeDtypeStruct(hidden_in.shape, hidden_in.dtype),
            jax.ShapeDtypeStruct((cores * chunk, d_width), cotangent.dtype),
        ],
        in_specs=[hbm()] * 3 + [vmem()] * (cores - 1),
        out_specs=[vmem()] * 3,
        scratch_shapes=[
            pltpu.VMEM((slots, block, block), jnp.float32),
            pltpu.SemaphoreType.DMA((3,)),
        ],
        compiler_params=params(),
        cost_estimate=cost(hidden_in.size),
        name="early",
    )(stay(values[0, 0]), stay(hidden_in), stay(cotangent), *local)
    table, *picked = pl.pallas_call(
        functools.partial(pick_kernel, *sizes, d_blocks),
        out_shape=[jax.ShapeDtypeStruct((spans, 3 * slots), jnp.int32)]
        + [jax.ShapeDtypeStruct((slots + 1, chunk, block), jnp.bfloat16)] * spans,
        in_specs=[smem()] * spans + [vmem(), vmem()],
        out_specs=[smem()] + [vmem()] * spans,
        compiler_params=params(),
        cost_estimate=cost(hidden_in.size),
        name="pick",
    )(*metas, values_half, hidden_here)
    crossed = exchange(picked)

    laid = ranges[0][1]
    first_weight = pl.pallas_call(
        lay_kernel,
        out_shape=jax.ShapeDtypeStruct((laid * width, d_width), down_weight.dtype),
        in_specs=[hbm()],
        out_specs=vmem(),
        scratch_shapes=[pltpu.SemaphoreType.DMA],
        compiler_params=params(),
        cost_estimate=cost(AHEAD * laid * width * d_width),
        name="lay",
    )(stay(down_weight))

    firsts, picked = lax.optimization_barrier((firsts, picked))
    remote = []
    for first in firsts:
        remote += [first] + [take_from(first, "dp", d) for d in range(1, cores)]
    early, rows = early_matmul_call(width, laid * width, first_weight, [local_rows, *remote])
    first, held = begin_call(sizes, table, early, rows, crossed)
    moving = [take_from(first, "seq", -1)]
    partials = [delta_call(spans, table, early, rows, held)]
    for part, (low, high) in enumerate(ranges[1:], 1):
        partial, first = matmul_call(
            spans, low, (high - low,), width, table, down_weight, rows, held
        )
        if part == RIDE:
            grads = grad_call(sizes, table, rows, crossed)
            first = attach_call(first, grads[1:])
        partials.append(partial)
        moving.append(take_from(first, "seq", -1))

    tiles = [grads[0]]
    for t in range(2, spans):
        for part in range(len(ranges)):
            moving[part], *mine = add_call(t, partials[part], moving[part], block)
            tiles += mine
            moving[part] = take_from(moving[part], "seq", -1)
    tiles.append(moving[RIDE])
    columns = partials[RIDE].shape[2]

    hidden_grad = None
    shape = jax.ShapeDtypeStruct((chunk, f_width), jnp.bfloat16)
    order = [part for part in range(len(ranges)) if part != LAST] + [LAST]
    for part in order:
        if part == LAST:
            tiles[0], hidden_grad = lax.optimization_barrier((tiles[0], hidden_grad))
            new = adam_call(sizes, columns, table, tiles, values, moment_one, moment_two)
            moving[part], new = lax.optimization_barrier((moving[part], new))
        hidden_grad = last_call(
            ranges[part][0] * width, partials[part], moving[part], hidden_grad, shape
        )
    return (hidden_grad,) + tuple(array[None, None] for array in new)


def solution(mesh):
    shards = P(("groups", "seq"), ("tensor", "dp"))
    tiles = P(("groups", "seq"), ("tensor", "dp"), None, None, None)
    lists = P(("groups", "seq"), ("tensor", "dp"), None)
    return jax.shard_map(
        per_device,
        mesh=mesh,
        in_specs=(
            shards,
            P(("groups", "tensor", "dp"), "seq"),
            P(("tensor", "dp"), "seq"),
            lists,
            lists,
            tiles,
            tiles,
            tiles,
        ),
        out_specs=(shards, tiles, tiles, tiles),
        check_vma=False,
    )
```

```python
import functools

import jax
import jax.numpy as jnp
from jax import lax
from jax.experimental import pallas as pl
from jax.experimental.pallas import tpu as pltpu
from jax.sharding import PartitionSpec as P

STEP = 100
BETA_ONE = 0.9
BETA_TWO = 0.999
RATE = 0.01
EPSILON = 1e-08
VMEM_LIMIT = 12 * 1024 * 1024
MATMUL = 4096
EARLY = 1
AHEAD = 5000
PARTS = (3, 2, 2)
RIDE = 2
LAST = 1
NT = (((1,), (1,)), ((), ()))
TN = (((0,), (0,)), ((), ()))


def vmem():
    return pl.BlockSpec(memory_space=pltpu.VMEM)


def smem():
    return pl.BlockSpec(memory_space=pltpu.SMEM)


def hbm():
    return pl.BlockSpec(memory_space=pltpu.HBM)


def stay(array):
    return pltpu.with_memory_space_constraint(array, pltpu.HBM)


def cost(count):
    return pl.CostEstimate(flops=count, bytes_accessed=2 * count, transcendentals=0)


def params():
    return pltpu.CompilerParams(vmem_limit_bytes=VMEM_LIMIT)


def wrap(index, size):
    return lax.rem(index + size, size)


def live_count(table, row, slots):
    count = table[row, 2 * slots]
    for slot in range(1, slots):
        count = count + table[row, 2 * slots + slot]
    return count


def rank_before(table, row, spans, slots):
    me = lax.axis_index("seq")
    before = jnp.int32(0)
    for other in range(spans):
        ahead = wrap(me - other, spans) < wrap(me - row, spans)
        before = before + jnp.where(ahead, live_count(table, other, slots), 0)
    return before


def early_kernel(values, hidden, own, *refs):
    others, (values_half, hidden_here, rows, stored, sems) = refs[:-5], refs[-5:]
    chunk = own.shape[0]
    copies = [
        pltpu.make_async_copy(values, stored, sems.at[0]),
        pltpu.make_async_copy(hidden, hidden_here, sems.at[1]),
        pltpu.make_async_copy(own, rows.at[pl.ds(0, chunk)], sems.at[2]),
    ]
    for copy in copies:
        copy.start()
    for p, other in enumerate(others):
        rows[(p + 1) * chunk : (p + 2) * chunk] = other[...]
    copies[0].wait()
    values_half[...] = stored[...].astype(values_half.dtype)
    copies[1].wait()
    copies[2].wait()


def table_kernel(slots, d_blocks, *refs):
    metas, table = refs[:-1], refs[-1]
    for s, meta in enumerate(metas):
        for j in range(slots):
            table[s, j] = lax.div(meta[0, j], d_blocks)
            table[s, slots + j] = lax.rem(meta[0, j], d_blocks)
            table[s, 2 * slots + j] = meta[0, slots + j]


def pick_kernel(spans, slots, block, d_blocks, *refs):
    metas, (values, hidden), outs, table = refs[:spans], refs[spans : spans + 2], refs[spans + 2 : -1], refs[-1]
    me = lax.axis_index("seq")
    table_kernel(slots, d_blocks, *metas, table)
    for s in range(spans):
        row = (spans - s) % spans
        before = rank_before(table, row, spans, slots)
        slot = wrap(me - lax.rem(before, spans), spans)
        tile = values[jnp.minimum(lax.div(before + slot, spans), slots - 1)]
        live = slot < live_count(table, row, slots)
        outs[s][slots] = jnp.where(live, tile.astype(jnp.float32), 0.0).astype(tile.dtype)
        for j in range(slots):
            start = pl.multiple_of(table[row, j] * block, block)
            outs[s][j] = hidden[:, pl.ds(start, block)]


def lay_kernel(weight, first_weight, sem):
    copy = pltpu.make_async_copy(weight.at[pl.ds(0, first_weight.shape[0])], first_weight, sem)
    copy.start()
    copy.wait()


def chunk_at(place):
    tensors, cores = lax.axis_size("tensor"), lax.axis_size("dp")
    t_place = lax.rem(lax.axis_index("tensor") + place // cores, tensors)
    d_place = lax.rem(lax.axis_index("dp") + place % cores, cores)
    return t_place * cores + d_place


def early_matmul_kernel(width, weight, *refs):
    pieces, (out, rows) = refs[:-2], refs[-2:]
    step = pl.program_id(0)

    @pl.when(step == 0)
    def _():
        at = 0
        for piece in pieces:
            rows[at : at + piece.shape[0]] = piece[...]
            at += piece.shape[0]

    here = pl.ds(pl.multiple_of(step * width, width), width)
    out[:, here] = lax.dot_general(
        rows[...], weight[here], NT, preferred_element_type=jnp.float32
    )


def early_matmul_call(width, columns, weight, pieces):
    tokens, d_width = sum(piece.shape[0] for piece in pieces), weight.shape[1]
    return pl.pallas_call(
        functools.partial(early_matmul_kernel, width),
        grid=(columns // width,),
        out_shape=[
            jax.ShapeDtypeStruct((tokens, columns), jnp.float32),
            jax.ShapeDtypeStruct((tokens, d_width), weight.dtype),
        ],
        in_specs=[vmem()] * (1 + len(pieces)),
        out_specs=[vmem()] * 2,
        compiler_params=params(),
        cost_estimate=cost(EARLY * tokens * columns),
        name="partial",
    )(weight, *pieces)


def add_delta(table, rows, held, total, low):
    slots, block, _ = held.shape
    count = live_count(table, 0, slots)
    for j in range(slots):
        f_start = table[0, j] * block - low

        @pl.when((j < count) & (f_start >= 0) & (f_start < total.shape[1]))
        def _():
            d_start = pl.multiple_of(table[0, slots + j] * block, block)
            place = pl.ds(pl.multiple_of(f_start, block), block)
            total[:, place] += lax.dot_general(
                rows[:, pl.ds(d_start, block)], held[j], NT, preferred_element_type=jnp.float32
            )


def put_chunks(total, out, first, here):
    spans, chunk = out.shape[:2]
    me = lax.axis_index("seq")
    for p in range(spans):
        result = total[p * chunk : (p + 1) * chunk].astype(out.dtype)
        out[chunk_at(p), :, here] = result

        @pl.when(chunk_at(p) == wrap(me - 1, spans))
        def _():
            first[:, here] = result


def begin_kernel(spans, slots, block, table, early, rows, *refs):
    stored, (first, held, total, chunk_rows) = refs[:spans], refs[spans:]
    me = lax.axis_index("seq")
    before = rank_before(table, 0, spans, slots)
    for j in range(slots):
        for s in range(spans):

            @pl.when(lax.rem(before + j, spans) == wrap(me - s, spans))
            def _():
                held[j] = stored[s][slots]

    chunk = first.shape[0]
    for p in range(spans):

        @pl.when(chunk_at(p) == wrap(me - 1, spans))
        def _():
            total[...] = early[p * chunk : (p + 1) * chunk]
            chunk_rows[...] = rows[p * chunk : (p + 1) * chunk]

    add_delta(table, chunk_rows, held, total, 0)
    first[...] = total[...].astype(first.dtype)


def begin_call(sizes, table, early, rows, stored):
    spans, slots, block = sizes
    (tokens, columns), d_width = early.shape, rows.shape[1]
    chunk = tokens // spans
    return pl.pallas_call(
        functools.partial(begin_kernel, *sizes),
        out_shape=[
            jax.ShapeDtypeStruct((chunk, columns), rows.dtype),
            jax.ShapeDtypeStruct((slots, block, block), rows.dtype),
        ],
        in_specs=[smem()] + [vmem()] * (2 + spans),
        out_specs=[vmem()] * 2,
        scratch_shapes=[
            pltpu.VMEM((chunk, columns), jnp.float32),
            pltpu.VMEM((chunk, d_width), rows.dtype),
        ],
        compiler_params=params(),
        cost_estimate=cost(chunk * columns),
        name="begin",
    )(table, early, rows, *stored)


def delta_kernel(table, early, rows, held, out, total):
    total[...] = early[...]
    add_delta(table, rows, held, total, 0)
    chunk = out.shape[1]
    for p in range(out.shape[0]):
        out[chunk_at(p)] = total[p * chunk : (p + 1) * chunk].astype(out.dtype)


def delta_call(spans, table, early, rows, held):
    tokens, columns = early.shape
    return pl.pallas_call(
        delta_kernel,
        out_shape=jax.ShapeDtypeStruct((spans, tokens // spans, columns), rows.dtype),
        in_specs=[smem()] + [vmem()] * 3,
        out_specs=vmem(),
        scratch_shapes=[pltpu.VMEM((tokens, columns), jnp.float32)],
        compiler_params=params(),
        cost_estimate=cost(early.size),
        name="delta",
    )(table, early, rows, held)


def matmul_kernel(low, ends, table, weight, rows, held, *refs):
    outs, total = refs[:-1], refs[-1]
    step, width = pl.program_id(0), total.shape[1]
    total[...] = lax.dot_general(rows[...], weight[...], NT, preferred_element_type=jnp.float32)
    add_delta(table, rows, held, total, (low + step) * width)
    for part, (begin, end) in enumerate(zip((0, *ends), ends)):

        @pl.when((step >= begin) & (step < end))
        def _():
            here = pl.ds(pl.multiple_of((step - begin) * width, width), width)
            put_chunks(total, *outs[2 * part : 2 * part + 2], here)


def matmul_call(spans, low, ends, width, table, weight, rows, held):
    tokens, d_width = rows.shape
    weight_spec = pl.BlockSpec((width, d_width), lambda i: (i + low, 0))
    shapes = []
    for begin, end in zip((0, *ends), ends):
        columns = (end - begin) * width
        shapes.append(jax.ShapeDtypeStruct((spans, tokens // spans, columns), rows.dtype))
        shapes.append(jax.ShapeDtypeStruct((tokens // spans, columns), rows.dtype))
    return pl.pallas_call(
        functools.partial(matmul_kernel, low, ends),
        grid=(ends[-1],),
        out_shape=shapes,
        in_specs=[smem(), weight_spec, vmem(), vmem()],
        out_specs=[vmem()] * len(shapes),
        scratch_shapes=[pltpu.VMEM((tokens, width), jnp.float32)],
        compiler_params=params(),
        cost_estimate=cost(MATMUL * tokens * ends[-1] * width),
        name="partial",
    )(table, stay(weight), rows, held)


def attach_kernel(first, *refs):
    riders, out = refs[:-1], refs[-1]
    at = first.shape[1]
    out[:, :at] = first[...]
    for rider in riders:
        out[:, at : at + rider.shape[1]] = rider[...]
        at += rider.shape[1]


def attach_call(first, riders):
    chunk, columns = first.shape
    columns += sum(rider.shape[1] for rider in riders)
    return pl.pallas_call(
        attach_kernel,
        out_shape=jax.ShapeDtypeStruct((chunk, columns), first.dtype),
        in_specs=[vmem()] * (1 + len(riders)),
        out_specs=vmem(),
        compiler_params=params(),
        cost_estimate=cost(first.size),
        name="attach",
    )(first, *riders)


def add_kernel(t, riders, partials, arrived, out, *mine):
    spans, _, columns = partials.shape
    chunk = wrap(lax.axis_index("seq") - t, spans)
    result = partials[chunk].astype(jnp.float32) + arrived[:, :columns].astype(jnp.float32)
    out[:, :columns] = result.astype(out.dtype)
    if riders:
        block = mine[0].shape[1]
        mine[0][...] = arrived[:, columns : columns + block]
        out[:, columns:] = arrived[:, columns + block :]


def add_call(t, partials, arrived, block):
    chunk, columns = partials.shape[1:]
    riders = (arrived.shape[1] - columns) // block
    shapes = [jax.ShapeDtypeStruct((chunk, arrived.shape[1] - min(riders, 1) * block), arrived.dtype)]
    if riders:
        shapes.append(jax.ShapeDtypeStruct((chunk, block), arrived.dtype))
    return pl.pallas_call(
        functools.partial(add_kernel, t, riders),
        out_shape=shapes,
        in_specs=[vmem(), vmem()],
        out_specs=[vmem()] * len(shapes),
        compiler_params=params(),
        cost_estimate=cost(arrived.size),
        name="add",
    )(partials, arrived)


def last_kernel(low, partials, arrived, *refs):
    out, total, sems = refs[-3:]
    me, columns = lax.axis_index("seq"), total.shape[1]
    middle, copies = columns // 256 * 128, []
    for k, here in enumerate((slice(0, middle), slice(middle, columns))):
        result = partials[me, :, here].astype(jnp.float32) + arrived[:, here].astype(jnp.float32)
        total[:, here] = result.astype(out.dtype)
        copy = pltpu.make_async_copy(
            total.at[:, here], out.at[:, pl.ds(low + here.start, here.stop - here.start)], sems.at[k]
        )
        copy.start()
        copies.append(copy)
    for copy in copies:
        copy.wait()


def last_call(low, partials, arrived, out, shape):
    _, chunk, columns = partials.shape
    given = [] if out is None else [out]
    return pl.pallas_call(
        functools.partial(last_kernel, low),
        out_shape=shape,
        in_specs=[vmem()] * 2 + [hbm()] * len(given),
        out_specs=hbm(),
        scratch_shapes=[
            pltpu.VMEM((chunk, columns), shape.dtype),
            pltpu.SemaphoreType.DMA((2,)),
        ],
        input_output_aliases={2: 0} if given else {},
        compiler_params=params(),
        cost_estimate=cost(partials.size),
        name="last_sum",
    )(partials, arrived, *given)


def grad_kernel(spans, slots, block, table, rows, *refs):
    hidden, outs, (cols,) = refs[:spans], refs[spans : 2 * spans], refs[2 * spans :]
    me = lax.axis_index("seq")
    count, before = live_count(table, 0, slots), rank_before(table, 0, spans, slots)
    chunk = rows.shape[0] // spans
    for s in range(spans):
        cols[s] = hidden[s][:slots]
    for s in range(spans):
        slot = wrap(lax.rem(me + s, spans) - lax.rem(before, spans), spans)
        outs[s][...] = jnp.zeros_like(outs[s])

        @pl.when(slot < count)
        def _():
            d_start = pl.multiple_of(table[0, slots + slot] * block, block)
            total = jnp.zeros((block, block), jnp.float32)
            for p in range(spans):
                total = total + lax.dot_general(
                    cols[wrap(me - chunk_at(p), spans), slot],
                    rows[p * chunk : (p + 1) * chunk, pl.ds(d_start, block)],
                    TN,
                    preferred_element_type=jnp.float32,
                )
            outs[s][...] = total.astype(outs[s].dtype)


def grad_call(sizes, table, rows, hidden_cols):
    spans = sizes[0]
    slots, chunk, block = hidden_cols[0].shape
    slots -= 1
    return pl.pallas_call(
        functools.partial(grad_kernel, *sizes),
        out_shape=[jax.ShapeDtypeStruct((block, block), jnp.bfloat16)] * spans,
        in_specs=[smem()] + [vmem()] * (spans + 1),
        out_specs=[vmem()] * spans,
        scratch_shapes=[pltpu.VMEM((spans, slots, chunk, block), jnp.bfloat16)],
        compiler_params=params(),
        cost_estimate=cost(rows.size),
        name="tile_grad",
    )(table, rows, *hidden_cols)


def adam_kernel(spans, slots, columns, table, *refs):
    arrived, refs = refs[:spans], refs[spans:]
    values, one, two, values_new, one_new, two_new, grads = refs
    me = lax.axis_index("seq")
    for s in range(spans - 1):
        grads[s] = arrived[s][...]
    grads[spans - 1] = arrived[-1][:, columns:]
    befores = [rank_before(table, s, spans, slots) for s in range(spans)]
    counts = [live_count(table, s, slots) for s in range(spans)]
    for owned in range(slots):
        rank = owned * spans + me
        source, live = jnp.int32(0), jnp.int32(0)
        for s in range(spans):
            holds = (befores[s] <= rank) & (rank < befores[s] + counts[s])
            source, live = jnp.where(holds, s, source), jnp.where(holds, 1, live)
        grad = grads[source].astype(jnp.float32)
        stored, old_one, old_two = values[owned], one[owned], two[owned]
        new_one = BETA_ONE * old_one + (1.0 - BETA_ONE) * grad
        new_two = BETA_TWO * old_two + (1.0 - BETA_TWO) * grad * grad
        stepped = (
            new_one
            / (1.0 - BETA_ONE**STEP)
            / (jnp.sqrt(new_two / (1.0 - BETA_TWO**STEP)) + EPSILON)
        )
        values_new[owned] = jnp.where(live > 0, stored - RATE * stepped, stored)
        one_new[owned] = jnp.where(live > 0, new_one, old_one)
        two_new[owned] = jnp.where(live > 0, new_two, old_two)


def adam_call(sizes, columns, table, grads, *states):
    spans, slots, block = sizes
    tile = jax.ShapeDtypeStruct((slots, block, block), jnp.float32)
    return pl.pallas_call(
        functools.partial(adam_kernel, spans, slots, columns),
        out_shape=(tile, tile, tile),
        in_specs=[smem()] + [vmem()] * (spans + 3),
        out_specs=(vmem(), vmem(), vmem()),
        scratch_shapes=[pltpu.VMEM((spans, block, block), jnp.bfloat16)],
        compiler_params=params(),
        cost_estimate=cost(slots * block * block),
        name="adam",
    )(table, *grads, *[state[0, 0] for state in states])


def take_from(array, axis, places):
    size = lax.axis_size(axis)
    return lax.ppermute(array, axis, [((i + places) % size, i) for i in range(size)])


def take_chunk(own, place):
    tensors, cores = lax.axis_size("tensor"), lax.axis_size("dp")
    t_place, d_place = divmod(place, cores)
    pairs = []
    for t in range(tensors):
        for d in range(cores):
            source = (t + t_place) % tensors * cores + (d + d_place) % cores
            pairs.append((source, t * cores + d))
    return lax.ppermute(own, ("tensor", "dp"), pairs)


def exchange(pieces):
    return [pieces[0]] + [take_from(pieces[s], "seq", -s) for s in range(1, len(pieces))]


def per_device(
    hidden_in, cotangent, down_weight, tile_ids, tile_live, values, moment_one, moment_two
):
    spans, cores = lax.axis_size("seq"), lax.axis_size("dp")
    slots, block = values.shape[2], values.shape[3]
    f_width, d_width = down_weight.shape
    d_blocks, f_blocks = d_width // block, f_width // block
    chunk = hidden_in.shape[0]
    sizes = (spans, slots, block)
    group = max(size for size in range(1, 5) if f_blocks % size == 0)
    width = group * block
    ends = [sum(PARTS[:part]) for part in range(len(PARTS) + 1)]
    cuts = [(f_blocks // group) * end // ends[-1] for end in ends]
    ranges = list(zip(cuts[:-1], cuts[1:]))

    local = [take_chunk(cotangent, place) for place in range(1, cores)]
    firsts = [take_from(cotangent, "tensor", t) for t in range(1, lax.axis_size("tensor"))]

    meta = jnp.concatenate([tile_ids[0], tile_live[0]], axis=1)
    metas = exchange([meta] * spans)
    values_half, hidden_here, local_rows = pl.pallas_call(
        early_kernel,
        out_shape=[
            jax.ShapeDtypeStruct((slots, block, block), jnp.bfloat16),
            jax.ShapeDtypeStruct(hidden_in.shape, hidden_in.dtype),
            jax.ShapeDtypeStruct((cores * chunk, d_width), cotangent.dtype),
        ],
        in_specs=[hbm()] * 3 + [vmem()] * (cores - 1),
        out_specs=[vmem()] * 3,
        scratch_shapes=[
            pltpu.VMEM((slots, block, block), jnp.float32),
            pltpu.SemaphoreType.DMA((3,)),
        ],
        compiler_params=params(),
        cost_estimate=cost(hidden_in.size),
        name="early",
    )(stay(values[0, 0]), stay(hidden_in), stay(cotangent), *local)
    picked = pl.pallas_call(
        functools.partial(pick_kernel, *sizes, d_blocks),
        out_shape=[jax.ShapeDtypeStruct((slots + 1, chunk, block), jnp.bfloat16)] * spans,
        in_specs=[smem()] * spans + [vmem(), vmem()],
        out_specs=[vmem()] * spans,
        scratch_shapes=[pltpu.SMEM((spans, 3 * slots), jnp.int32)],
        compiler_params=params(),
        cost_estimate=cost(hidden_in.size),
        name="pick",
    )(*metas, values_half, hidden_here)
    crossed = exchange(picked)

    laid = ranges[0][1]
    first_weight = pl.pallas_call(
        lay_kernel,
        out_shape=jax.ShapeDtypeStruct((laid * width, d_width), down_weight.dtype),
        in_specs=[hbm()],
        out_specs=vmem(),
        scratch_shapes=[pltpu.SemaphoreType.DMA],
        compiler_params=params(),
        cost_estimate=cost(AHEAD * laid * width * d_width),
        name="lay",
    )(stay(down_weight))

    firsts, picked = lax.optimization_barrier((firsts, picked))
    remote = []
    for first in firsts:
        remote += [first] + [take_from(first, "dp", d) for d in range(1, cores)]
    metas, first_weight = lax.optimization_barrier((metas, first_weight))
    table = pl.pallas_call(
        functools.partial(table_kernel, slots, d_blocks),
        out_shape=jax.ShapeDtypeStruct((spans, 3 * slots), jnp.int32),
        in_specs=[smem()] * spans,
        out_specs=smem(),
        compiler_params=params(),
        cost_estimate=cost(spans * slots),
        name="table",
    )(*metas)

    early, rows = early_matmul_call(width, laid * width, first_weight, [local_rows, *remote])
    first, held = begin_call(sizes, table, early, rows, crossed)
    moving = [take_from(first, "seq", -1)]
    partials = [delta_call(spans, table, early, rows, held)]
    for part, (low, high) in enumerate(ranges[1:], 1):
        partial, first = matmul_call(
            spans, low, (high - low,), width, table, down_weight, rows, held
        )
        if part == RIDE:
            grads = grad_call(sizes, table, rows, crossed)
            first = attach_call(first, grads[1:])
        partials.append(partial)
        moving.append(take_from(first, "seq", -1))

    tiles = [grads[0]]
    for t in range(2, spans):
        for part in range(len(ranges)):
            moving[part], *mine = add_call(t, partials[part], moving[part], block)
            tiles += mine
            moving[part] = take_from(moving[part], "seq", -1)
    tiles.append(moving[RIDE])
    columns = partials[RIDE].shape[2]

    hidden_grad = None
    shape = jax.ShapeDtypeStruct((chunk, f_width), jnp.bfloat16)
    order = [part for part in range(len(ranges)) if part != LAST] + [LAST]
    for part in order:
        if part == LAST:
            tiles[0], hidden_grad = lax.optimization_barrier((tiles[0], hidden_grad))
            new = adam_call(sizes, columns, table, tiles, values, moment_one, moment_two)
            moving[part], new = lax.optimization_barrier((moving[part], new))
        hidden_grad = last_call(
            ranges[part][0] * width, partials[part], moving[part], hidden_grad, shape
        )
    return (hidden_grad,) + tuple(array[None, None] for array in new)


def solution(mesh):
    shards = P(("groups", "seq"), ("tensor", "dp"))
    tiles = P(("groups", "seq"), ("tensor", "dp"), None, None, None)
    lists = P(("groups", "seq"), ("tensor", "dp"), None)
    return jax.shard_map(
        per_device,
        mesh=mesh,
        in_specs=(
            shards,
            P(("groups", "tensor", "dp"), "seq"),
            P(("tensor", "dp"), "seq"),
            lists,
            lists,
            tiles,
            tiles,
            tiles,
        ),
        out_specs=(shards, tiles, tiles, tiles),
        check_vma=False,
    )
```

```python
import functools

import jax
import jax.numpy as jnp
from jax import lax
from jax.experimental import pallas as pl
from jax.experimental.pallas import tpu as pltpu
from jax.sharding import PartitionSpec as P

STEP = 100
BETA_ONE = 0.9
BETA_TWO = 0.999
RATE = 0.01
EPSILON = 1e-08
VMEM_LIMIT = 12 * 1024 * 1024
MATMUL = 4096
EARLY = 1
AHEAD = 5000
PARTS = (3, 2, 2)
RIDE = 2
LAST = 1
NT = (((1,), (1,)), ((), ()))
TN = (((0,), (0,)), ((), ()))


def vmem():
    return pl.BlockSpec(memory_space=pltpu.VMEM)


def smem():
    return pl.BlockSpec(memory_space=pltpu.SMEM)


def hbm():
    return pl.BlockSpec(memory_space=pltpu.HBM)


def stay(array):
    return pltpu.with_memory_space_constraint(array, pltpu.HBM)


def cost(count):
    return pl.CostEstimate(flops=count, bytes_accessed=2 * count, transcendentals=0)


def params():
    return pltpu.CompilerParams(vmem_limit_bytes=VMEM_LIMIT)


def wrap(index, size):
    return lax.rem(index + size, size)


def live_count(table, row, slots):
    count = table[row, 2 * slots]
    for slot in range(1, slots):
        count = count + table[row, 2 * slots + slot]
    return count


def rank_before(table, row, spans, slots):
    me = lax.axis_index("seq")
    before = jnp.int32(0)
    for other in range(spans):
        ahead = wrap(me - other, spans) < wrap(me - row, spans)
        before = before + jnp.where(ahead, live_count(table, other, slots), 0)
    return before


def early_kernel(values, hidden, own, *refs):
    others, (values_half, hidden_here, rows, stored, sems) = refs[:-5], refs[-5:]
    chunk = own.shape[0]
    copies = [
        pltpu.make_async_copy(values, stored, sems.at[0]),
        pltpu.make_async_copy(hidden, hidden_here, sems.at[1]),
        pltpu.make_async_copy(own, rows.at[pl.ds(0, chunk)], sems.at[2]),
    ]
    for copy in copies:
        copy.start()
    for p, other in enumerate(others):
        rows[(p + 1) * chunk : (p + 2) * chunk] = other[...]
    copies[0].wait()
    values_half[...] = stored[...].astype(values_half.dtype)
    copies[1].wait()
    copies[2].wait()


def table_kernel(slots, d_blocks, *refs):
    metas, table = refs[:-1], refs[-1]
    for s, meta in enumerate(metas):
        for j in range(slots):
            table[s, j] = lax.div(meta[0, j], d_blocks)
            table[s, slots + j] = lax.rem(meta[0, j], d_blocks)
            table[s, 2 * slots + j] = meta[0, slots + j]


def pick_kernel(spans, slots, block, d_blocks, *refs):
    metas, (values, hidden), outs, table = refs[:spans], refs[spans : spans + 2], refs[spans + 2 : -1], refs[-1]
    me = lax.axis_index("seq")
    table_kernel(slots, d_blocks, *metas, table)
    for s in range(spans):
        row = (spans - s) % spans
        before = rank_before(table, row, spans, slots)
        slot = wrap(me - lax.rem(before, spans), spans)
        tile = values[jnp.minimum(lax.div(before + slot, spans), slots - 1)]
        live = slot < live_count(table, row, slots)
        outs[s][slots] = jnp.where(live, tile.astype(jnp.float32), 0.0).astype(tile.dtype)
        for j in range(slots):
            start = pl.multiple_of(table[row, j] * block, block)
            outs[s][j] = hidden[:, pl.ds(start, block)]


def lay_kernel(weight, first_weight, sem):
    copy = pltpu.make_async_copy(weight.at[pl.ds(0, first_weight.shape[0])], first_weight, sem)
    copy.start()
    copy.wait()


def chunk_at(place):
    tensors, cores = lax.axis_size("tensor"), lax.axis_size("dp")
    t_place = lax.rem(lax.axis_index("tensor") + place // cores, tensors)
    d_place = lax.rem(lax.axis_index("dp") + place % cores, cores)
    return t_place * cores + d_place


def early_matmul_kernel(width, weight, *refs):
    pieces, (out, rows) = refs[:-2], refs[-2:]
    step = pl.program_id(0)

    @pl.when(step == 0)
    def _():
        at = 0
        for piece in pieces:
            rows[at : at + piece.shape[0]] = piece[...]
            at += piece.shape[0]

    here = pl.ds(pl.multiple_of(step * width, width), width)
    out[:, here] = lax.dot_general(
        rows[...], weight[here], NT, preferred_element_type=jnp.float32
    )


def early_matmul_call(width, columns, weight, pieces):
    tokens, d_width = sum(piece.shape[0] for piece in pieces), weight.shape[1]
    return pl.pallas_call(
        functools.partial(early_matmul_kernel, width),
        grid=(columns // width,),
        out_shape=[
            jax.ShapeDtypeStruct((tokens, columns), jnp.float32),
            jax.ShapeDtypeStruct((tokens, d_width), weight.dtype),
        ],
        in_specs=[vmem()] * (1 + len(pieces)),
        out_specs=[vmem()] * 2,
        compiler_params=params(),
        cost_estimate=cost(EARLY * tokens * columns),
        name="partial",
    )(weight, *pieces)


def add_delta(table, rows, held, total, low):
    slots, block, _ = held.shape
    count = live_count(table, 0, slots)
    for j in range(slots):
        f_start = table[0, j] * block - low

        @pl.when((j < count) & (f_start >= 0) & (f_start < total.shape[1]))
        def _():
            d_start = pl.multiple_of(table[0, slots + j] * block, block)
            place = pl.ds(pl.multiple_of(f_start, block), block)
            total[:, place] += lax.dot_general(
                rows[:, pl.ds(d_start, block)], held[j], NT, preferred_element_type=jnp.float32
            )


def put_chunks(total, out, first, here):
    spans, chunk = out.shape[:2]
    me = lax.axis_index("seq")
    for p in range(spans):
        result = total[p * chunk : (p + 1) * chunk].astype(out.dtype)
        out[chunk_at(p), :, here] = result

        @pl.when(chunk_at(p) == wrap(me - 1, spans))
        def _():
            first[:, here] = result


def begin_kernel(spans, slots, block, table, early, rows, *refs):
    stored, (first, held, total) = refs[:spans], refs[spans:]
    me = lax.axis_index("seq")
    before = rank_before(table, 0, spans, slots)
    for j in range(slots):
        for s in range(spans):

            @pl.when(lax.rem(before + j, spans) == wrap(me - s, spans))
            def _():
                held[j] = stored[s][slots]

    chunk = first.shape[0]
    for p in range(spans):

        @pl.when(chunk_at(p) == wrap(me - 1, spans))
        def _():
            total[...] = early[p * chunk : (p + 1) * chunk]
            add_delta(table, rows.at[pl.ds(p * chunk, chunk)], held, total, 0)

    first[...] = total[...].astype(first.dtype)


def begin_call(sizes, table, early, rows, stored):
    spans, slots, block = sizes
    tokens, columns = early.shape
    chunk = tokens // spans
    return pl.pallas_call(
        functools.partial(begin_kernel, *sizes),
        out_shape=[
            jax.ShapeDtypeStruct((chunk, columns), rows.dtype),
            jax.ShapeDtypeStruct((slots, block, block), rows.dtype),
        ],
        in_specs=[smem()] + [vmem()] * (2 + spans),
        out_specs=[vmem()] * 2,
        scratch_shapes=[pltpu.VMEM((chunk, columns), jnp.float32)],
        compiler_params=params(),
        cost_estimate=cost(chunk * columns),
        name="begin",
    )(table, early, rows, *stored)


def delta_kernel(table, early, rows, held, out, total):
    total[...] = early[...]
    add_delta(table, rows, held, total, 0)
    chunk = out.shape[1]
    for p in range(out.shape[0]):
        out[chunk_at(p)] = total[p * chunk : (p + 1) * chunk].astype(out.dtype)


def delta_call(spans, table, early, rows, held):
    tokens, columns = early.shape
    return pl.pallas_call(
        delta_kernel,
        out_shape=jax.ShapeDtypeStruct((spans, tokens // spans, columns), rows.dtype),
        in_specs=[smem()] + [vmem()] * 3,
        out_specs=vmem(),
        scratch_shapes=[pltpu.VMEM((tokens, columns), jnp.float32)],
        compiler_params=params(),
        cost_estimate=cost(early.size),
        name="delta",
    )(table, early, rows, held)


def matmul_kernel(low, ends, table, weight, rows, held, *refs):
    outs, total = refs[:-1], refs[-1]
    step, width = pl.program_id(0), total.shape[1]
    total[...] = lax.dot_general(rows[...], weight[...], NT, preferred_element_type=jnp.float32)
    add_delta(table, rows, held, total, (low + step) * width)
    for part, (begin, end) in enumerate(zip((0, *ends), ends)):

        @pl.when((step >= begin) & (step < end))
        def _():
            here = pl.ds(pl.multiple_of((step - begin) * width, width), width)
            put_chunks(total, *outs[2 * part : 2 * part + 2], here)


def matmul_call(spans, low, ends, width, table, weight, rows, held):
    tokens, d_width = rows.shape
    weight_spec = pl.BlockSpec((width, d_width), lambda i: (i + low, 0))
    shapes = []
    for begin, end in zip((0, *ends), ends):
        columns = (end - begin) * width
        shapes.append(jax.ShapeDtypeStruct((spans, tokens // spans, columns), rows.dtype))
        shapes.append(jax.ShapeDtypeStruct((tokens // spans, columns), rows.dtype))
    return pl.pallas_call(
        functools.partial(matmul_kernel, low, ends),
        grid=(ends[-1],),
        out_shape=shapes,
        in_specs=[smem(), weight_spec, vmem(), vmem()],
        out_specs=[vmem()] * len(shapes),
        scratch_shapes=[pltpu.VMEM((tokens, width), jnp.float32)],
        compiler_params=params(),
        cost_estimate=cost(MATMUL * tokens * ends[-1] * width),
        name="partial",
    )(table, stay(weight), rows, held)


def attach_kernel(first, *refs):
    riders, out = refs[:-1], refs[-1]
    at = first.shape[1]
    out[:, :at] = first[...]
    for rider in riders:
        out[:, at : at + rider.shape[1]] = rider[...]
        at += rider.shape[1]


def attach_call(first, riders):
    chunk, columns = first.shape
    columns += sum(rider.shape[1] for rider in riders)
    return pl.pallas_call(
        attach_kernel,
        out_shape=jax.ShapeDtypeStruct((chunk, columns), first.dtype),
        in_specs=[vmem()] * (1 + len(riders)),
        out_specs=vmem(),
        compiler_params=params(),
        cost_estimate=cost(first.size),
        name="attach",
    )(first, *riders)


def add_kernel(t, riders, partials, arrived, out, *mine):
    spans, _, columns = partials.shape
    chunk = wrap(lax.axis_index("seq") - t, spans)
    result = partials[chunk].astype(jnp.float32) + arrived[:, :columns].astype(jnp.float32)
    out[:, :columns] = result.astype(out.dtype)
    if riders:
        block = mine[0].shape[1]
        mine[0][...] = arrived[:, columns : columns + block]
        out[:, columns:] = arrived[:, columns + block :]


def add_call(t, partials, arrived, block):
    chunk, columns = partials.shape[1:]
    riders = (arrived.shape[1] - columns) // block
    shapes = [jax.ShapeDtypeStruct((chunk, arrived.shape[1] - min(riders, 1) * block), arrived.dtype)]
    if riders:
        shapes.append(jax.ShapeDtypeStruct((chunk, block), arrived.dtype))
    return pl.pallas_call(
        functools.partial(add_kernel, t, riders),
        out_shape=shapes,
        in_specs=[vmem(), vmem()],
        out_specs=[vmem()] * len(shapes),
        compiler_params=params(),
        cost_estimate=cost(arrived.size),
        name="add",
    )(partials, arrived)


def last_kernel(low, partials, arrived, *refs):
    out, total, sems = refs[-3:]
    me, columns = lax.axis_index("seq"), total.shape[1]
    middle, copies = columns // 256 * 128, []
    for k, here in enumerate((slice(0, middle), slice(middle, columns))):
        result = partials[me, :, here].astype(jnp.float32) + arrived[:, here].astype(jnp.float32)
        total[:, here] = result.astype(out.dtype)
        copy = pltpu.make_async_copy(
            total.at[:, here], out.at[:, pl.ds(low + here.start, here.stop - here.start)], sems.at[k]
        )
        copy.start()
        copies.append(copy)
    for copy in copies:
        copy.wait()


def last_call(low, partials, arrived, out, shape):
    _, chunk, columns = partials.shape
    given = [] if out is None else [out]
    return pl.pallas_call(
        functools.partial(last_kernel, low),
        out_shape=shape,
        in_specs=[vmem()] * 2 + [hbm()] * len(given),
        out_specs=hbm(),
        scratch_shapes=[
            pltpu.VMEM((chunk, columns), shape.dtype),
            pltpu.SemaphoreType.DMA((2,)),
        ],
        input_output_aliases={2: 0} if given else {},
        compiler_params=params(),
        cost_estimate=cost(partials.size),
        name="last_sum",
    )(partials, arrived, *given)


def grad_kernel(spans, slots, block, table, rows, *refs):
    hidden, outs, (cols,) = refs[:spans], refs[spans : 2 * spans], refs[2 * spans :]
    me = lax.axis_index("seq")
    count, before = live_count(table, 0, slots), rank_before(table, 0, spans, slots)
    chunk = rows.shape[0] // spans
    for s in range(spans):
        cols[s] = hidden[s][:slots]
    for s in range(spans):
        slot = wrap(lax.rem(me + s, spans) - lax.rem(before, spans), spans)
        outs[s][...] = jnp.zeros_like(outs[s])

        @pl.when(slot < count)
        def _():
            d_start = pl.multiple_of(table[0, slots + slot] * block, block)
            total = jnp.zeros((block, block), jnp.float32)
            for p in range(spans):
                total = total + lax.dot_general(
                    cols[wrap(me - chunk_at(p), spans), slot],
                    rows[p * chunk : (p + 1) * chunk, pl.ds(d_start, block)],
                    TN,
                    preferred_element_type=jnp.float32,
                )
            outs[s][...] = total.astype(outs[s].dtype)


def grad_call(sizes, table, rows, hidden_cols):
    spans = sizes[0]
    slots, chunk, block = hidden_cols[0].shape
    slots -= 1
    return pl.pallas_call(
        functools.partial(grad_kernel, *sizes),
        out_shape=[jax.ShapeDtypeStruct((block, block), jnp.bfloat16)] * spans,
        in_specs=[smem()] + [vmem()] * (spans + 1),
        out_specs=[vmem()] * spans,
        scratch_shapes=[pltpu.VMEM((spans, slots, chunk, block), jnp.bfloat16)],
        compiler_params=params(),
        cost_estimate=cost(rows.size),
        name="tile_grad",
    )(table, rows, *hidden_cols)


def adam_kernel(spans, slots, columns, table, *refs):
    arrived, refs = refs[:spans], refs[spans:]
    values, one, two, values_new, one_new, two_new, grads = refs
    me = lax.axis_index("seq")
    for s in range(spans - 1):
        grads[s] = arrived[s][...]
    grads[spans - 1] = arrived[-1][:, columns:]
    befores = [rank_before(table, s, spans, slots) for s in range(spans)]
    counts = [live_count(table, s, slots) for s in range(spans)]
    for owned in range(slots):
        rank = owned * spans + me
        source, live = jnp.int32(0), jnp.int32(0)
        for s in range(spans):
            holds = (befores[s] <= rank) & (rank < befores[s] + counts[s])
            source, live = jnp.where(holds, s, source), jnp.where(holds, 1, live)
        grad = grads[source].astype(jnp.float32)
        stored, old_one, old_two = values[owned], one[owned], two[owned]
        new_one = BETA_ONE * old_one + (1.0 - BETA_ONE) * grad
        new_two = BETA_TWO * old_two + (1.0 - BETA_TWO) * grad * grad
        stepped = (
            new_one
            / (1.0 - BETA_ONE**STEP)
            / (jnp.sqrt(new_two / (1.0 - BETA_TWO**STEP)) + EPSILON)
        )
        values_new[owned] = jnp.where(live > 0, stored - RATE * stepped, stored)
        one_new[owned] = jnp.where(live > 0, new_one, old_one)
        two_new[owned] = jnp.where(live > 0, new_two, old_two)


def adam_call(sizes, columns, table, grads, *states):
    spans, slots, block = sizes
    tile = jax.ShapeDtypeStruct((slots, block, block), jnp.float32)
    return pl.pallas_call(
        functools.partial(adam_kernel, spans, slots, columns),
        out_shape=(tile, tile, tile),
        in_specs=[smem()] + [vmem()] * (spans + 3),
        out_specs=(vmem(), vmem(), vmem()),
        scratch_shapes=[pltpu.VMEM((spans, block, block), jnp.bfloat16)],
        compiler_params=params(),
        cost_estimate=cost(slots * block * block),
        name="adam",
    )(table, *grads, *[state[0, 0] for state in states])


def take_from(array, axis, places):
    size = lax.axis_size(axis)
    return lax.ppermute(array, axis, [((i + places) % size, i) for i in range(size)])


def take_chunk(own, place):
    tensors, cores = lax.axis_size("tensor"), lax.axis_size("dp")
    t_place, d_place = divmod(place, cores)
    pairs = []
    for t in range(tensors):
        for d in range(cores):
            source = (t + t_place) % tensors * cores + (d + d_place) % cores
            pairs.append((source, t * cores + d))
    return lax.ppermute(own, ("tensor", "dp"), pairs)


def exchange(pieces):
    return [pieces[0]] + [take_from(pieces[s], "seq", -s) for s in range(1, len(pieces))]


def per_device(
    hidden_in, cotangent, down_weight, tile_ids, tile_live, values, moment_one, moment_two
):
    spans, cores = lax.axis_size("seq"), lax.axis_size("dp")
    slots, block = values.shape[2], values.shape[3]
    f_width, d_width = down_weight.shape
    d_blocks, f_blocks = d_width // block, f_width // block
    chunk = hidden_in.shape[0]
    sizes = (spans, slots, block)
    group = max(size for size in range(1, 5) if f_blocks % size == 0)
    width = group * block
    ends = [sum(PARTS[:part]) for part in range(len(PARTS) + 1)]
    cuts = [(f_blocks // group) * end // ends[-1] for end in ends]
    ranges = list(zip(cuts[:-1], cuts[1:]))

    local = [take_chunk(cotangent, place) for place in range(1, cores)]
    firsts = [take_from(cotangent, "tensor", t) for t in range(1, lax.axis_size("tensor"))]

    meta = jnp.concatenate([tile_ids[0], tile_live[0]], axis=1)
    metas = exchange([meta] * spans)
    values_half, hidden_here, local_rows = pl.pallas_call(
        early_kernel,
        out_shape=[
            jax.ShapeDtypeStruct((slots, block, block), jnp.bfloat16),
            jax.ShapeDtypeStruct(hidden_in.shape, hidden_in.dtype),
            jax.ShapeDtypeStruct((cores * chunk, d_width), cotangent.dtype),
        ],
        in_specs=[hbm()] * 3 + [vmem()] * (cores - 1),
        out_specs=[vmem()] * 3,
        scratch_shapes=[
            pltpu.VMEM((slots, block, block), jnp.float32),
            pltpu.SemaphoreType.DMA((3,)),
        ],
        compiler_params=params(),
        cost_estimate=cost(hidden_in.size),
        name="early",
    )(stay(values[0, 0]), stay(hidden_in), stay(cotangent), *local)
    picked = pl.pallas_call(
        functools.partial(pick_kernel, *sizes, d_blocks),
        out_shape=[jax.ShapeDtypeStruct((slots + 1, chunk, block), jnp.bfloat16)] * spans,
        in_specs=[smem()] * spans + [vmem(), vmem()],
        out_specs=[vmem()] * spans,
        scratch_shapes=[pltpu.SMEM((spans, 3 * slots), jnp.int32)],
        compiler_params=params(),
        cost_estimate=cost(hidden_in.size),
        name="pick",
    )(*metas, values_half, hidden_here)
    crossed = exchange(picked)

    laid = ranges[0][1]
    first_weight = pl.pallas_call(
        lay_kernel,
        out_shape=jax.ShapeDtypeStruct((laid * width, d_width), down_weight.dtype),
        in_specs=[hbm()],
        out_specs=vmem(),
        scratch_shapes=[pltpu.SemaphoreType.DMA],
        compiler_params=params(),
        cost_estimate=cost(AHEAD * laid * width * d_width),
        name="lay",
    )(stay(down_weight))

    firsts, picked = lax.optimization_barrier((firsts, picked))
    remote = []
    for first in firsts:
        remote += [first] + [take_from(first, "dp", d) for d in range(1, cores)]
    metas, first_weight = lax.optimization_barrier((metas, first_weight))
    table = pl.pallas_call(
        functools.partial(table_kernel, slots, d_blocks),
        out_shape=jax.ShapeDtypeStruct((spans, 3 * slots), jnp.int32),
        in_specs=[smem()] * spans,
        out_specs=smem(),
        compiler_params=params(),
        cost_estimate=cost(spans * slots),
        name="table",
    )(*metas)

    early, rows = early_matmul_call(width, laid * width, first_weight, [local_rows, *remote])
    first, held = begin_call(sizes, table, early, rows, crossed)
    moving = [take_from(first, "seq", -1)]
    partials = [delta_call(spans, table, early, rows, held)]
    for part, (low, high) in enumerate(ranges[1:], 1):
        partial, first = matmul_call(
            spans, low, (high - low,), width, table, down_weight, rows, held
        )
        if part == RIDE:
            grads = grad_call(sizes, table, rows, crossed)
            first = attach_call(first, grads[1:])
        partials.append(partial)
        moving.append(take_from(first, "seq", -1))

    tiles = [grads[0]]
    for t in range(2, spans):
        for part in range(len(ranges)):
            moving[part], *mine = add_call(t, partials[part], moving[part], block)
            tiles += mine
            moving[part] = take_from(moving[part], "seq", -1)
    tiles.append(moving[RIDE])
    columns = partials[RIDE].shape[2]

    hidden_grad = None
    shape = jax.ShapeDtypeStruct((chunk, f_width), jnp.bfloat16)
    order = [part for part in range(len(ranges)) if part != LAST] + [LAST]
    for part in order:
        if part == LAST:
            tiles[0], hidden_grad = lax.optimization_barrier((tiles[0], hidden_grad))
            new = adam_call(sizes, columns, table, tiles, values, moment_one, moment_two)
            moving[part], new = lax.optimization_barrier((moving[part], new))
        hidden_grad = last_call(
            ranges[part][0] * width, partials[part], moving[part], hidden_grad, shape
        )
    return (hidden_grad,) + tuple(array[None, None] for array in new)


def solution(mesh):
    shards = P(("groups", "seq"), ("tensor", "dp"))
    tiles = P(("groups", "seq"), ("tensor", "dp"), None, None, None)
    lists = P(("groups", "seq"), ("tensor", "dp"), None)
    return jax.shard_map(
        per_device,
        mesh=mesh,
        in_specs=(
            shards,
            P(("groups", "tensor", "dp"), "seq"),
            P(("tensor", "dp"), "seq"),
            lists,
            lists,
            tiles,
            tiles,
            tiles,
        ),
        out_specs=(shards, tiles, tiles, tiles),
        check_vma=False,
    )
```
